32 devices in a mesh: row: 8 (over z, core), col: 4 (over y, x).
Axes of the slice: x: 2, y: 2, z: 4, core: 2. Of those that a mesh axis runs over, the one named last changes fastest.
Arguments:
- front_entries: float32 [16384, 16384], P('row', 'col'), may hold values from 0 to 3, as said below
- tile_group: int32 [32], replicated, may hold values from 0 to 3
- child_factor: bfloat16 [16384, 256], P('row', 'col'), may hold values from -0.375 to 0.375
- row_map: int32 [128], replicated, may hold values from 0 to 127, as said below
Outputs:
- factor_panels: bfloat16 [16384, 512], P('row', 'col')
- schur_block: float32 [16384, 16384], P('row', 'col')
The draws below stay inside these ranges and needn't reach their ends.
Inputs may be any that keep to these rules, and one draw needn't show every extreme that they name: `front_entries`: Symmetric; assembled is positive definite. `row_map`: A permutation of the parent tiles. The tile in row block r (blocks of 2048 rows) goes to a parent tile in row block r or in the row block whose index differs from r in the highest bit.
All inputs are finite; a program needn't handle non-finite values.
Results may differ from the reference program's by a relative error of at most 0.0026.
Values may be sent and summed in bfloat16 or wider, within the bound.
No kernel may reach another device: no remote copies, remote signals or barrier semaphores. Data moves between devices by JAX's collectives and lax.ppermute only.
A program may use at most 192 MiB of HBM per device.

```python
import jax
import jax.numpy as jnp
from jax import lax

F = 16384
PW = 256
NP = 2
KC = 256
TS = 128
MT = 512
N_ROW = 8
N_COL = 4


def draw_front_entries(key, part):
    point_key = jax.random.fold_in(key, 11)
    shift_key = jax.random.fold_in(key, 23)
    points = jax.random.uniform(point_key, (F, 3), jnp.float32)
    diag_shift = jnp.exp(jax.random.uniform(shift_key, (F,), jnp.float32, jnp.log(0.5), jnp.log(2.0)))
    length_scale = 2.0 * float(F) ** (-1.0 / 3.0)
    distance_sq = jnp.zeros((F, F), jnp.float32)
    for dim_index in range(3):
        offset_dim = points[:, dim_index][:, None] - points[:, dim_index][None, :]
        distance_sq = distance_sq + offset_dim * offset_dim
    kernel = jnp.exp(-jnp.sqrt(distance_sq) / length_scale)
    diag_ids = jnp.arange(F)
    return kernel.at[diag_ids, diag_ids].add(diag_shift)


def draw_row_map(key, part):
    tile_count = F // TS // N_ROW
    half_rows = N_ROW // 2
    pair_keys = jax.random.split(jax.random.fold_in(key, 37), half_rows)
    shuffles = jax.vmap(lambda single: jax.random.permutation(single, 2 * tile_count))(pair_keys)
    device = jnp.arange(half_rows, dtype=jnp.int32)[:, None]
    target = (device + shuffles // tile_count * half_rows) * tile_count + shuffles % tile_count
    child_first = target[:, :tile_count].reshape(-1)
    child_second = target[:, tile_count:].reshape(-1)
    return jnp.concatenate([child_first, child_second]).astype(jnp.int32)


def with_ends(drawn, stream_key, smallest, high):
    dims = drawn.shape
    index_at = [jax.random.randint(jax.random.fold_in(stream_key, axis), (), 0, dims[axis]) for axis in range(len(dims))]
    drawn = drawn.at[tuple(index_at)].set(smallest)
    longest = dims.index(max(dims))
    index_at[longest] = (index_at[longest] + 1) % dims[longest]
    return drawn.at[tuple(index_at)].set(high)


def levels(key, shape, cuts, smallest, largest):
    gain, own = 1.0, jax.random.fold_in(key, 6)
    for dim, blocks in cuts:
        heights = jnp.exp(jax.random.uniform(jax.random.fold_in(own, dim), (blocks,), jnp.float32, smallest / len(cuts), largest / len(cuts)))
        gain = gain * jnp.repeat(heights, shape[dim] // blocks).reshape([-1 if axis == dim else 1 for axis in range(len(shape))])
    return gain


def bell_draw(rng, dims, deviation, reach, shards=(), held_as=jnp.bfloat16):
    level = levels(rng, dims, shards, -0.22, 0.18) if shards else 1.0
    values = jax.random.normal(rng, dims, jnp.float32) * deviation * level
    return jnp.minimum(jnp.maximum(values, -reach), reach).astype(held_as)


def setup_inputs(seed: int = 0) -> dict:
    streams_of = jax.random.split(jax.random.key(seed), 5)
    return {
        "front_entries": draw_front_entries(jax.random.fold_in(streams_of[4], 71), 0),
        "tile_group": with_ends(jax.random.randint(streams_of[1], (F // MT,), 0, 4), jax.random.fold_in(streams_of[1], 1), 0, 3).astype(jnp.int32),
        "child_factor": bell_draw(streams_of[2], (F, KC), KC ** -0.5, 0.375, ((0, 8), (1, 4))),
        "row_map": draw_row_map(jax.random.fold_in(streams_of[4], 71), 0),
    }


def reference(front_entries, tile_group, child_factor, row_map):
    block_rows = F // N_ROW
    row_share = PW // N_ROW
    col_share = PW // N_COL
    mask_tiles = F // MT
    same_group = (tile_group[:, None] == tile_group[None, :]).astype(jnp.float32)
    masked = (front_entries.reshape(mask_tiles, MT, mask_tiles, MT) * same_group[:, None, :, None]).reshape(F, F)
    child_tiles = F // TS
    half_tiles = child_tiles // 2
    pieces = child_factor.reshape(child_tiles, TS, KC)
    child_first = jnp.zeros((child_tiles, TS, KC), jnp.bfloat16).at[row_map[:half_tiles]].set(pieces[:half_tiles])
    child_second = jnp.zeros((child_tiles, TS, KC), jnp.bfloat16).at[row_map[half_tiles:]].set(pieces[half_tiles:])
    child_wide = jnp.concatenate([child_first.reshape(F, KC), child_second.reshape(F, KC)], axis=1).astype(jnp.float32)
    assembled = masked + jnp.dot(child_wide, child_wide.T, precision=lax.Precision.HIGHEST)
    block_ids = jnp.arange(N_ROW, dtype=jnp.int32)
    pivots = (block_ids[None, :, None] * block_rows + jnp.arange(NP, dtype=jnp.int32)[:, None, None] * row_share + jnp.arange(row_share, dtype=jnp.int32)[None, None, :]).reshape(-1)
    pivot_done = NP * row_share
    remaining = (block_ids[:, None] * block_rows + pivot_done + jnp.arange(block_rows - pivot_done, dtype=jnp.int32)[None, :]).reshape(-1)
    pivot_order = jnp.concatenate([pivots, remaining]).astype(jnp.int32)
    inverse = jnp.zeros((F,), jnp.int32).at[pivot_order].set(jnp.arange(F, dtype=jnp.int32))
    working = assembled[pivot_order][:, pivot_order]
    columns = []
    for k in range(NP):
        low = k * PW
        high = low + PW
        lower_factor = jnp.linalg.cholesky(working[low:high, low:high])
        below = lax.linalg.triangular_solve(lower_factor, working[high:, low:high], left_side=False, lower=True, transpose_a=True)
        panel = jnp.concatenate([jnp.zeros((low, PW), jnp.float32), lower_factor, below], axis=0).astype(jnp.bfloat16)
        columns.append(panel)
        lead_rows = panel[high:].astype(jnp.float32)
        working = working.at[high:, high:].add(-jnp.dot(lead_rows, lead_rows.T, precision=lax.Precision.HIGHEST))
    factor_full = jnp.concatenate(columns, axis=1)
    factor_store = factor_full[inverse]
    factor_panels = factor_store.reshape(F, NP, N_COL, col_share).transpose(0, 2, 1, 3).reshape(F, NP * PW)
    pivot_total = NP * PW
    trailing = jnp.zeros((F, F), jnp.float32).at[pivot_total:, pivot_total:].set(working[pivot_total:, pivot_total:])
    schur_block = trailing[inverse][:, inverse]
    return (factor_panels, schur_block)
```

```python
import functools

import jax
import jax.numpy as jnp
from jax import lax
from jax.experimental import pallas as pl
from jax.experimental.pallas import tpu as pltpu
from jax.sharding import PartitionSpec as P

PW = 256
NP = 2
TS = 128
MT = 512
NPIV = NP * PW
BLK = 32
F32 = jnp.float32
BF16 = jnp.bfloat16
VMEM_BYTES = 50 * 1024 * 1024

NN = (((1,), (0,)), ((), ()))
NT = (((1,), (1,)), ((), ()))
TN = (((0,), (0,)), ((), ()))


def dot(left, right, dims=NN, precision=None):
    return lax.dot_general(left, right, dims, precision=precision, preferred_element_type=F32)


def exact(left, right, dims=NN):
    return dot(left, right, dims, lax.Precision.HIGHEST)


def split(value):
    high = value.astype(BF16)
    return high, (value - high.astype(F32)).astype(BF16)


def swapped(value, axis, mask):
    if mask == 0:
        return value
    return lax.ppermute(value, axis, [(i, i ^ mask) for i in range(lax.axis_size(axis))])


def whole_spec():
    return pl.BlockSpec(memory_space=pltpu.VMEM)


def any_spec():
    return pl.BlockSpec(memory_space=pl.ANY)


def smem_spec():
    return pl.BlockSpec(memory_space=pltpu.SMEM)


def factor_diagonal(block):
    groups = BLK // 8
    lane = lax.broadcasted_iota(jnp.int32, (BLK, 128), 1)
    row = lax.broadcasted_iota(jnp.int32, (BLK, 128), 0)
    row8 = lax.broadcasted_iota(jnp.int32, (8, 128), 0)
    start = jnp.where(lane < BLK, block, jnp.where(lane == row + BLK, 1.0, 0.0))
    work = [start[8 * g : 8 * g + 8] for g in range(groups)]
    cols = []
    for k in range(BLK):
        base = 8 * (k // 8)
        cols.append(jnp.broadcast_to(block[base:, k : k + 1], (BLK - base, 128)))
    scale = [jnp.ones((8, 128), F32) for _ in range(groups)]
    for j in range(BLK):
        g0 = j // 8
        base = 8 * g0
        column = cols[j]
        pivot = column[j - base : j - base + 1]
        root = lax.rsqrt(pivot)
        root = root * (1.5 - 0.5 * pivot * root * root)
        factor = jnp.where(row[base:] > j, column * (root * root), 0.0)
        lead = work[g0][j - base : j - base + 1]
        for g in range(g0, groups):
            work[g] = work[g] - factor[8 * (g - g0) : 8 * (g - g0) + 8] * lead
        for k in range(j + 1, BLK):
            skip = 8 * (k // 8 - g0)
            cols[k] = cols[k] - factor[skip:] * column[k - base : k - base + 1]
        scale[g0] = jnp.where(row8 == j - base, root, scale[g0])
    return jnp.concatenate([work[g] * scale[g] for g in range(groups)], axis=0)


def factor_panel(work):
    per_tile = 128 // BLK
    row = lax.broadcasted_iota(jnp.int32, (PW, BLK), 0)
    lane = lax.broadcasted_iota(jnp.int32, (BLK, 128), 1)

    def step(b, carry):
        low = pl.multiple_of(b * BLK, BLK)
        tile = pl.multiple_of((b // per_tile) * 128, 128)
        turn = (128 - (b % per_tile) * BLK) % 128
        columns = pltpu.roll(work[:, pl.ds(tile, 128)], turn, 1)
        block = pltpu.roll(work[pl.ds(low, BLK), pl.ds(tile, 128)], turn, 1)
        done = factor_diagonal(block)
        inverse = jnp.where(lane < BLK, pltpu.roll(done, 128 - BLK, 1), 0.0)
        upper = exact(inverse[:, :BLK], work[pl.ds(low, BLK), :])
        lead = exact(columns, inverse, NT)
        lead = jnp.where(row >= low + BLK, lead, 0.0)
        work[...] = work[...] - exact(lead, upper)
        work[pl.ds(low, BLK), :] = upper
        return carry

    lax.fori_loop(0, PW // BLK, step, 0)


def pivot_kernel(sizes, place, front, child, group_col, group_row, kid_col, kid_row,
                 lower, store_hi, store_lo, flip_hi, flip_lo, link_hi, link_lo, piv_t, piv,
                 pile, other, work):
    rows, cols, fan, share, held, slice_cols = sizes
    my_row, my_col = place[0], place[1]
    my_q, my_a = my_row % fan, my_row // fan

    def slot(r, c):
        return (r % fan) ^ my_q, c ^ my_col, (r // fan) ^ my_a

    for r in range(rows):
        pile[r * held : (r + 1) * held, :] = jnp.concatenate(
            [front[slot(r, c)] for c in range(cols)], axis=1
        )
    half = rows // 2
    for c in range(cols):
        parts = []
        for r in range(rows):
            own = child[slot(r, c)].astype(F32)
            other_half = child[slot(r ^ half, c)].astype(F32)
            parts.append(own[:, :held] + other_half[:, held:])
        piv_t[c * slice_cols : (c + 1) * slice_cols, :] = jnp.concatenate(parts, axis=1).astype(BF16)
    piv[...] = piv_t[...].astype(F32).T.astype(BF16)
    product = dot(piv[...], piv_t[...])
    pile[...] = jnp.where(group_col[...] == group_row[...], pile[...], 0.0) + jnp.where(
        kid_col[...] == kid_row[...], product, 0.0
    )

    def to_pivot_order(source, target):
        for k in range(NP):
            for r in range(rows):
                target[k * PW + r * share : k * PW + (r + 1) * share, :] = source[
                    r * held + k * share : r * held + (k + 1) * share, :
                ]

    to_pivot_order(pile, other)
    pile[...] = other[...].T
    to_pivot_order(pile, other)
    eye_row = lax.broadcasted_iota(jnp.int32, (PW, PW), 0)
    eye_col = lax.broadcasted_iota(jnp.int32, (PW, PW), 1)
    eye = jnp.where(eye_row == eye_col, 1.0, 0.0)
    zero = jnp.zeros((PW, PW), F32)
    work[:, :PW] = other[:PW, :PW]
    work[:, PW:] = eye
    factor_panel(work)
    lower[:PW, :PW] = jnp.where(eye_col <= eye_row, work[:, :PW].T, 0.0)
    lower[:PW, PW:] = zero
    first_inverse = work[:, PW:]
    link = exact(other[PW:, :PW], first_inverse, NT).astype(BF16)
    lower[PW:, :PW] = link.astype(F32)
    work[:, :PW] = other[PW:, PW:] - dot(link, link, NT)
    work[:, PW:] = eye
    pile[:PW, :PW] = first_inverse.T
    factor_panel(work)
    lower[PW:, PW:] = jnp.where(eye_col <= eye_row, work[:, :PW].T, 0.0)
    second_inverse = work[:, PW:]
    cross = exact(second_inverse, link.astype(F32))
    link_hi[...], link_lo[...] = split(cross)
    pile[PW:, PW:] = second_inverse.T
    other[...] = jnp.zeros_like(other)
    for r in range(rows):
        for k in range(NP):
            other[r * held + k * share : r * held + (k + 1) * share, k * PW : (k + 1) * PW] = pile[
                k * PW + r * share : k * PW + (r + 1) * share, k * PW : (k + 1) * PW
            ]
    store_hi[...], store_lo[...] = split(other[...])
    flip_hi[...], flip_lo[...] = split(other[...].T)


def place_kernel(sizes, place, inverse_map, *refs):
    cols, fan, tiles = sizes
    sources, outs = refs[:cols], refs[cols : 2 * cols + 1]
    held, sems = refs[2 * cols + 1 :]
    my_row, my_col = place[0], place[1]
    my_q, my_a = my_row % fan, my_row // fan
    copies = [
        pltpu.make_async_copy(sources[d], held.at[my_a ^ d], sems.at[d]) for d in range(cols)
    ]
    for copy in copies:
        copy.start()
    for copy in copies:
        copy.wait()

    def fill(block, out):
        for i in range(tiles):
            tile = inverse_map[block * tiles + i]
            source = (tile // tiles) // fan
            at = pl.multiple_of((tile % tiles) * TS, TS)
            out[:, i * TS : (i + 1) * TS] = held[source, :, pl.ds(at, TS)]

    fill(my_row, outs[0])
    for d in range(cols):
        fill((my_col ^ d) * fan + my_q, outs[1 + d])


def row_kernel(sizes, place, group_of, kid_of, strips, group_row, kid_row, piv_t, lower,
               store_hi, store_lo, link_hi, link_lo, *refs):
    cols, fan, share, held, slice_cols, block_rows, kid_cols = sizes
    sources = refs[:cols]
    lead, panel = refs[cols : cols + 2]
    flipped, solved, sems = refs[cols + 2 :]
    my_row, my_col = place[0], place[1]
    step = pl.program_id(0)

    @pl.when(step == 0)
    def _():
        copies = [
            pltpu.make_async_copy(
                sources[d],
                flipped.at[pl.ds(pl.multiple_of((my_col ^ d) * slice_cols, slice_cols), slice_cols), :],
                sems.at[d],
            )
            for d in range(cols)
        ]
        for copy in copies:
            copy.start()
        for copy in copies:
            copy.wait()

    subs = block_rows // TS
    own_t = flipped[:, pl.ds(pl.multiple_of(step * block_rows, block_rows), block_rows)]
    own = own_t.astype(F32).T.astype(BF16)
    product = dot(own, piv_t[...])
    entries = jnp.concatenate([strips[c] for c in range(cols)], axis=1)
    parts = []
    for i in range(subs):
        tile = step * subs + i
        part = slice(i * TS, (i + 1) * TS)
        parts.append(
            jnp.where(group_row[...] == group_of[tile], entries[part], 0.0)
            + jnp.where(kid_row[...] == kid_of[tile], product[part], 0.0)
        )
        mine = own[part].astype(F32)
        second = jnp.full(mine.shape, kid_of[tile], F32) > 0.5
        lead[part, :kid_cols] = jnp.where(second, 0.0, mine).astype(BF16)
        lead[part, kid_cols : 2 * kid_cols] = jnp.where(second, mine, 0.0).astype(BF16)
    high, low = split(jnp.concatenate(parts, axis=0))
    answer = dot(high, store_hi[...]) + dot(high, store_lo[...]) + dot(low, store_hi[...])
    first = answer[:, :PW].astype(BF16)
    second = answer[:, PW:] - dot(first, link_hi[...], NT) - dot(first, link_lo[...], NT)
    solved[:, :PW] = answer[:, :PW]
    solved[:, PW:] = second

    @pl.when(step == 0)
    def _():
        for k in range(NP):
            at = pl.multiple_of(k * PW + my_row * share, share)
            solved[k * share : (k + 1) * share, :] = lower[pl.ds(at, share), :]

    lead[:, 2 * kid_cols :] = solved[...].astype(BF16)
    col_share = PW // cols
    per_tile = 128 // col_share
    lane = lax.broadcasted_iota(jnp.int32, (block_rows, 128), 1)
    out = jnp.zeros((block_rows, 128), F32)
    for k in range(NP):
        tile = pl.multiple_of(k * PW + (my_col // per_tile) * 128, 128)
        turn = (128 + k * col_share - (my_col % per_tile) * col_share) % 128
        moved = pltpu.roll(solved[:, pl.ds(tile, 128)], turn, 1)
        out = jnp.where(lane // col_share == k, moved, out)
    panel[...] = out[:, : NP * col_share].astype(BF16)


def col_kernel(sizes, place, group_col, kid_col, group_all, kid_all, piv,
               flip_hi, flip_lo, link_hi, link_lo, *refs):
    cols, fan, held, slice_cols, block_cols, local_rows, kid_cols = sizes
    count = cols * fan
    strips, kids = refs[:count], refs[count : 2 * count]
    out = refs[2 * count]
    pile, flipped, sems = refs[2 * count + 1 :]
    my_row, my_col = place[0], place[1]
    my_q, my_a = my_row % fan, my_row // fan
    step = pl.program_id(0)

    @pl.when(step == 0)
    def _():
        copies = []
        for dq in range(fan):
            for d in range(cols):
                i = dq * cols + d
                block = (my_a ^ d) * fan + (my_q ^ dq)
                copies.append(
                    pltpu.make_async_copy(
                        strips[i], pile.at[pl.ds(pl.multiple_of(block * held, held), held), :], sems.at[i]
                    )
                )
                copies.append(
                    pltpu.make_async_copy(
                        kids[i],
                        flipped.at[
                            pl.ds(pl.multiple_of((my_col ^ d) * slice_cols, slice_cols), slice_cols),
                            pl.ds(pl.multiple_of((my_q ^ dq) * local_rows, local_rows), local_rows),
                        ],
                        sems.at[count + i],
                    )
                )
        for copy in copies:
            copy.start()
        for copy in copies:
            copy.wait()

    at = pl.ds(pl.multiple_of(step * block_cols, block_cols), block_cols)
    mine = flipped[:, at]
    product = dot(piv[...], mine)
    entries = pile[:, at].astype(F32)
    strip = jnp.where(group_col[...] == group_all[...], entries, 0.0) + jnp.where(
        kid_col[...] == kid_all[...], product, 0.0
    )
    high, low = split(strip)
    answer = dot(flip_hi[...], high) + dot(flip_lo[...], high) + dot(flip_hi[...], low)
    first = answer[:PW].astype(BF16)
    second = answer[PW:] - dot(link_hi[...], first) - dot(link_lo[...], first)
    mine = mine.astype(F32)
    out[:kid_cols] = jnp.where(kid_all[...] == 0.0, mine, 0.0).astype(BF16)
    out[kid_cols : 2 * kid_cols] = jnp.where(kid_all[...] == 1.0, mine, 0.0).astype(BF16)
    out[2 * kid_cols : 2 * kid_cols + PW] = -first
    out[2 * kid_cols + PW :] = (-second).astype(BF16)


def schur_kernel(sizes, group_of, front, lead, flipped, group_all, out):
    block_rows, block_cols, local_rows, held = sizes
    j, i = pl.program_id(0), pl.program_id(1)
    at = pl.ds(pl.multiple_of(i * block_rows, block_rows), block_rows)
    product = dot(lead[at, :], flipped[...])
    group = group_of[i * (block_rows // TS)]
    out[...] = jnp.where(group_all[...] == group, front[...], 0.0) + product

    @pl.when(i == 0)
    def _():
        out[:held, :] = jnp.zeros((held, block_cols), F32)

    @pl.when((j * block_cols) % local_rows == 0)
    def _():
        out[:, :held] = jnp.zeros((block_rows, held), F32)


def params():
    return pltpu.CompilerParams(vmem_limit_bytes=VMEM_BYTES)


def local(front_entries, tile_group, child_factor, row_map):
    rows, cols = lax.axis_size("row"), lax.axis_size("col")
    fan = rows // cols
    local_rows, local_cols = front_entries.shape
    slice_cols = child_factor.shape[1]
    kid_cols = slice_cols * cols
    tiles = local_rows // TS
    share = PW // rows
    held = NP * share
    my_row, my_col = lax.axis_index("row"), lax.axis_index("col")
    half = rows // 2
    place = jnp.stack([my_row, my_col]).astype(jnp.int32)

    corner = jnp.concatenate(
        [front_entries[:held, q * local_rows : q * local_rows + held] for q in range(fan)], axis=1
    )
    flipped = child_factor.T
    own_map = lax.dynamic_slice_in_dim(row_map, my_row * tiles, tiles)
    starts = flipped.reshape(slice_cols, tiles, TS)[:, :, :held]

    def chosen(block):
        keep = (own_map == block * tiles)[None, :, None]
        return jnp.sum(jnp.where(keep, starts, 0), axis=1, dtype=F32).astype(BF16)

    kids = jnp.concatenate([chosen(my_row), chosen(jnp.bitwise_xor(my_row, half))], axis=1)

    def spread(value):
        value = jnp.stack([swapped(value, "row", d * fan) for d in range(cols)])
        value = jnp.stack([swapped(value, "col", d) for d in range(cols)])
        return jnp.stack([swapped(value, "row", d) for d in range(fan)])

    corner_all, kids_all = spread(corner), spread(kids)

    tile_ids = jnp.arange(row_map.shape[0], dtype=jnp.int32)
    inverse_map = jnp.sum(
        jnp.where(row_map[None, :] == tile_ids[:, None], tile_ids[None, :], 0), axis=1, dtype=jnp.int32
    )
    kid_of_tile = (inverse_map >= row_map.shape[0] // 2).astype(jnp.int32)
    group_of_tile = jnp.repeat(tile_group, MT // TS)
    own_kid = lax.dynamic_slice_in_dim(kid_of_tile, my_row * tiles, tiles)
    own_group = lax.dynamic_slice_in_dim(group_of_tile, my_row * tiles, tiles)
    col_kid = lax.dynamic_slice_in_dim(kid_of_tile, my_col * fan * tiles, fan * tiles)
    col_group = lax.dynamic_slice_in_dim(group_of_tile, my_col * fan * tiles, fan * tiles)
    kid_all = jnp.repeat(col_kid.astype(F32), TS)[None, :]
    group_all = jnp.repeat(col_group.astype(F32), TS)[None, :]
    kid_piv = jnp.repeat(kid_of_tile[::tiles].astype(F32), held)
    group_piv = jnp.repeat(group_of_tile[::tiles].astype(F32), held)

    square = jax.ShapeDtypeStruct((NPIV, NPIV), BF16)
    small = jax.ShapeDtypeStruct((PW, PW), BF16)
    lower, store_hi, store_lo, flip_hi, flip_lo, link_hi, link_lo, piv_t, piv = pl.pallas_call(
        functools.partial(pivot_kernel, (rows, cols, fan, share, held, slice_cols)),
        out_shape=[
            jax.ShapeDtypeStruct((NPIV, NPIV), F32),
            square, square, square, square, small, small,
            jax.ShapeDtypeStruct((kid_cols, NPIV), BF16),
            jax.ShapeDtypeStruct((NPIV, kid_cols), BF16),
        ],
        in_specs=[smem_spec()] + [whole_spec()] * 6,
        out_specs=[whole_spec()] * 9,
        scratch_shapes=[
            pltpu.VMEM((NPIV, NPIV), F32),
            pltpu.VMEM((NPIV, NPIV), F32),
            pltpu.VMEM((PW, 2 * PW), F32),
        ],
        compiler_params=params(),
        name="pivot_block",
    )(place, corner_all, kids_all, group_piv[:, None], group_piv[None, :], kid_piv[:, None], kid_piv[None, :])

    kid_rows = [swapped(flipped, "row", d * fan) for d in range(cols)]
    placed = pl.pallas_call(
        functools.partial(place_kernel, (cols, fan, tiles)),
        out_shape=[jax.ShapeDtypeStruct((slice_cols, local_rows), BF16)] * (cols + 1),
        in_specs=[smem_spec()] * 2 + [any_spec()] * cols,
        out_specs=[whole_spec()] * (cols + 1),
        scratch_shapes=[
            pltpu.VMEM((cols, slice_cols, local_rows), BF16),
            pltpu.SemaphoreType.DMA((cols,)),
        ],
        compiler_params=params(),
        name="place_tiles",
    )(place, inverse_map, *kid_rows)
    own_kids = [swapped(placed[0], "col", d) for d in range(cols)]
    col_kids = [swapped(placed[1 + d], "col", d) for d in range(cols)]
    col_kids = [swapped(value, "row", d) for d in range(fan) for value in col_kids]

    row_strip = jnp.concatenate(
        [front_entries[:, q * local_rows : q * local_rows + held] for q in range(fan)], axis=1
    )
    row_strips = lax.all_gather(row_strip, "col", axis=0)
    col_strip = front_entries[:held].astype(BF16)
    col_strips = [swapped(col_strip, "row", d * fan) for d in range(cols)]
    col_strips = [swapped(value, "row", d) for d in range(fan) for value in col_strips]

    block_rows = min(256, local_rows)
    width = 2 * kid_cols + NPIV
    lead, factor_panels = pl.pallas_call(
        functools.partial(row_kernel, (cols, fan, share, held, slice_cols, block_rows, kid_cols)),
        grid=(local_rows // block_rows,),
        out_shape=[
            jax.ShapeDtypeStruct((local_rows, width), BF16),
            jax.ShapeDtypeStruct((local_rows, NP * PW // cols), BF16),
        ],
        in_specs=[smem_spec()] * 3
        + [pl.BlockSpec((cols, block_rows, fan * held), lambda i: (0, i, 0))]
        + [whole_spec()] * 8
        + [any_spec()] * cols,
        out_specs=[
            pl.BlockSpec((block_rows, width), lambda i: (i, 0)),
            pl.BlockSpec((block_rows, NP * PW // cols), lambda i: (i, 0)),
        ],
        scratch_shapes=[
            pltpu.VMEM((kid_cols, local_rows), BF16),
            pltpu.VMEM((block_rows, NPIV), F32),
            pltpu.SemaphoreType.DMA((cols,)),
        ],
        compiler_params=params(),
        name="row_factors",
    )(
        place, own_group.astype(F32), own_kid.astype(F32), row_strips, group_piv[None, :], kid_piv[None, :], piv_t, lower,
        store_hi, store_lo, link_hi, link_lo, *own_kids,
    )

    block_cols = min(512, local_cols)
    count = cols * fan
    rhs = pl.pallas_call(
        functools.partial(
            col_kernel, (cols, fan, held, slice_cols, block_cols, local_rows, kid_cols)
        ),
        grid=(local_cols // block_cols,),
        out_shape=jax.ShapeDtypeStruct((width, local_cols), BF16),
        in_specs=[smem_spec()]
        + [whole_spec()] * 2
        + [pl.BlockSpec((1, block_cols), lambda j: (0, j))] * 2
        + [whole_spec()] * 5
        + [any_spec()] * (2 * count),
        out_specs=pl.BlockSpec((width, block_cols), lambda j: (0, j)),
        scratch_shapes=[
            pltpu.VMEM((NPIV, local_cols), BF16),
            pltpu.VMEM((kid_cols, local_cols), BF16),
            pltpu.SemaphoreType.DMA((2 * count,)),
        ],
        compiler_params=params(),
        name="col_factors",
    )(
        place, group_piv[:, None], kid_piv[:, None], group_all, kid_all, piv,
        flip_hi, flip_lo, link_hi, link_lo, *col_strips, *col_kids,
    )

    block_rows = min(512, local_rows)
    block_cols = min(1024, local_rows)
    schur_block = pl.pallas_call(
        functools.partial(schur_kernel, (block_rows, block_cols, local_rows, held)),
        grid=(local_cols // block_cols, local_rows // block_rows),
        out_shape=jax.ShapeDtypeStruct((local_rows, local_cols), F32),
        in_specs=[
            smem_spec(),
            pl.BlockSpec((block_rows, block_cols), lambda j, i: (i, j)),
            pl.BlockSpec((local_rows, width), lambda j, i: (0, 0)),
            pl.BlockSpec((width, block_cols), lambda j, i: (0, j)),
            pl.BlockSpec((1, block_cols), lambda j, i: (0, j)),
        ],
        out_specs=pl.BlockSpec((block_rows, block_cols), lambda j, i: (i, j)),
        compiler_params=params(),
        name="schur_update",
    )(own_group.astype(F32), front_entries, lead, rhs, group_all)
    return (factor_panels, schur_block)


def solution(mesh):
    placed = (P("row", "col"), P(), P("row", "col"), P())
    return jax.shard_map(
        local,
        mesh=mesh,
        in_specs=placed,
        out_specs=(P("row", "col"), P("row", "col")),
        check_vma=False,
    )
```

```python
import functools

import jax
import jax.numpy as jnp
from jax import lax
from jax.experimental import pallas as pl
from jax.experimental.pallas import tpu as pltpu
from jax.sharding import PartitionSpec as P

PW = 256
NP = 2
TS = 128
MT = 512
NPIV = NP * PW
BLK = 32
F32 = jnp.float32
BF16 = jnp.bfloat16
VMEM_BYTES = 50 * 1024 * 1024

NN = (((1,), (0,)), ((), ()))
NT = (((1,), (1,)), ((), ()))


def dot(left, right, dims=NN, precision=None):
    return lax.dot_general(left, right, dims, precision=precision, preferred_element_type=F32)


def exact(left, right, dims=NN):
    return dot(left, right, dims, lax.Precision.HIGHEST)


def split(value):
    high = value.astype(BF16)
    return high, (value - high.astype(F32)).astype(BF16)


def swapped(value, axis, mask):
    if mask == 0:
        return value
    return lax.ppermute(value, axis, [(i, i ^ mask) for i in range(lax.axis_size(axis))])


def whole_spec():
    return pl.BlockSpec(memory_space=pltpu.VMEM)


def smem_spec():
    return pl.BlockSpec(memory_space=pltpu.SMEM)


def factor_diagonal(block):
    groups = BLK // 8
    lane = lax.broadcasted_iota(jnp.int32, (BLK, 128), 1)
    row = lax.broadcasted_iota(jnp.int32, (BLK, 128), 0)
    row8 = lax.broadcasted_iota(jnp.int32, (8, 128), 0)
    start = jnp.where(lane < BLK, block, jnp.where(lane == row + BLK, 1.0, 0.0))
    work = [start[8 * g : 8 * g + 8] for g in range(groups)]
    cols = []
    for k in range(BLK):
        base = 8 * (k // 8)
        cols.append(jnp.broadcast_to(block[base:, k : k + 1], (BLK - base, 128)))
    scale = [jnp.ones((8, 128), F32) for _ in range(groups)]
    for j in range(BLK):
        g0 = j // 8
        base = 8 * g0
        column = cols[j]
        pivot = column[j - base : j - base + 1]
        root = lax.rsqrt(pivot)
        root = root * (1.5 - 0.5 * pivot * root * root)
        factor = jnp.where(row[base:] > j, column * (root * root), 0.0)
        lead = work[g0][j - base : j - base + 1]
        for g in range(g0, groups):
            work[g] = work[g] - factor[8 * (g - g0) : 8 * (g - g0) + 8] * lead
        for k in range(j + 1, BLK):
            skip = 8 * (k // 8 - g0)
            cols[k] = cols[k] - factor[skip:] * column[k - base : k - base + 1]
        scale[g0] = jnp.where(row8 == j - base, root, scale[g0])
    return jnp.concatenate([work[g] * scale[g] for g in range(groups)], axis=0)


def factor_panel(work):
    per_tile = 128 // BLK
    row = lax.broadcasted_iota(jnp.int32, (PW, BLK), 0)
    lane = lax.broadcasted_iota(jnp.int32, (BLK, 128), 1)

    def step(b, carry):
        low = pl.multiple_of(b * BLK, BLK)
        tile = pl.multiple_of((b // per_tile) * 128, 128)
        turn = (128 - (b % per_tile) * BLK) % 128
        columns = pltpu.roll(work[:, pl.ds(tile, 128)], turn, 1)
        block = pltpu.roll(work[pl.ds(low, BLK), pl.ds(tile, 128)], turn, 1)
        done = factor_diagonal(block)
        inverse = jnp.where(lane < BLK, pltpu.roll(done, 128 - BLK, 1), 0.0)
        upper = exact(inverse[:, :BLK], work[pl.ds(low, BLK), :])
        lead = exact(columns, inverse, NT)
        lead = jnp.where(row >= low + BLK, lead, 0.0)
        work[...] = work[...] - exact(lead, upper)
        work[pl.ds(low, BLK), :] = upper
        return carry

    lax.fori_loop(0, PW // BLK, step, 0)


def pivot_kernel(sizes, place, near, far, group_col, group_row, kid_col, kid_row,
                 lower, inv_hi, inv_lo, inv_t_hi, inv_t_lo, link_out, link_t, piv_t, piv,
                 pile, wide, work):
    cols, fan, share, held, slice_cols = sizes
    my_row, my_col = place[0], place[1]
    my_q, my_a = my_row % fan, my_row // fan
    col_share = PW // cols
    for dq, source in enumerate((near, far)):
        for d in range(cols):
            r = (my_a ^ d) * fan + (my_q ^ dq)
            pieces = [source[c ^ my_col, d, :held, :] for c in range(cols)]
            line = jnp.concatenate(
                [piece[:, k * col_share : (k + 1) * col_share] for k in range(NP) for piece in pieces],
                axis=1,
            )
            kids = []
            for e in range(cols):
                packed = source[e, d, held:, :]
                kids += [packed[:, :held], packed[:, held:]]
            kids = jnp.concatenate(kids, axis=0).T
            for k in range(NP):
                at = pl.ds(pl.multiple_of(k * PW + r * share, share), share)
                pile[at, :] = line[k * share : (k + 1) * share]
                wide[at, :] = kids[k * share : (k + 1) * share]
    piv[...] = wide[...].astype(BF16)
    piv_t[...] = wide[...].T.astype(BF16)
    product = dot(piv[...], piv_t[...])
    pile[...] = jnp.where(group_col[...] == group_row[...], pile[...], 0.0) + jnp.where(
        kid_col[...] == kid_row[...], product, 0.0
    )
    eye_row = lax.broadcasted_iota(jnp.int32, (PW, PW), 0)
    eye_col = lax.broadcasted_iota(jnp.int32, (PW, PW), 1)
    eye = jnp.where(eye_row == eye_col, 1.0, 0.0)

    def finish(k):
        part = slice(k * PW, (k + 1) * PW)
        lower[part, part] = jnp.where(eye_col <= eye_row, work[:, :PW].T, 0.0)
        inverse = work[:, PW:]
        inv_hi[part, :], inv_lo[part, :] = split(inverse)
        inv_t_hi[part, :], inv_t_lo[part, :] = split(inverse.T)
        return inverse

    work[:, :PW] = pile[:PW, :PW]
    work[:, PW:] = eye
    factor_panel(work)
    inverse = finish(0)
    lower[:PW, PW:] = jnp.zeros((PW, PW), F32)
    link = exact(pile[PW:, :PW], inverse, NT).astype(BF16)
    link_out[...] = link
    lower[PW:, :PW] = link.astype(F32)
    link_t[...] = link.astype(F32).T.astype(BF16)
    work[:, :PW] = pile[PW:, PW:] - dot(link, link, NT)
    work[:, PW:] = eye
    factor_panel(work)
    finish(1)


def place_kernel(sizes, place, inverse_map, *refs):
    cols, fan, tiles, slice_cols = sizes
    sources, outs = refs[:cols], refs[cols : 2 * cols]
    held = refs[2 * cols]
    my_row, my_col = place[0], place[1]
    my_q, my_a = my_row % fan, my_row // fan
    for d in range(cols):
        held[my_a ^ d] = sources[d][...]

    def fetch(block, i):
        tile = inverse_map[block * tiles + i]
        source = (tile // tiles) // fan
        at = pl.multiple_of((tile % tiles) * TS, TS)
        return held[source, :, pl.ds(at, TS)]

    for i in range(tiles):
        mine = fetch(my_row, i)
        for d in range(cols):
            outs[d][:slice_cols, i * TS : (i + 1) * TS] = mine
    for d in range(cols):
        for i in range(tiles):
            outs[d][slice_cols:, i * TS : (i + 1) * TS] = fetch((my_col ^ d) * fan + my_q, i)


def solve_rows(first, second, inv_hi, inv_lo, link):
    high, low = split(first)
    head = dot(high, inv_hi[:PW]) + dot(high, inv_lo[:PW]) + dot(low, inv_hi[:PW])
    high, low = split(second - dot(head.astype(BF16), link))
    tail = dot(high, inv_hi[PW:]) + dot(high, inv_lo[PW:]) + dot(low, inv_hi[PW:])
    return head, tail


def solve_cols(first, second, inv_hi, inv_lo, link):
    high, low = split(first)
    head = dot(inv_hi[:PW], high) + dot(inv_lo[:PW], high) + dot(inv_hi[:PW], low)
    high, low = split(second - dot(link, head.astype(BF16)))
    tail = dot(inv_hi[PW:], high) + dot(inv_lo[PW:], high) + dot(inv_hi[PW:], low)
    return head, tail


def row_kernel(sizes, place, group_of, kid_of, strips, group_row, kid_row, piv_t, lower,
               inv_t_hi, inv_t_lo, link_t, *refs):
    cols, share, slice_cols, block_rows, kid_cols = sizes
    sources = refs[:cols]
    lead, panel, solved = refs[cols:]
    my_row, my_col = place[0], place[1]
    step = pl.program_id(0)
    col_share = PW // cols
    subs = block_rows // TS
    own_t = jnp.concatenate([source[:slice_cols, :] for source in sources], axis=0)
    own = own_t.astype(F32).T.astype(BF16)
    product = dot(own, piv_t[...])
    entries = jnp.concatenate(
        [strips[c][:, k * col_share : (k + 1) * col_share] for k in range(NP) for c in range(cols)],
        axis=1,
    )
    parts = []
    for i in range(subs):
        tile = step * subs + i
        part = slice(i * TS, (i + 1) * TS)
        parts.append(
            jnp.where(group_row[...] == group_of[tile], entries[part], 0.0)
            + jnp.where(kid_row[...] == kid_of[tile], product[part], 0.0)
        )
    strip = jnp.concatenate(parts, axis=0)
    head, tail = solve_rows(strip[:, :PW], strip[:, PW:], inv_t_hi[...], inv_t_lo[...], link_t[...])
    solved[:, :PW] = head
    solved[:, PW:] = tail

    @pl.when(step == 0)
    def _():
        for k in range(NP):
            at = pl.multiple_of(k * PW + my_row * share, share)
            solved[k * share : (k + 1) * share, :] = lower[pl.ds(at, share), :]

    lead[:, :kid_cols] = own
    lead[:, kid_cols:] = solved[...].astype(BF16)
    per_tile = 128 // col_share
    lane = lax.broadcasted_iota(jnp.int32, (block_rows, 128), 1)
    out = jnp.zeros((block_rows, 128), F32)
    for k in range(NP):
        tile = pl.multiple_of(k * PW + (my_col // per_tile) * 128, 128)
        turn = (128 + k * col_share - (my_col % per_tile) * col_share) % 128
        moved = pltpu.roll(solved[:, pl.ds(tile, 128)], turn, 1)
        out = jnp.where(lane // col_share == k, moved, out)
    panel[...] = out[:, : NP * col_share].astype(BF16)


def schur_kernel(sizes, place, group_of, kid_of, front, lead, near_strips, far_strips, near_kids,
                 far_kids, group_all, kid_all, group_col, kid_col, piv, inv_hi, inv_lo, link,
                 out, strip, flipped, kids):
    cols, fan, share, held, block_rows, block_cols, local_rows, kid_cols = sizes
    my_row = place[0]
    my_q, my_a = my_row % fan, my_row // fan
    j, i = pl.program_id(0), pl.program_id(1)

    @pl.when(i == 0)
    def _():
        for dq, source in enumerate((near_strips, far_strips)):
            for d in range(cols):
                r = (my_a ^ d) * fan + (my_q ^ dq)
                piece = source[d * held : (d + 1) * held, :].astype(F32)
                for k in range(NP):
                    at = pl.ds(pl.multiple_of(k * PW + r * share, share), share)
                    strip[at, :] = piece[k * share : (k + 1) * share]
        q = (j * block_cols) // local_rows

        @pl.when(q == my_q)
        def _():
            kids[...] = near_kids[...]

        @pl.when(q != my_q)
        def _():
            kids[...] = far_kids[...]

        product = dot(piv[...], kids[...])
        full = jnp.where(group_col[...] == group_all[...], strip[...], 0.0) + jnp.where(
            kid_col[...] == kid_all[...], product, 0.0
        )
        head, tail = solve_cols(full[:PW], full[PW:], inv_hi[...], inv_lo[...], link[...])
        flipped[:PW] = (-head).astype(BF16)
        flipped[PW:] = (-tail).astype(BF16)

    at = pl.ds(pl.multiple_of(i * block_rows, block_rows), block_rows)
    update = dot(lead[at, kid_cols:], flipped[...])
    product = dot(lead[at, :kid_cols], kids[...])
    subs = block_rows // TS
    for sub in range(subs):
        tile = i * subs + sub
        part = slice(sub * TS, (sub + 1) * TS)
        out[part, :] = (
            jnp.where(group_all[...] == group_of[tile], front[part, :], 0.0)
            + jnp.where(kid_all[...] == kid_of[tile], product[part], 0.0)
            + update[part]
        )

    @pl.when(i == 0)
    def _():
        out[:held, :] = jnp.zeros((held, block_cols), F32)

    @pl.when((j * block_cols) % local_rows == 0)
    def _():
        out[:, :held] = jnp.zeros((block_rows, held), F32)


def params():
    return pltpu.CompilerParams(vmem_limit_bytes=VMEM_BYTES)


def local(front_entries, tile_group, child_factor, row_map):
    rows, cols = lax.axis_size("row"), lax.axis_size("col")
    fan = rows // cols
    assert fan == 2
    local_rows, local_cols = front_entries.shape
    slice_cols = child_factor.shape[1]
    kid_cols = slice_cols * cols
    tiles = local_rows // TS
    share = PW // rows
    held = NP * share
    my_row, my_col = lax.axis_index("row"), lax.axis_index("col")
    place = jnp.stack([my_row, my_col]).astype(jnp.int32)

    row_strip = jnp.concatenate(
        [
            front_entries[:, q * local_rows + k * share : q * local_rows + (k + 1) * share]
            for k in range(NP)
            for q in range(fan)
        ],
        axis=1,
    )
    row_strips = lax.all_gather(row_strip, "col", axis=0)
    col_strip = front_entries[:held].astype(BF16)

    flipped = child_factor.T
    own_map = lax.dynamic_slice_in_dim(row_map, my_row * tiles, tiles)
    starts = flipped.reshape(slice_cols, tiles, TS)[:, :, :held]

    def chosen(block):
        keep = (own_map == block * tiles)[None, :, None]
        return jnp.sum(jnp.where(keep, starts, 0), axis=1, dtype=F32)

    corner = jnp.concatenate(
        [
            front_entries[:held, q * local_rows + k * share : q * local_rows + (k + 1) * share]
            for k in range(NP)
            for q in range(fan)
        ],
        axis=1,
    )
    kids = jnp.concatenate([chosen(my_row), chosen(jnp.bitwise_xor(my_row, rows // 2))], axis=1)
    packet = jnp.concatenate([corner, kids], axis=0)
    packets = [swapped(packet, "row", d * fan) for d in range(cols)]
    flipped, col_strip, *packets = lax.optimization_barrier((flipped, col_strip, *packets))
    merged = []
    for d in range(cols):
        kid = packets[d][held:, :held] + packets[d ^ (cols // 2)][held:, held:]
        half = slice_cols // 2
        merged.append(
            jnp.concatenate(
                [packets[d][:held], jnp.concatenate([kid[:half], kid[half:]], axis=1)], axis=0
            )
        )
    merged = jnp.stack(merged)
    near = jnp.stack([swapped(merged, "col", d) for d in range(cols)])
    far = swapped(near, "row", 1)

    tile_ids = jnp.arange(row_map.shape[0], dtype=jnp.int32)
    inverse_map = jnp.sum(
        jnp.where(row_map[None, :] == tile_ids[:, None], tile_ids[None, :], 0), axis=1, dtype=jnp.int32
    )
    kid_of_tile = (inverse_map >= row_map.shape[0] // 2).astype(F32)
    group_of_tile = jnp.repeat(tile_group, MT // TS).astype(F32)
    own_kid = lax.dynamic_slice_in_dim(kid_of_tile, my_row * tiles, tiles)
    own_group = lax.dynamic_slice_in_dim(group_of_tile, my_row * tiles, tiles)
    col_kid = lax.dynamic_slice_in_dim(kid_of_tile, my_col * fan * tiles, fan * tiles)
    col_group = lax.dynamic_slice_in_dim(group_of_tile, my_col * fan * tiles, fan * tiles)
    kid_all = jnp.repeat(col_kid, TS)[None, :]
    group_all = jnp.repeat(col_group, TS)[None, :]
    kid_piv = jnp.tile(jnp.repeat(kid_of_tile[::tiles], share), NP)
    group_piv = jnp.tile(jnp.repeat(group_of_tile[::tiles], share), NP)

    kid_rows = [swapped(flipped, "row", d * fan) for d in range(cols)]
    col_strip, *kid_rows = lax.optimization_barrier((col_strip, *kid_rows))
    col_strips = [swapped(col_strip, "row", d * fan) for d in range(cols)]
    placed = pl.pallas_call(
        functools.partial(place_kernel, (cols, fan, tiles, slice_cols)),
        out_shape=[jax.ShapeDtypeStruct((2 * slice_cols, local_rows), BF16)] * cols,
        in_specs=[smem_spec()] * 2 + [whole_spec()] * cols,
        out_specs=[whole_spec()] * cols,
        scratch_shapes=[pltpu.VMEM((cols, slice_cols, local_rows), BF16)],
        compiler_params=params(),
        cost_estimate=pl.CostEstimate(flops=0, bytes_accessed=8 * 2**20, transcendentals=0),
        name="place_tiles",
    )(place, inverse_map, *kid_rows)
    near, far, *placed = lax.optimization_barrier((near, far, *placed))
    kid_parts = [swapped(placed[d], "col", d) for d in range(cols)]

    square = jax.ShapeDtypeStruct((NPIV, PW), BF16)
    small = jax.ShapeDtypeStruct((PW, PW), BF16)
    lower, inv_hi, inv_lo, inv_t_hi, inv_t_lo, link, link_t, piv_t, piv = pl.pallas_call(
        functools.partial(pivot_kernel, (cols, fan, share, held, slice_cols)),
        out_shape=[
            jax.ShapeDtypeStruct((NPIV, NPIV), F32),
            square, square, square, square, small, small,
            jax.ShapeDtypeStruct((kid_cols, NPIV), BF16),
            jax.ShapeDtypeStruct((NPIV, kid_cols), BF16),
        ],
        in_specs=[smem_spec()] + [whole_spec()] * 6,
        out_specs=[whole_spec()] * 9,
        scratch_shapes=[
            pltpu.VMEM((NPIV, NPIV), F32),
            pltpu.VMEM((NPIV, kid_cols), F32),
            pltpu.VMEM((PW, 2 * PW), F32),
        ],
        compiler_params=params(),
        cost_estimate=pl.CostEstimate(flops=4 * 10**10, bytes_accessed=10**8, transcendentals=0),
        name="pivot_block",
    )(place, near, far, group_piv[:, None], group_piv[None, :], kid_piv[:, None], kid_piv[None, :])

    link, *arrived = lax.optimization_barrier((link, *col_strips, *kid_parts))
    near_strips = jnp.concatenate(arrived[:cols], axis=0)
    kid_parts = arrived[cols:]
    near_kids = jnp.concatenate([part[slice_cols:] for part in kid_parts], axis=0)
    far_strips = swapped(near_strips, "row", 1)
    far_kids = swapped(near_kids, "row", 1)

    block_rows = min(512, local_rows)
    width = kid_cols + NPIV
    lead, factor_panels = pl.pallas_call(
        functools.partial(row_kernel, (cols, share, slice_cols, block_rows, kid_cols)),
        grid=(local_rows // block_rows,),
        out_shape=[
            jax.ShapeDtypeStruct((local_rows, width), BF16),
            jax.ShapeDtypeStruct((local_rows, NP * PW // cols), BF16),
        ],
        in_specs=[smem_spec()] * 3
        + [pl.BlockSpec((cols, block_rows, fan * held), lambda i: (0, i, 0))]
        + [whole_spec()] * 7
        + [pl.BlockSpec((2 * slice_cols, block_rows), lambda i: (0, i))] * cols,
        out_specs=[
            pl.BlockSpec((block_rows, width), lambda i: (i, 0)),
            pl.BlockSpec((block_rows, NP * PW // cols), lambda i: (i, 0)),
        ],
        scratch_shapes=[pltpu.VMEM((block_rows, NPIV), F32)],
        compiler_params=params(),
        cost_estimate=pl.CostEstimate(flops=8 * 10**9, bytes_accessed=2 * 10**7, transcendentals=0),
        name="row_factors",
    )(
        place, own_group, own_kid, row_strips, group_piv[None, :], kid_piv[None, :], piv_t, lower,
        inv_t_hi, inv_t_lo, link_t, *kid_parts,
    )

    block_cols = min(1024, local_rows)
    per_block = local_rows // block_cols
    schur_block = pl.pallas_call(
        functools.partial(
            schur_kernel, (cols, fan, share, held, block_rows, block_cols, local_rows, kid_cols)
        ),
        grid=(local_cols // block_cols, local_rows // block_rows),
        out_shape=jax.ShapeDtypeStruct((local_rows, local_cols), F32),
        in_specs=[smem_spec()] * 3
        + [
            pl.BlockSpec((block_rows, block_cols), lambda j, i: (i, j)),
            whole_spec(),
            pl.BlockSpec((cols * held, block_cols), lambda j, i: (0, j)),
            pl.BlockSpec((cols * held, block_cols), lambda j, i: (0, j)),
            pl.BlockSpec((kid_cols, block_cols), lambda j, i: (0, j % per_block)),
            pl.BlockSpec((kid_cols, block_cols), lambda j, i: (0, j % per_block)),
            pl.BlockSpec((1, block_cols), lambda j, i: (0, j)),
            pl.BlockSpec((1, block_cols), lambda j, i: (0, j)),
        ]
        + [whole_spec()] * 6,
        out_specs=pl.BlockSpec((block_rows, block_cols), lambda j, i: (i, j)),
        scratch_shapes=[
            pltpu.VMEM((NPIV, block_cols), F32),
            pltpu.VMEM((NPIV, block_cols), BF16),
            pltpu.VMEM((kid_cols, block_cols), BF16),
        ],
        compiler_params=params(),
        cost_estimate=pl.CostEstimate(flops=2 * 10**10, bytes_accessed=8 * 10**7, transcendentals=0),
        name="schur_update",
    )(
        place, own_group, own_kid, front_entries, lead, near_strips, far_strips, near_kids, far_kids,
        group_all, kid_all, group_piv[:, None], kid_piv[:, None], piv, inv_hi, inv_lo, link,
    )
    return (factor_panels, schur_block)


def solution(mesh):
    placed = (P("row", "col"), P(), P("row", "col"), P())
    return jax.shard_map(
        local,
        mesh=mesh,
        in_specs=placed,
        out_specs=(P("row", "col"), P("row", "col")),
        check_vma=False,
    )
```

```python
import functools

import jax
import jax.numpy as jnp
from jax import lax
from jax.experimental import pallas as pl
from jax.experimental.pallas import tpu as pltpu
from jax.sharding import PartitionSpec as P

PW = 256
NP = 2
TS = 128
MT = 512
NPIV = NP * PW
BLK = 32
F32 = jnp.float32
BF16 = jnp.bfloat16
VMEM_BYTES = 60 * 1024 * 1024

NN = (((1,), (0,)), ((), ()))
NT = (((1,), (1,)), ((), ()))


def dot(left, right, dims=NN, precision=None):
    return lax.dot_general(left, right, dims, precision=precision, preferred_element_type=F32)


def exact(left, right, dims=NN):
    return dot(left, right, dims, lax.Precision.HIGHEST)


def split(value):
    high = value.astype(BF16)
    return high, (value - high.astype(F32)).astype(BF16)


def swapped(value, axis, mask):
    if mask == 0:
        return value
    return lax.ppermute(value, axis, [(i, i ^ mask) for i in range(lax.axis_size(axis))])


def whole_spec():
    return pl.BlockSpec(memory_space=pltpu.VMEM)


def smem_spec():
    return pl.BlockSpec(memory_space=pltpu.SMEM)


def factor_diagonal(block):
    groups = BLK // 8
    lane = lax.broadcasted_iota(jnp.int32, (BLK, 128), 1)
    row = lax.broadcasted_iota(jnp.int32, (BLK, 128), 0)
    row8 = lax.broadcasted_iota(jnp.int32, (8, 128), 0)
    start = jnp.where(lane < BLK, block, jnp.where(lane == row + BLK, 1.0, 0.0))
    work = [start[8 * g : 8 * g + 8] for g in range(groups)]
    cols = []
    for k in range(BLK):
        base = 8 * (k // 8)
        cols.append(jnp.broadcast_to(block[base:, k : k + 1], (BLK - base, 128)))
    scale = [jnp.ones((8, 128), F32) for _ in range(groups)]
    for j in range(BLK):
        g0 = j // 8
        base = 8 * g0
        column = cols[j]
        pivot = column[j - base : j - base + 1]
        root = lax.rsqrt(pivot)
        root = root * (1.5 - 0.5 * pivot * root * root)
        factor = jnp.where(row[base:] > j, column * (root * root), 0.0)
        lead = work[g0][j - base : j - base + 1]
        for g in range(g0, groups):
            work[g] = work[g] - factor[8 * (g - g0) : 8 * (g - g0) + 8] * lead
        for k in range(j + 1, BLK):
            skip = 8 * (k // 8 - g0)
            cols[k] = cols[k] - factor[skip:] * column[k - base : k - base + 1]
        scale[g0] = jnp.where(row8 == j - base, root, scale[g0])
    return jnp.concatenate([work[g] * scale[g] for g in range(groups)], axis=0)


def factor_panel(work):
    per_tile = 128 // BLK
    row = lax.broadcasted_iota(jnp.int32, (PW, BLK), 0)
    lane = lax.broadcasted_iota(jnp.int32, (BLK, 128), 1)

    def step(b, carry):
        low = pl.multiple_of(b * BLK, BLK)
        tile = pl.multiple_of((b // per_tile) * 128, 128)
        turn = (128 - (b % per_tile) * BLK) % 128
        columns = pltpu.roll(work[:, pl.ds(tile, 128)], turn, 1)
        block = pltpu.roll(work[pl.ds(low, BLK), pl.ds(tile, 128)], turn, 1)
        done = factor_diagonal(block)
        inverse = jnp.where(lane < BLK, pltpu.roll(done, 128 - BLK, 1), 0.0)
        upper = exact(inverse[:, :BLK], work[pl.ds(low, BLK), :])
        lead = exact(columns, inverse, NT)
        lead = jnp.where(row >= low + BLK, lead, 0.0)
        work[...] = work[...] - exact(lead, upper)
        work[pl.ds(low, BLK), :] = upper
        return carry

    lax.fori_loop(0, PW // BLK, step, 0)


def pivot_values(table, stride, share, along_rows):
    shape = (NPIV, 1) if along_rows else (1, NPIV)
    block = lax.broadcasted_iota(jnp.int32, shape, 0 if along_rows else 1) % PW // share
    values = jnp.zeros(shape, F32)
    for r in range(PW // share):
        values = jnp.where(block == r, table[r * stride], values)
    return values


def tile_values(table, start, count):
    return jnp.concatenate([jnp.full((1, TS), table[start + i], F32) for i in range(count)], axis=1)


def finish_panel(work, lower, inv_hi, inv_lo, inv_t_hi, inv_t_lo):
    row = lax.broadcasted_iota(jnp.int32, (PW, PW), 0)
    col = lax.broadcasted_iota(jnp.int32, (PW, PW), 1)
    lower[:PW, :] = jnp.where(col <= row, work[:, :PW].T, 0.0)
    inverse = work[:, PW:]
    inv_hi[...], inv_lo[...] = split(inverse)
    inv_t_hi[...], inv_t_lo[...] = split(inverse.T)
    return inverse


def unit():
    row = lax.broadcasted_iota(jnp.int32, (PW, PW), 0)
    col = lax.broadcasted_iota(jnp.int32, (PW, PW), 1)
    return jnp.where(row == col, 1.0, 0.0)


def first_kernel(sizes, place, group_of, kid_of, near, far,
                 lower, inv_hi, inv_lo, inv_t_hi, inv_t_lo, link_out, link_t, rest, piv_t, piv,
                 pile, wide, work):
    cols, fan, share, held, tiles = sizes
    my_row, my_col = place[0], place[1]
    my_q, my_a = my_row % fan, my_row // fan
    col_share = PW // cols
    for dq, source in enumerate((near, far)):
        for d in range(cols):
            r = (my_a ^ d) * fan + (my_q ^ dq)
            pieces = [source[c ^ my_col, d, :held, :] for c in range(cols)]
            line = jnp.concatenate(
                [piece[:, k * col_share : (k + 1) * col_share] for k in range(NP) for piece in pieces],
                axis=1,
            )
            kids = []
            for e in range(cols):
                packed = source[e, d, held:, :]
                kids += [packed[:, :held], packed[:, held:]]
            kids = jnp.concatenate(kids, axis=0).T
            for k in range(NP):
                at = pl.ds(pl.multiple_of(k * PW + r * share, share), share)
                pile[at, :] = line[k * share : (k + 1) * share]
                wide[at, :] = kids[k * share : (k + 1) * share]
    piv[...] = wide[...].astype(BF16)
    piv_t[...] = wide[...].T.astype(BF16)
    product = dot(piv[...], piv_t[...])
    same_group = pivot_values(group_of, tiles, share, True) == pivot_values(group_of, tiles, share, False)
    same_kid = pivot_values(kid_of, tiles, share, True) == pivot_values(kid_of, tiles, share, False)
    pile[...] = jnp.where(same_group, pile[...], 0.0) + jnp.where(same_kid, product, 0.0)
    work[:, :PW] = pile[:PW, :PW]
    work[:, PW:] = unit()
    factor_panel(work)
    inverse = finish_panel(work, lower, inv_hi, inv_lo, inv_t_hi, inv_t_lo)
    link = exact(pile[PW:, :PW], inverse, NT).astype(BF16)
    link_out[...] = link
    lower[PW:, :] = link.astype(F32)
    link_t[...] = link.astype(F32).T.astype(BF16)
    rest[...] = pile[PW:, PW:] - dot(link, link, NT)


def second_kernel(rest, lower, inv_hi, inv_lo, inv_t_hi, inv_t_lo, work):
    work[:, :PW] = rest[...]
    work[:, PW:] = unit()
    factor_panel(work)
    finish_panel(work, lower, inv_hi, inv_lo, inv_t_hi, inv_t_lo)


def place_kernel(sizes, place, inverse_map, *refs):
    cols, fan, tiles, slice_cols = sizes
    sources, outs = refs[:cols], refs[cols : 2 * cols]
    held = refs[2 * cols]
    my_row, my_col = place[0], place[1]
    my_q, my_a = my_row % fan, my_row // fan
    for d in range(cols):
        held[my_a ^ d] = sources[d][...]

    def fetch(block, i):
        tile = inverse_map[block * tiles + i]
        source = (tile // tiles) // fan
        at = pl.multiple_of((tile % tiles) * TS, TS)
        return held[source, :, pl.ds(at, TS)]

    for i in range(tiles):
        mine = fetch(my_row, i)
        for d in range(cols):
            outs[d][:slice_cols, i * TS : (i + 1) * TS] = mine
    for d in range(cols):
        for i in range(tiles):
            outs[d][slice_cols:, i * TS : (i + 1) * TS] = fetch((my_col ^ d) * fan + my_q, i)


def solve_rows(first, second, inv1_hi, inv1_lo, inv2_hi, inv2_lo, link):
    high, low = split(first)
    head = dot(high, inv1_hi) + dot(high, inv1_lo) + dot(low, inv1_hi)
    high, low = split(second - dot(head.astype(BF16), link))
    tail = dot(high, inv2_hi) + dot(high, inv2_lo) + dot(low, inv2_hi)
    return head, tail


def solve_cols(first, second, inv1_hi, inv1_lo, inv2_hi, inv2_lo, link):
    high, low = split(first)
    head = dot(inv1_hi, high) + dot(inv1_lo, high) + dot(inv1_hi, low)
    high, low = split(second - dot(link, head.astype(BF16)))
    tail = dot(inv2_hi, high) + dot(inv2_lo, high) + dot(inv2_hi, low)
    return head, tail


def row_kernel(sizes, place, group_of, kid_of, strips, piv_t, lower1, lower2,
               inv1_hi, inv1_lo, inv2_hi, inv2_lo, link_t, *refs):
    cols, share, slice_cols, block_rows, kid_cols, tiles = sizes
    sources = refs[:cols]
    lead, panel, solved = refs[cols:]
    my_row, my_col = place[0], place[1]
    step = pl.program_id(0)
    col_share = PW // cols
    subs = block_rows // TS
    own_t = jnp.concatenate([source[:slice_cols, :] for source in sources], axis=0)
    own = own_t.astype(F32).T.astype(BF16)
    product = dot(own, piv_t[...])
    entries = jnp.concatenate(
        [strips[c][:, k * col_share : (k + 1) * col_share] for k in range(NP) for c in range(cols)],
        axis=1,
    )
    group_row = pivot_values(group_of, tiles, share, False)
    kid_row = pivot_values(kid_of, tiles, share, False)
    parts = []
    for i in range(subs):
        tile = my_row * tiles + step * subs + i
        part = slice(i * TS, (i + 1) * TS)
        parts.append(
            jnp.where(group_row == group_of[tile], entries[part], 0.0)
            + jnp.where(kid_row == kid_of[tile], product[part], 0.0)
        )
    strip = jnp.concatenate(parts, axis=0)
    head, tail = solve_rows(
        strip[:, :PW], strip[:, PW:], inv1_hi[...], inv1_lo[...], inv2_hi[...], inv2_lo[...], link_t[...]
    )
    solved[:, :PW] = head
    solved[:, PW:] = tail

    @pl.when(step == 0)
    def _():
        at = pl.multiple_of(my_row * share, share)
        solved[:share, :PW] = lower1[pl.ds(at, share), :]
        solved[:share, PW:] = jnp.zeros((share, PW), F32)
        solved[share : 2 * share, :PW] = lower1[pl.ds(PW + at, share), :]
        solved[share : 2 * share, PW:] = lower2[pl.ds(at, share), :]

    lead[:, :kid_cols] = own
    lead[:, kid_cols:] = solved[...].astype(BF16)
    per_tile = 128 // col_share
    lane = lax.broadcasted_iota(jnp.int32, (block_rows, 128), 1)
    out = jnp.zeros((block_rows, 128), F32)
    for k in range(NP):
        tile = pl.multiple_of(k * PW + (my_col // per_tile) * 128, 128)
        turn = (128 + k * col_share - (my_col % per_tile) * col_share) % 128
        moved = pltpu.roll(solved[:, pl.ds(tile, 128)], turn, 1)
        out = jnp.where(lane // col_share == k, moved, out)
    panel[...] = out[:, : NP * col_share].astype(BF16)


def schur_kernel(sizes, place, group_of, kid_of, front, lead, strips, near_kids, far_kids,
                 piv, inv1_hi, inv1_lo, inv2_hi, inv2_lo, link, out, strip, flipped, kids):
    rows, cols, fan, share, held, block_rows, block_cols, local_rows, kid_cols, tiles = sizes
    my_row, my_col = place[0], place[1]
    my_q = my_row % fan
    j, i = pl.program_id(0), pl.program_id(1)
    first_tile = my_col * fan * tiles + j * (block_cols // TS)
    group_all = tile_values(group_of, first_tile, block_cols // TS)
    kid_all = tile_values(kid_of, first_tile, block_cols // TS)

    @pl.when(i == 0)
    def _():
        for r in range(rows):
            piece = strips[r].astype(F32)
            for k in range(NP):
                at = k * PW + r * share
                strip[at : at + share, :] = piece[k * share : (k + 1) * share]
        q = (j * block_cols) // local_rows

        @pl.when(q == my_q)
        def _():
            kids[...] = near_kids[...]

        @pl.when(q != my_q)
        def _():
            kids[...] = far_kids[...]

        product = dot(piv[...], kids[...])
        group_col = pivot_values(group_of, tiles, share, True)
        kid_col = pivot_values(kid_of, tiles, share, True)
        full = jnp.where(group_col == group_all, strip[...], 0.0) + jnp.where(
            kid_col == kid_all, product, 0.0
        )
        head, tail = solve_cols(
            full[:PW], full[PW:], inv1_hi[...], inv1_lo[...], inv2_hi[...], inv2_lo[...], link[...]
        )
        flipped[:PW] = (-head).astype(BF16)
        flipped[PW:] = (-tail).astype(BF16)

    at = pl.ds(pl.multiple_of(i * block_rows, block_rows), block_rows)
    subs = block_rows // TS
    wide = min(256, block_cols)
    for n in range(block_cols // wide):
        span = slice(n * wide, (n + 1) * wide)
        update = dot(lead[at, kid_cols:], flipped[:, span])
        product = dot(lead[at, :kid_cols], kids[:, span])
        for sub in range(subs):
            tile = my_row * tiles + i * subs + sub
            part = slice(sub * TS, (sub + 1) * TS)
            out[part, span] = (
                jnp.where(group_all[:, span] == group_of[tile], front[part, span], 0.0)
                + jnp.where(kid_all[:, span] == kid_of[tile], product[part], 0.0)
                + update[part]
            )

    @pl.when(i == 0)
    def _():
        out[:held, :] = jnp.zeros((held, block_cols), F32)

    @pl.when((j * block_cols) % local_rows == 0)
    def _():
        out[:, :held] = jnp.zeros((block_rows, held), F32)


def params():
    return pltpu.CompilerParams(vmem_limit_bytes=VMEM_BYTES)


def local(front_entries, tile_group, child_factor, row_map):
    rows, cols = lax.axis_size("row"), lax.axis_size("col")
    fan = rows // cols
    assert fan == 2
    local_rows, local_cols = front_entries.shape
    slice_cols = child_factor.shape[1]
    kid_cols = slice_cols * cols
    tiles = local_rows // TS
    share = PW // rows
    held = NP * share
    my_row, my_col = lax.axis_index("row"), lax.axis_index("col")
    place = jnp.stack([my_row, my_col]).astype(jnp.int32)

    row_strip = jnp.concatenate(
        [
            front_entries[:, q * local_rows + k * share : q * local_rows + (k + 1) * share]
            for k in range(NP)
            for q in range(fan)
        ],
        axis=1,
    )
    row_strips = lax.all_gather(row_strip, "col", axis=0)
    col_strips = lax.all_gather(front_entries[:held].astype(BF16), "row", axis=0)

    flipped = child_factor.T
    own_map = lax.dynamic_slice_in_dim(row_map, my_row * tiles, tiles)
    starts = flipped.reshape(slice_cols, tiles, TS)[:, :, :held]

    def chosen(block):
        keep = (own_map == block * tiles)[None, :, None]
        return jnp.sum(jnp.where(keep, starts, 0), axis=1, dtype=F32)

    corner = jnp.concatenate(
        [
            front_entries[:held, q * local_rows + k * share : q * local_rows + (k + 1) * share]
            for k in range(NP)
            for q in range(fan)
        ],
        axis=1,
    )
    kids = jnp.concatenate([chosen(my_row), chosen(jnp.bitwise_xor(my_row, rows // 2))], axis=1)
    packet = jnp.concatenate([corner, kids], axis=0)
    packets = [swapped(packet, "row", d * fan) for d in range(cols)]
    flipped, *packets = lax.optimization_barrier((flipped, *packets))
    merged = []
    for d in range(cols):
        kid = packets[d][held:, :held] + packets[d ^ (cols // 2)][held:, held:]
        half = slice_cols // 2
        merged.append(
            jnp.concatenate(
                [packets[d][:held], jnp.concatenate([kid[:half], kid[half:]], axis=1)], axis=0
            )
        )
    merged = jnp.stack(merged)
    near = jnp.stack([swapped(merged, "col", d) for d in range(cols)])
    far = swapped(near, "row", 1)

    tile_ids = jnp.arange(row_map.shape[0], dtype=jnp.int32)
    inverse_map = jnp.sum(
        jnp.where(row_map[None, :] == tile_ids[:, None], tile_ids[None, :], 0), axis=1, dtype=jnp.int32
    )
    kid_of = (inverse_map >= row_map.shape[0] // 2).astype(F32)
    group_of = jnp.repeat(tile_group, MT // TS).astype(F32)

    kid_rows = [swapped(flipped, "row", d * fan) for d in range(cols)]
    square = jax.ShapeDtypeStruct((PW, PW), BF16)
    lower1, inv1_hi, inv1_lo, inv1_t_hi, inv1_t_lo, link, link_t, rest, piv_t, piv = pl.pallas_call(
        functools.partial(first_kernel, (cols, fan, share, held, tiles)),
        out_shape=[
            jax.ShapeDtypeStruct((2 * PW, PW), F32),
            square, square, square, square, square, square,
            jax.ShapeDtypeStruct((PW, PW), F32),
            jax.ShapeDtypeStruct((kid_cols, NPIV), BF16),
            jax.ShapeDtypeStruct((NPIV, kid_cols), BF16),
        ],
        in_specs=[smem_spec()] * 3 + [whole_spec()] * 2,
        out_specs=[whole_spec()] * 10,
        scratch_shapes=[
            pltpu.VMEM((NPIV, NPIV), F32),
            pltpu.VMEM((NPIV, kid_cols), F32),
            pltpu.VMEM((PW, 2 * PW), F32),
        ],
        compiler_params=params(),
        cost_estimate=pl.CostEstimate(flops=2 * 10**10, bytes_accessed=5 * 10**7, transcendentals=0),
        name="first_pivots",
    )(place, group_of, kid_of, near, far)

    rest, *kid_rows = lax.optimization_barrier((rest, *kid_rows))
    placed = pl.pallas_call(
        functools.partial(place_kernel, (cols, fan, tiles, slice_cols)),
        out_shape=[jax.ShapeDtypeStruct((2 * slice_cols, local_rows), BF16)] * cols,
        in_specs=[smem_spec()] * 2 + [whole_spec()] * cols,
        out_specs=[whole_spec()] * cols,
        scratch_shapes=[pltpu.VMEM((cols, slice_cols, local_rows), BF16)],
        compiler_params=params(),
        cost_estimate=pl.CostEstimate(flops=0, bytes_accessed=8 * 2**20, transcendentals=0),
        name="place_tiles",
    )(place, inverse_map, *kid_rows)
    rest, *placed = lax.optimization_barrier((rest, *placed))
    kid_parts = [swapped(placed[d], "col", d) for d in range(cols)]

    lower2, inv2_hi, inv2_lo, inv2_t_hi, inv2_t_lo = pl.pallas_call(
        second_kernel,
        out_shape=[jax.ShapeDtypeStruct((PW, PW), F32), square, square, square, square],
        in_specs=[whole_spec()],
        out_specs=[whole_spec()] * 5,
        scratch_shapes=[pltpu.VMEM((PW, 2 * PW), F32)],
        compiler_params=params(),
        cost_estimate=pl.CostEstimate(flops=2 * 10**10, bytes_accessed=5 * 10**7, transcendentals=0),
        name="second_pivots",
    )(rest)

    lower2, *kid_parts = lax.optimization_barrier((lower2, *kid_parts))
    near_kids = jnp.concatenate([part[slice_cols:] for part in kid_parts], axis=0)
    far_kids = swapped(near_kids, "row", 1)

    block_rows = min(512, local_rows)
    width = kid_cols + NPIV
    lead, factor_panels = pl.pallas_call(
        functools.partial(row_kernel, (cols, share, slice_cols, block_rows, kid_cols, tiles)),
        grid=(local_rows // block_rows,),
        out_shape=[
            jax.ShapeDtypeStruct((local_rows, width), BF16),
            jax.ShapeDtypeStruct((local_rows, NP * PW // cols), BF16),
        ],
        in_specs=[smem_spec()] * 3
        + [pl.BlockSpec((cols, block_rows, fan * held), lambda i: (0, i, 0))]
        + [whole_spec()] * 8
        + [pl.BlockSpec((2 * slice_cols, block_rows), lambda i: (0, i))] * cols,
        out_specs=[
            pl.BlockSpec((block_rows, width), lambda i: (i, 0)),
            pl.BlockSpec((block_rows, NP * PW // cols), lambda i: (i, 0)),
        ],
        scratch_shapes=[pltpu.VMEM((block_rows, NPIV), F32)],
        compiler_params=params(),
        cost_estimate=pl.CostEstimate(flops=8 * 10**9, bytes_accessed=2 * 10**7, transcendentals=0),
        name="row_factors",
    )(
        place, group_of, kid_of, row_strips, piv_t, lower1, lower2,
        inv1_t_hi, inv1_t_lo, inv2_t_hi, inv2_t_lo, link_t, *kid_parts,
    )

    block_rows = min(1024, local_rows)
    block_cols = min(512, local_rows)
    per_block = local_rows // block_cols
    schur_block = pl.pallas_call(
        functools.partial(
            schur_kernel,
            (rows, cols, fan, share, held, block_rows, block_cols, local_rows, kid_cols, tiles),
        ),
        grid=(local_cols // block_cols, local_rows // block_rows),
        out_shape=jax.ShapeDtypeStruct((local_rows, local_cols), F32),
        in_specs=[smem_spec()] * 3
        + [
            pl.BlockSpec((block_rows, block_cols), lambda j, i: (i, j)),
            whole_spec(),
            pl.BlockSpec((rows, held, block_cols), lambda j, i: (0, 0, j)),
            pl.BlockSpec((kid_cols, block_cols), lambda j, i: (0, j % per_block)),
            pl.BlockSpec((kid_cols, block_cols), lambda j, i: (0, j % per_block)),
        ]
        + [whole_spec()] * 6,
        out_specs=pl.BlockSpec((block_rows, block_cols), lambda j, i: (i, j)),
        scratch_shapes=[
            pltpu.VMEM((NPIV, block_cols), F32),
            pltpu.VMEM((NPIV, block_cols), BF16),
            pltpu.VMEM((kid_cols, block_cols), BF16),
        ],
        compiler_params=params(),
        cost_estimate=pl.CostEstimate(flops=2 * 10**10, bytes_accessed=8 * 10**7, transcendentals=0),
        name="schur_update",
    )(
        place, group_of, kid_of, front_entries, lead, col_strips, near_kids, far_kids,
        piv, inv1_hi, inv1_lo, inv2_hi, inv2_lo, link,
    )
    return (factor_panels, schur_block)


def solution(mesh):
    placed = (P("row", "col"), P(), P("row", "col"), P())
    return jax.shard_map(
        local,
        mesh=mesh,
        in_specs=placed,
        out_specs=(P("row", "col"), P("row", "col")),
        check_vma=False,
    )
```

```python
import functools

import jax
import jax.numpy as jnp
from jax import lax
from jax.experimental import pallas as pl
from jax.experimental.pallas import tpu as pltpu
from jax.sharding import PartitionSpec as P

PW = 256
NP = 2
TS = 128
MT = 512
NPIV = NP * PW
BLK = 32
F32 = jnp.float32
BF16 = jnp.bfloat16
VMEM_BYTES = 60 * 1024 * 1024

NN = (((1,), (0,)), ((), ()))
NT = (((1,), (1,)), ((), ()))


def dot(left, right, dims=NN, precision=None):
    return lax.dot_general(left, right, dims, precision=precision, preferred_element_type=F32)


def exact(left, right, dims=NN):
    return dot(left, right, dims, lax.Precision.HIGHEST)


def split(value):
    high = value.astype(BF16)
    return high, (value - high.astype(F32)).astype(BF16)


def swapped(value, axis, mask):
    if mask == 0:
        return value
    return lax.ppermute(value, axis, [(i, i ^ mask) for i in range(lax.axis_size(axis))])


def whole_spec():
    return pl.BlockSpec(memory_space=pltpu.VMEM)


def smem_spec():
    return pl.BlockSpec(memory_space=pltpu.SMEM)


def factor_diagonal(block):
    groups = BLK // 8
    lane = lax.broadcasted_iota(jnp.int32, (BLK, 128), 1)
    row = lax.broadcasted_iota(jnp.int32, (BLK, 128), 0)
    row8 = lax.broadcasted_iota(jnp.int32, (8, 128), 0)
    start = jnp.where(lane < BLK, block, jnp.where(lane == row + BLK, 1.0, 0.0))
    work = [start[8 * g : 8 * g + 8] for g in range(groups)]
    cols = []
    for k in range(BLK):
        base = 8 * (k // 8)
        cols.append(jnp.broadcast_to(block[base:, k : k + 1], (BLK - base, 128)))
    scale = [jnp.ones((8, 128), F32) for _ in range(groups)]
    for j in range(BLK):
        g0 = j // 8
        base = 8 * g0
        column = cols[j]
        pivot = column[j - base : j - base + 1]
        root = lax.rsqrt(pivot)
        root = root * (1.5 - 0.5 * pivot * root * root)
        factor = jnp.where(row[base:] > j, column * (root * root), 0.0)
        lead = work[g0][j - base : j - base + 1]
        for g in range(g0, groups):
            work[g] = work[g] - factor[8 * (g - g0) : 8 * (g - g0) + 8] * lead
        for k in range(j + 1, BLK):
            skip = 8 * (k // 8 - g0)
            cols[k] = cols[k] - factor[skip:] * column[k - base : k - base + 1]
        scale[g0] = jnp.where(row8 == j - base, root, scale[g0])
    return jnp.concatenate([work[g] * scale[g] for g in range(groups)], axis=0)


def factor_panel(work):
    per_tile = 128 // BLK
    row = lax.broadcasted_iota(jnp.int32, (PW, BLK), 0)
    lane = lax.broadcasted_iota(jnp.int32, (BLK, 128), 1)

    def step(b, carry):
        low = pl.multiple_of(b * BLK, BLK)
        tile = pl.multiple_of((b // per_tile) * 128, 128)
        turn = (128 - (b % per_tile) * BLK) % 128
        columns = pltpu.roll(work[:, pl.ds(tile, 128)], turn, 1)
        block = pltpu.roll(work[pl.ds(low, BLK), pl.ds(tile, 128)], turn, 1)
        done = factor_diagonal(block)
        inverse = jnp.where(lane < BLK, pltpu.roll(done, 128 - BLK, 1), 0.0)
        upper = exact(inverse[:, :BLK], work[pl.ds(low, BLK), :])
        lead = exact(columns, inverse, NT)
        lead = jnp.where(row >= low + BLK, lead, 0.0)
        work[...] = work[...] - exact(lead, upper)
        work[pl.ds(low, BLK), :] = upper
        return carry

    lax.fori_loop(0, PW // BLK, step, 0)


def pivot_values(table, stride, share, along_rows):
    shape = (NPIV, 1) if along_rows else (1, NPIV)
    block = lax.broadcasted_iota(jnp.int32, shape, 0 if along_rows else 1) % PW // share
    values = jnp.zeros(shape, F32)
    for r in range(PW // share):
        values = jnp.where(block == r, table[r * stride], values)
    return values


def tile_values(table, start, count):
    return jnp.concatenate([jnp.full((1, TS), table[start + i], F32) for i in range(count)], axis=1)


def finish_panel(work, lower, inv_hi, inv_lo, inv_t_hi, inv_t_lo):
    row = lax.broadcasted_iota(jnp.int32, (PW, PW), 0)
    col = lax.broadcasted_iota(jnp.int32, (PW, PW), 1)
    lower[:PW, :] = jnp.where(col <= row, work[:, :PW].T, 0.0)
    inverse = work[:, PW:]
    inv_hi[...], inv_lo[...] = split(inverse)
    inv_t_hi[...], inv_t_lo[...] = split(inverse.T)
    return inverse


def unit():
    row = lax.broadcasted_iota(jnp.int32, (PW, PW), 0)
    col = lax.broadcasted_iota(jnp.int32, (PW, PW), 1)
    return jnp.where(row == col, 1.0, 0.0)


def first_kernel(sizes, place, group_of, kid_of, near, far,
                 lower, inv_hi, inv_lo, inv_t_hi, inv_t_lo, link_out, link_t, rest, piv_t, piv,
                 pile, wide, work):
    cols, fan, share, held, tiles = sizes
    my_row, my_col = place[0], place[1]
    my_q, my_a = my_row % fan, my_row // fan
    col_share = PW // cols
    for dq, source in enumerate((near, far)):
        for d in range(cols):
            r = (my_a ^ d) * fan + (my_q ^ dq)
            pieces = [source[c ^ my_col, d, :held, :] for c in range(cols)]
            line = jnp.concatenate(
                [piece[:, k * col_share : (k + 1) * col_share] for k in range(NP) for piece in pieces],
                axis=1,
            )
            kids = []
            for e in range(cols):
                packed = source[e, d, held:, :]
                kids += [packed[:, :held], packed[:, held:]]
            kids = jnp.concatenate(kids, axis=0).T
            for k in range(NP):
                at = pl.ds(pl.multiple_of(k * PW + r * share, share), share)
                pile[at, :] = line[k * share : (k + 1) * share]
                wide[at, :] = kids[k * share : (k + 1) * share]
    piv[...] = wide[...].astype(BF16)
    piv_t[...] = wide[...].T.astype(BF16)
    product = dot(piv[...], piv_t[...])
    same_group = pivot_values(group_of, tiles, share, True) == pivot_values(group_of, tiles, share, False)
    same_kid = pivot_values(kid_of, tiles, share, True) == pivot_values(kid_of, tiles, share, False)
    pile[...] = jnp.where(same_group, pile[...], 0.0) + jnp.where(same_kid, product, 0.0)
    work[:, :PW] = pile[:PW, :PW]
    work[:, PW:] = unit()
    factor_panel(work)
    inverse = finish_panel(work, lower, inv_hi, inv_lo, inv_t_hi, inv_t_lo)
    link = exact(pile[PW:, :PW], inverse, NT).astype(BF16)
    link_out[...] = link
    lower[PW:, :] = link.astype(F32)
    link_t[...] = link.astype(F32).T.astype(BF16)
    rest[...] = pile[PW:, PW:] - dot(link, link, NT)


def second_kernel(rest, lower, inv_hi, inv_lo, inv_t_hi, inv_t_lo, work):
    work[:, :PW] = rest[...]
    work[:, PW:] = unit()
    factor_panel(work)
    finish_panel(work, lower, inv_hi, inv_lo, inv_t_hi, inv_t_lo)


def place_kernel(sizes, place, inverse_map, *refs):
    cols, fan, tiles, slice_cols = sizes
    sources, outs = refs[:cols], refs[cols : 2 * cols]
    held = refs[2 * cols]
    my_row, my_col = place[0], place[1]
    my_q, my_a = my_row % fan, my_row // fan
    for d in range(cols):
        held[my_a ^ d] = sources[d][...]

    def fetch(block, i):
        tile = inverse_map[block * tiles + i]
        source = (tile // tiles) // fan
        at = pl.multiple_of((tile % tiles) * TS, TS)
        return held[source, :, pl.ds(at, TS)]

    for i in range(tiles):
        mine = fetch(my_row, i)
        for d in range(cols):
            outs[d][:slice_cols, i * TS : (i + 1) * TS] = mine
    for d in range(cols):
        for i in range(tiles):
            outs[d][slice_cols:, i * TS : (i + 1) * TS] = fetch((my_col ^ d) * fan + my_q, i)


def solve_rows(first, second, inv1_hi, inv1_lo, inv2_hi, inv2_lo, link):
    high, low = split(first)
    head = dot(high, inv1_hi) + dot(high, inv1_lo) + dot(low, inv1_hi)
    high, low = split(second - dot(head.astype(BF16), link))
    tail = dot(high, inv2_hi) + dot(high, inv2_lo) + dot(low, inv2_hi)
    return head, tail


def solve_cols(first, second, inv1_hi, inv1_lo, inv2_hi, inv2_lo, link):
    def apply(inv_hi, inv_lo, value):
        high, low = split(value)
        both = dot(jnp.concatenate([inv_hi, inv_lo], axis=0), high)
        return both[:PW] + both[PW:] + dot(inv_hi, low)

    head = apply(inv1_hi, inv1_lo, first)
    return head, apply(inv2_hi, inv2_lo, second - dot(link, head.astype(BF16)))


def row_kernel(sizes, masks, place, group_of, kid_of, piv_t, lower1, lower2,
               inv1_hi, inv1_lo, inv2_hi, inv2_lo, link_t, *refs):
    cols, share, slice_cols, block_rows, kid_cols, tiles = sizes
    sources = refs[:cols]
    halves = [refs[cols : cols + 2], refs[cols + 2 : cols + 4]]
    lead, panel, solved, strips = refs[cols + 4 :]
    my_row, my_col = place[0], place[1]
    step = pl.program_id(0)
    for half in range(2):

        @pl.when(step // (pl.num_programs(0) // 2) == half)
        def _():
            for i, mask in enumerate(masks[half]):
                source = halves[half][i // (cols // 2)]
                strips[my_col ^ mask] = source[i % (cols // 2)]

    col_share = PW // cols
    subs = block_rows // TS
    own_t = jnp.concatenate([source[:slice_cols, :] for source in sources], axis=0)
    own = own_t.astype(F32).T.astype(BF16)
    product = dot(own, piv_t[...])
    entries = jnp.concatenate(
        [strips[c][:, k * col_share : (k + 1) * col_share] for k in range(NP) for c in range(cols)],
        axis=1,
    )
    group_row = pivot_values(group_of, tiles, share, False)
    kid_row = pivot_values(kid_of, tiles, share, False)
    parts = []
    for i in range(subs):
        tile = my_row * tiles + step * subs + i
        part = slice(i * TS, (i + 1) * TS)
        parts.append(
            jnp.where(group_row == group_of[tile], entries[part], 0.0)
            + jnp.where(kid_row == kid_of[tile], product[part], 0.0)
        )
    strip = jnp.concatenate(parts, axis=0)
    head, tail = solve_rows(
        strip[:, :PW], strip[:, PW:], inv1_hi[...], inv1_lo[...], inv2_hi[...], inv2_lo[...], link_t[...]
    )
    solved[:, :PW] = head
    solved[:, PW:] = tail

    @pl.when(step == 0)
    def _():
        at = pl.multiple_of(my_row * share, share)
        solved[:share, :PW] = lower1[pl.ds(at, share), :]
        solved[:share, PW:] = jnp.zeros((share, PW), F32)
        solved[share : 2 * share, :PW] = lower1[pl.ds(PW + at, share), :]
        solved[share : 2 * share, PW:] = lower2[pl.ds(at, share), :]

    for i in range(subs):
        part = slice(i * TS, (i + 1) * TS)
        mine = own[part].astype(F32)
        second = jnp.full(mine.shape, kid_of[my_row * tiles + step * subs + i], F32) > 0.5
        lead[part, :kid_cols] = jnp.where(second, 0.0, mine).astype(BF16)
        lead[part, kid_cols : 2 * kid_cols] = jnp.where(second, mine, 0.0).astype(BF16)
    lead[:, 2 * kid_cols :] = solved[...].astype(BF16)
    per_tile = 128 // col_share
    lane = lax.broadcasted_iota(jnp.int32, (block_rows, 128), 1)
    out = jnp.zeros((block_rows, 128), F32)
    for k in range(NP):
        tile = pl.multiple_of(k * PW + (my_col // per_tile) * 128, 128)
        turn = (128 + k * col_share - (my_col % per_tile) * col_share) % 128
        moved = pltpu.roll(solved[:, pl.ds(tile, 128)], turn, 1)
        out = jnp.where(lane // col_share == k, moved, out)
    panel[...] = out[:, : NP * col_share].astype(BF16)


def col_kernel(sizes, place, group_of, kid_of, strips, near_kids, far_kids,
               piv, inv1_hi, inv1_lo, inv2_hi, inv2_lo, link, out, strip, kids):
    rows, fan, share, block_cols, local_rows, kid_cols, tiles = sizes
    my_row, my_col = place[0], place[1]
    my_q = my_row % fan
    j = pl.program_id(0)
    first_tile = my_col * fan * tiles + j * (block_cols // TS)
    group_all = tile_values(group_of, first_tile, block_cols // TS)
    kid_all = tile_values(kid_of, first_tile, block_cols // TS)
    for r in range(rows):
        piece = strips[r].astype(F32)
        for k in range(NP):
            at = k * PW + r * share
            strip[at : at + share, :] = piece[k * share : (k + 1) * share]
    q = (j * block_cols) // local_rows

    @pl.when(q == my_q)
    def _():
        kids[...] = near_kids[...]

    @pl.when(q != my_q)
    def _():
        kids[...] = far_kids[...]

    product = dot(piv[...], kids[...])
    group_col = pivot_values(group_of, tiles, share, True)
    kid_col = pivot_values(kid_of, tiles, share, True)
    full = jnp.where(group_col == group_all, strip[...], 0.0) + jnp.where(
        kid_col == kid_all, product, 0.0
    )
    head, tail = solve_cols(
        full[:PW], full[PW:], inv1_hi[...], inv1_lo[...], inv2_hi[...], inv2_lo[...], link[...]
    )
    mine = kids[...].astype(F32)
    out[:kid_cols] = jnp.where(kid_all == 0.0, mine, 0.0).astype(BF16)
    out[kid_cols : 2 * kid_cols] = jnp.where(kid_all == 1.0, mine, 0.0).astype(BF16)
    out[2 * kid_cols : 2 * kid_cols + PW] = (-head).astype(BF16)
    out[2 * kid_cols + PW :] = (-tail).astype(BF16)


def params():
    return pltpu.CompilerParams(vmem_limit_bytes=VMEM_BYTES)


def local(front_entries, tile_group, child_factor, row_map):
    rows, cols = lax.axis_size("row"), lax.axis_size("col")
    fan = rows // cols
    assert fan == 2
    local_rows, local_cols = front_entries.shape
    slice_cols = child_factor.shape[1]
    kid_cols = slice_cols * cols
    tiles = local_rows // TS
    share = PW // rows
    held = NP * share
    my_row, my_col = lax.axis_index("row"), lax.axis_index("col")
    place = jnp.stack([my_row, my_col]).astype(jnp.int32)

    flipped = child_factor.T
    own_map = lax.dynamic_slice_in_dim(row_map, my_row * tiles, tiles)
    starts = flipped.reshape(slice_cols, tiles, TS)[:, :, :held]

    def chosen(block):
        keep = (own_map == block * tiles)[None, :, None]
        return jnp.sum(jnp.where(keep, starts, 0), axis=1, dtype=F32)

    corner = jnp.concatenate(
        [
            front_entries[:held, q * local_rows + k * share : q * local_rows + (k + 1) * share]
            for k in range(NP)
            for q in range(fan)
        ],
        axis=1,
    )
    kids = jnp.concatenate([chosen(my_row), chosen(jnp.bitwise_xor(my_row, rows // 2))], axis=1)
    packet = jnp.concatenate([corner, kids], axis=0)
    packets = [swapped(packet, "row", d * fan) for d in range(cols)]

    row_strip = jnp.concatenate(
        [
            front_entries[:, q * local_rows + k * share : q * local_rows + (k + 1) * share]
            for k in range(NP)
            for q in range(fan)
        ],
        axis=1,
    )
    steps = [1 << i for i in range(cols.bit_length() - 1)]
    orders = [steps, steps[::-1]]
    halves = [row_strip[None, : local_rows // 2], row_strip[None, local_rows // 2 :]]
    masks = [[0], [0]]
    for h in range(2):
        for step in orders[h][:-1]:
            halves[h] = jnp.concatenate([halves[h], swapped(halves[h], "col", step)], axis=0)
            masks[h] = masks[h] + [m ^ step for m in masks[h]]
    col_strips = lax.all_gather(front_entries[:held].astype(BF16), "row", axis=0)
    flipped, *packets = lax.optimization_barrier((flipped, *packets))
    merged = []
    for d in range(cols):
        kid = packets[d][held:, :held] + packets[d ^ (cols // 2)][held:, held:]
        half = slice_cols // 2
        merged.append(
            jnp.concatenate(
                [packets[d][:held], jnp.concatenate([kid[:half], kid[half:]], axis=1)], axis=0
            )
        )
    merged = jnp.stack(merged)
    near = jnp.stack([swapped(merged, "col", d) for d in range(cols)])
    far = swapped(near, "row", 1)
    near, far, *halves = lax.optimization_barrier((near, far, *halves))
    others = [swapped(halves[h], "col", orders[h][-1]) for h in range(2)]
    masks = [masks[h] + [m ^ orders[h][-1] for m in masks[h]] for h in range(2)]

    tile_ids = jnp.arange(row_map.shape[0], dtype=jnp.int32)
    inverse_map = jnp.sum(
        jnp.where(row_map[None, :] == tile_ids[:, None], tile_ids[None, :], 0), axis=1, dtype=jnp.int32
    )
    kid_of = (inverse_map >= row_map.shape[0] // 2).astype(F32)
    group_of = jnp.repeat(tile_group, MT // TS).astype(F32)

    kid_rows = [swapped(flipped, "row", d * fan) for d in range(cols)]
    square = jax.ShapeDtypeStruct((PW, PW), BF16)
    lower1, inv1_hi, inv1_lo, inv1_t_hi, inv1_t_lo, link, link_t, rest, piv_t, piv = pl.pallas_call(
        functools.partial(first_kernel, (cols, fan, share, held, tiles)),
        out_shape=[
            jax.ShapeDtypeStruct((2 * PW, PW), F32),
            square, square, square, square, square, square,
            jax.ShapeDtypeStruct((PW, PW), F32),
            jax.ShapeDtypeStruct((kid_cols, NPIV), BF16),
            jax.ShapeDtypeStruct((NPIV, kid_cols), BF16),
        ],
        in_specs=[smem_spec()] * 3 + [whole_spec()] * 2,
        out_specs=[whole_spec()] * 10,
        scratch_shapes=[
            pltpu.VMEM((NPIV, NPIV), F32),
            pltpu.VMEM((NPIV, kid_cols), F32),
            pltpu.VMEM((PW, 2 * PW), F32),
        ],
        compiler_params=params(),
        cost_estimate=pl.CostEstimate(flops=2 * 10**10, bytes_accessed=5 * 10**7, transcendentals=0),
        name="first_pivots",
    )(place, group_of, kid_of, near, far)

    rest, others[0], others[1], *kid_rows = lax.optimization_barrier((rest, *others, *kid_rows))
    placed = pl.pallas_call(
        functools.partial(place_kernel, (cols, fan, tiles, slice_cols)),
        out_shape=[jax.ShapeDtypeStruct((2 * slice_cols, local_rows), BF16)] * cols,
        in_specs=[smem_spec()] * 2 + [whole_spec()] * cols,
        out_specs=[whole_spec()] * cols,
        scratch_shapes=[pltpu.VMEM((cols, slice_cols, local_rows), BF16)],
        compiler_params=params(),
        cost_estimate=pl.CostEstimate(flops=0, bytes_accessed=8 * 2**20, transcendentals=0),
        name="place_tiles",
    )(place, inverse_map, *kid_rows)
    rest, *placed = lax.optimization_barrier((rest, *placed))
    kid_parts = [swapped(placed[d], "col", d) for d in range(cols)]

    lower2, inv2_hi, inv2_lo, inv2_t_hi, inv2_t_lo = pl.pallas_call(
        second_kernel,
        out_shape=[jax.ShapeDtypeStruct((PW, PW), F32), square, square, square, square],
        in_specs=[whole_spec()],
        out_specs=[whole_spec()] * 5,
        scratch_shapes=[pltpu.VMEM((PW, 2 * PW), F32)],
        compiler_params=params(),
        cost_estimate=pl.CostEstimate(flops=2 * 10**10, bytes_accessed=5 * 10**7, transcendentals=0),
        name="second_pivots",
    )(rest)

    lower2, *kid_parts = lax.optimization_barrier((lower2, *kid_parts))
    near_kids = jnp.concatenate([part[slice_cols:] for part in kid_parts], axis=0)
    far_kids = swapped(near_kids, "row", 1)

    block_rows = min(512, local_rows // 2)
    per_half = local_rows // 2 // block_rows
    width = 2 * kid_cols + NPIV
    piece = (cols // 2, block_rows, fan * held)
    lead, factor_panels = pl.pallas_call(
        functools.partial(row_kernel, (cols, share, slice_cols, block_rows, kid_cols, tiles), masks),
        grid=(2 * per_half,),
        out_shape=[
            jax.ShapeDtypeStruct((local_rows, width), BF16),
            jax.ShapeDtypeStruct((local_rows, NP * PW // cols), BF16),
        ],
        in_specs=[smem_spec()] * 3
        + [whole_spec()] * 8
        + [pl.BlockSpec((2 * slice_cols, block_rows), lambda i: (0, i))] * cols
        + [pl.BlockSpec(piece, lambda i: (0, jnp.minimum(i, per_half - 1), 0))] * 2
        + [pl.BlockSpec(piece, lambda i: (0, jnp.maximum(i - per_half, 0), 0))] * 2,
        out_specs=[
            pl.BlockSpec((block_rows, width), lambda i: (i, 0)),
            pl.BlockSpec((block_rows, NP * PW // cols), lambda i: (i, 0)),
        ],
        scratch_shapes=[
            pltpu.VMEM((block_rows, NPIV), F32),
            pltpu.VMEM((cols, block_rows, fan * held), F32),
        ],
        compiler_params=params(),
        cost_estimate=pl.CostEstimate(flops=8 * 10**9, bytes_accessed=2 * 10**7, transcendentals=0),
        name="row_factors",
    )(
        place, group_of, kid_of, piv_t, lower1, lower2,
        inv1_t_hi, inv1_t_lo, inv2_t_hi, inv2_t_lo, link_t, *kid_parts,
        halves[0], others[0], halves[1], others[1],
    )

    block_cols = min(1024, local_rows)
    per_block = local_rows // block_cols
    rhs = pl.pallas_call(
        functools.partial(col_kernel, (rows, fan, share, block_cols, local_rows, kid_cols, tiles)),
        grid=(local_cols // block_cols,),
        out_shape=jax.ShapeDtypeStruct((width, local_cols), BF16),
        in_specs=[smem_spec()] * 3
        + [
            pl.BlockSpec((rows, held, block_cols), lambda j: (0, 0, j)),
            pl.BlockSpec((kid_cols, block_cols), lambda j: (0, j % per_block)),
            pl.BlockSpec((kid_cols, block_cols), lambda j: (0, j % per_block)),
        ]
        + [whole_spec()] * 6,
        out_specs=pl.BlockSpec((width, block_cols), lambda j: (0, j)),
        scratch_shapes=[
            pltpu.VMEM((NPIV, block_cols), F32),
            pltpu.VMEM((kid_cols, block_cols), BF16),
        ],
        compiler_params=params(),
        cost_estimate=pl.CostEstimate(flops=8 * 10**9, bytes_accessed=2 * 10**7, transcendentals=0),
        name="col_factors",
    )(
        place, group_of, kid_of, col_strips, near_kids, far_kids,
        piv, inv1_hi, inv1_lo, inv2_hi, inv2_lo, link,
    )

    row_tiles, col_tiles = local_rows // MT, local_cols // MT
    row_group = lax.dynamic_slice_in_dim(tile_group, my_row * row_tiles, row_tiles)
    col_group = lax.dynamic_slice_in_dim(tile_group, my_col * col_tiles, col_tiles)
    kept = jnp.arange(local_cols, dtype=jnp.int32) % local_rows >= held
    same = (row_group[:, None] == jnp.repeat(col_group, MT)[None, :]).astype(F32)
    product = dot(lead, rhs)
    shape = (row_tiles, MT, local_cols)
    summed = front_entries.reshape(shape) * same[:, None, :] + product.reshape(shape)
    summed = summed.reshape(local_rows, local_cols)
    keep = (lax.broadcasted_iota(jnp.int32, summed.shape, 0) >= held) & kept[None, :]
    schur_block = jnp.where(keep, summed, 0.0)
    return (factor_panels, schur_block)


def solution(mesh):
    placed = (P("row", "col"), P(), P("row", "col"), P())
    return jax.shard_map(
        local,
        mesh=mesh,
        in_specs=placed,
        out_specs=(P("row", "col"), P("row", "col")),
        check_vma=False,
    )
```

```python
import functools

import jax
import jax.numpy as jnp
from jax import lax
from jax.experimental import pallas as pl
from jax.experimental.pallas import tpu as pltpu
from jax.sharding import PartitionSpec as P

PW = 256
NP = 2
TS = 128
MT = 512
NPIV = NP * PW
BLK = 32
F32 = jnp.float32
BF16 = jnp.bfloat16
VMEM_BYTES = 60 * 1024 * 1024

NN = (((1,), (0,)), ((), ()))
NT = (((1,), (1,)), ((), ()))


def dot(left, right, dims=NN, precision=None):
    return lax.dot_general(left, right, dims, precision=precision, preferred_element_type=F32)


def exact(left, right, dims=NN):
    return dot(left, right, dims, lax.Precision.HIGHEST)


def split(value):
    high = value.astype(BF16)
    return high, (value - high.astype(F32)).astype(BF16)


def swapped(value, axis, mask):
    if mask == 0:
        return value
    return lax.ppermute(value, axis, [(i, i ^ mask) for i in range(lax.axis_size(axis))])


def whole_spec():
    return pl.BlockSpec(memory_space=pltpu.VMEM)


def smem_spec():
    return pl.BlockSpec(memory_space=pltpu.SMEM)


def factor_diagonal(block):
    groups = BLK // 8
    lane = lax.broadcasted_iota(jnp.int32, (BLK, 128), 1)
    row = lax.broadcasted_iota(jnp.int32, (BLK, 128), 0)
    row8 = lax.broadcasted_iota(jnp.int32, (8, 128), 0)
    start = jnp.where(lane < BLK, block, jnp.where(lane == row + BLK, 1.0, 0.0))
    work = [start[8 * g : 8 * g + 8] for g in range(groups)]
    cols = []
    for k in range(BLK):
        base = 8 * (k // 8)
        cols.append(jnp.broadcast_to(block[base:, k : k + 1], (BLK - base, 128)))
    scale = [jnp.ones((8, 128), F32) for _ in range(groups)]
    for j in range(BLK):
        g0 = j // 8
        base = 8 * g0
        column = cols[j]
        pivot = column[j - base : j - base + 1]
        root = lax.rsqrt(pivot)
        root = root * (1.5 - 0.5 * pivot * root * root)
        factor = jnp.where(row[base:] > j, column * (root * root), 0.0)
        lead = work[g0][j - base : j - base + 1]
        for g in range(g0, groups):
            work[g] = work[g] - factor[8 * (g - g0) : 8 * (g - g0) + 8] * lead
        for k in range(j + 1, BLK):
            skip = 8 * (k // 8 - g0)
            cols[k] = cols[k] - factor[skip:] * column[k - base : k - base + 1]
        scale[g0] = jnp.where(row8 == j - base, root, scale[g0])
    return jnp.concatenate([work[g] * scale[g] for g in range(groups)], axis=0)


def factor_panel(work):
    per_tile = 128 // BLK
    row = lax.broadcasted_iota(jnp.int32, (PW, BLK), 0)
    lane = lax.broadcasted_iota(jnp.int32, (BLK, 128), 1)

    def step(b, carry):
        low = pl.multiple_of(b * BLK, BLK)
        tile = pl.multiple_of((b // per_tile) * 128, 128)
        turn = (128 - (b % per_tile) * BLK) % 128
        columns = pltpu.roll(work[:, pl.ds(tile, 128)], turn, 1)
        block = pltpu.roll(work[pl.ds(low, BLK), pl.ds(tile, 128)], turn, 1)
        done = factor_diagonal(block)
        inverse = jnp.where(lane < BLK, pltpu.roll(done, 128 - BLK, 1), 0.0)
        upper = exact(inverse[:, :BLK], work[pl.ds(low, BLK), :])
        lead = exact(columns, inverse, NT)
        lead = jnp.where(row >= low + BLK, lead, 0.0)
        work[...] = work[...] - exact(lead, upper)
        work[pl.ds(low, BLK), :] = upper
        return carry

    lax.fori_loop(0, PW // BLK, step, 0)


def pivot_values(table, stride, share, along_rows):
    shape = (NPIV, 1) if along_rows else (1, NPIV)
    block = lax.broadcasted_iota(jnp.int32, shape, 0 if along_rows else 1) % PW // share
    values = jnp.zeros(shape, F32)
    for r in range(PW // share):
        values = jnp.where(block == r, table[r * stride], values)
    return values


def tile_values(table, start, count):
    return jnp.concatenate([jnp.full((1, TS), table[start + i], F32) for i in range(count)], axis=1)


def finish_panel(work, lower, inv_hi, inv_lo, inv_t_hi, inv_t_lo):
    row = lax.broadcasted_iota(jnp.int32, (PW, PW), 0)
    col = lax.broadcasted_iota(jnp.int32, (PW, PW), 1)
    lower[:PW, :] = jnp.where(col <= row, work[:, :PW].T, 0.0)
    inverse = work[:, PW:]
    inv_hi[...], inv_lo[...] = split(inverse)
    inv_t_hi[...], inv_t_lo[...] = split(inverse.T)
    return inverse


def unit():
    row = lax.broadcasted_iota(jnp.int32, (PW, PW), 0)
    col = lax.broadcasted_iota(jnp.int32, (PW, PW), 1)
    return jnp.where(row == col, 1.0, 0.0)


def first_kernel(sizes, place, group_of, kid_of, near, far,
                 lower, inv_hi, inv_lo, inv_t_hi, inv_t_lo, link_out, link_t, rest, piv_t, piv,
                 pile, wide, work):
    cols, fan, share, held, tiles = sizes
    my_row, my_col = place[0], place[1]
    my_q, my_a = my_row % fan, my_row // fan
    col_share = PW // cols
    for dq, source in enumerate((near, far)):
        for d in range(cols):
            r = (my_a ^ d) * fan + (my_q ^ dq)
            pieces = [source[c ^ my_col, d, :held, :] for c in range(cols)]
            line = jnp.concatenate(
                [piece[:, k * col_share : (k + 1) * col_share] for k in range(NP) for piece in pieces],
                axis=1,
            )
            kids = []
            for e in range(cols):
                packed = source[e, d, held:, :]
                kids += [packed[:, :held], packed[:, held:]]
            kids = jnp.concatenate(kids, axis=0).T
            for k in range(NP):
                at = pl.ds(pl.multiple_of(k * PW + r * share, share), share)
                pile[at, :] = line[k * share : (k + 1) * share]
                wide[at, :] = kids[k * share : (k + 1) * share]
    piv[...] = wide[...].astype(BF16)
    piv_t[...] = wide[...].T.astype(BF16)
    product = dot(piv[...], piv_t[...])
    same_group = pivot_values(group_of, tiles, share, True) == pivot_values(group_of, tiles, share, False)
    same_kid = pivot_values(kid_of, tiles, share, True) == pivot_values(kid_of, tiles, share, False)
    pile[...] = jnp.where(same_group, pile[...], 0.0) + jnp.where(same_kid, product, 0.0)
    work[:, :PW] = pile[:PW, :PW]
    work[:, PW:] = unit()
    factor_panel(work)
    inverse = finish_panel(work, lower, inv_hi, inv_lo, inv_t_hi, inv_t_lo)
    link = exact(pile[PW:, :PW], inverse, NT).astype(BF16)
    link_out[...] = link
    lower[PW:, :] = link.astype(F32)
    link_t[...] = link.astype(F32).T.astype(BF16)
    rest[...] = pile[PW:, PW:] - dot(link, link, NT)


def second_kernel(rest, lower, inv_hi, inv_lo, inv_t_hi, inv_t_lo, work):
    work[:, :PW] = rest[...]
    work[:, PW:] = unit()
    factor_panel(work)
    finish_panel(work, lower, inv_hi, inv_lo, inv_t_hi, inv_t_lo)


def place_kernel(sizes, place, inverse_map, held, *outs):
    cols, fan, tiles, slice_cols = sizes
    my_row, my_col = place[0], place[1]
    my_q = my_row % fan

    def fetch(block, i):
        tile = inverse_map[block * tiles + i]
        at = pl.multiple_of((tile % tiles) * TS, TS)
        return held[tile // tiles, :, pl.ds(at, TS)]

    for i in range(tiles):
        mine = fetch(my_row, i)
        for d in range(cols):
            outs[d][:slice_cols, i * TS : (i + 1) * TS] = mine
    for d in range(cols):
        for i in range(tiles):
            outs[d][slice_cols:, i * TS : (i + 1) * TS] = fetch((my_col ^ d) * fan + my_q, i)


def solve_rows(first, second, inv1_hi, inv1_lo, inv2_hi, inv2_lo, link):
    high, low = split(first)
    head = dot(high, inv1_hi) + dot(high, inv1_lo) + dot(low, inv1_hi)
    high, low = split(second - dot(head.astype(BF16), link))
    tail = dot(high, inv2_hi) + dot(high, inv2_lo) + dot(low, inv2_hi)
    return head, tail


def solve_cols(first, second, inv1_hi, inv1_lo, inv2_hi, inv2_lo, link):
    def apply(inv_hi, inv_lo, value):
        high, low = split(value)
        both = dot(jnp.concatenate([inv_hi, inv_lo], axis=0), high)
        return both[:PW] + both[PW:] + dot(inv_hi, low)

    head = apply(inv1_hi, inv1_lo, first)
    return head, apply(inv2_hi, inv2_lo, second - dot(link, head.astype(BF16)))


def schur_kernel(sizes, masks, place, group_of, kid_of, front, strips, near_kids, far_kids,
                 piv, piv_t, lower1, lower2, inv1_hi, inv1_lo, inv2_hi, inv2_lo, link,
                 inv1_t_hi, inv1_t_lo, inv2_t_hi, inv2_t_lo, link_t, *refs):
    rows, cols, fan, share, held, slice_cols, block_rows, local_rows, local_cols, tiles = sizes
    sources = refs[:cols]
    halves = [refs[cols : cols + 2], refs[cols + 2 : cols + 4]]
    out, panel, flipped, kids, strip, solved, pieces = refs[cols + 4 :]
    my_row, my_col = place[0], place[1]
    my_q = my_row % fan
    step = pl.program_id(0)
    first_tile = my_col * fan * tiles
    wide = strip.shape[1]

    @pl.when(step == 0)
    def _():
        for q in range(fan):

            @pl.when(my_q == q)
            def _():
                kids[:, q * local_rows : (q + 1) * local_rows] = near_kids[...]

            @pl.when(my_q != q)
            def _():
                kids[:, q * local_rows : (q + 1) * local_rows] = far_kids[...]

        group_col = pivot_values(group_of, tiles, share, True)
        kid_col = pivot_values(kid_of, tiles, share, True)

        def solve(n, carry):
            at = pl.ds(pl.multiple_of(n * wide, wide), wide)
            for r in range(rows):
                piece = strips[r, :, at].astype(F32)
                for k in range(NP):
                    low = k * PW + r * share
                    strip[low : low + share, :] = piece[k * share : (k + 1) * share]
            tile = first_tile + n * (wide // TS)
            group_all = tile_values(group_of, tile, wide // TS)
            kid_all = tile_values(kid_of, tile, wide // TS)
            product = dot(piv[...], kids[:, at])
            full = jnp.where(group_col == group_all, strip[...], 0.0) + jnp.where(
                kid_col == kid_all, product, 0.0
            )
            head, tail = solve_cols(
                full[:PW], full[PW:], inv1_hi[...], inv1_lo[...], inv2_hi[...], inv2_lo[...], link[...]
            )
            flipped[:PW, at] = (-head).astype(BF16)
            flipped[PW:, at] = (-tail).astype(BF16)
            return carry

        lax.fori_loop(0, local_cols // wide, solve, 0)

    for half in range(2):

        @pl.when(step // (pl.num_programs(0) // 2) == half)
        def _():
            for i, mask in enumerate(masks[half]):
                source = halves[half][i // (cols // 2)]
                pieces[my_col ^ mask] = source[i % (cols // 2)]

    col_share = PW // cols
    subs = block_rows // TS
    own_t = jnp.concatenate([source[:slice_cols, :] for source in sources], axis=0)
    own = own_t.astype(F32).T.astype(BF16)
    product = dot(own, piv_t[...])
    entries = jnp.concatenate(
        [pieces[c, :, k * col_share : (k + 1) * col_share] for k in range(NP) for c in range(cols)],
        axis=1,
    )
    group_row = pivot_values(group_of, tiles, share, False)
    kid_row = pivot_values(kid_of, tiles, share, False)
    my_tile = my_row * tiles + step * subs
    parts = []
    for i in range(subs):
        part = slice(i * TS, (i + 1) * TS)
        parts.append(
            jnp.where(group_row == group_of[my_tile + i], entries[part], 0.0)
            + jnp.where(kid_row == kid_of[my_tile + i], product[part], 0.0)
        )
    full = jnp.concatenate(parts, axis=0)
    head, tail = solve_rows(
        full[:, :PW], full[:, PW:], inv1_t_hi[...], inv1_t_lo[...], inv2_t_hi[...], inv2_t_lo[...], link_t[...]
    )
    solved[:, :PW] = head
    solved[:, PW:] = tail

    @pl.when(step == 0)
    def _():
        at = pl.multiple_of(my_row * share, share)
        solved[:share, :PW] = lower1[pl.ds(at, share), :]
        solved[:share, PW:] = jnp.zeros((share, PW), F32)
        solved[share : 2 * share, :PW] = lower1[pl.ds(PW + at, share), :]
        solved[share : 2 * share, PW:] = lower2[pl.ds(at, share), :]

    per_tile = 128 // col_share
    lane = lax.broadcasted_iota(jnp.int32, (block_rows, 128), 1)
    moved_out = jnp.zeros((block_rows, 128), F32)
    for k in range(NP):
        tile = pl.multiple_of(k * PW + (my_col // per_tile) * 128, 128)
        turn = (128 + k * col_share - (my_col % per_tile) * col_share) % 128
        moved = pltpu.roll(solved[:, pl.ds(tile, 128)], turn, 1)
        moved_out = jnp.where(lane // col_share == k, moved, moved_out)
    panel[...] = moved_out[:, : NP * col_share].astype(BF16)

    lead = solved[...].astype(BF16)
    span = min(512, local_cols)
    for n in range(local_cols // span):
        at = slice(n * span, (n + 1) * span)
        update = dot(lead, flipped[:, at])
        product = dot(own, kids[:, at])
        group_all = tile_values(group_of, first_tile + n * (span // TS), span // TS)
        kid_all = tile_values(kid_of, first_tile + n * (span // TS), span // TS)
        for i in range(subs):
            part = slice(i * TS, (i + 1) * TS)
            out[part, at] = (
                jnp.where(group_all == group_of[my_tile + i], front[part, at], 0.0)
                + jnp.where(kid_all == kid_of[my_tile + i], product[part], 0.0)
                + update[part]
            )
    for q in range(fan):
        out[:, q * local_rows : q * local_rows + held] = jnp.zeros((block_rows, held), F32)

    @pl.when(step == 0)
    def _():
        out[:held, :] = jnp.zeros((held, local_cols), F32)


def params():
    return pltpu.CompilerParams(vmem_limit_bytes=VMEM_BYTES)


def local(front_entries, tile_group, child_factor, row_map):
    rows, cols = lax.axis_size("row"), lax.axis_size("col")
    fan = rows // cols
    assert fan == 2
    local_rows, local_cols = front_entries.shape
    slice_cols = child_factor.shape[1]
    kid_cols = slice_cols * cols
    tiles = local_rows // TS
    share = PW // rows
    held = NP * share
    my_row, my_col = lax.axis_index("row"), lax.axis_index("col")
    place = jnp.stack([my_row, my_col]).astype(jnp.int32)

    flipped = child_factor.T
    own_map = lax.dynamic_slice_in_dim(row_map, my_row * tiles, tiles)
    starts = flipped.reshape(slice_cols, tiles, TS)[:, :, :held]

    def chosen(block):
        keep = (own_map == block * tiles)[None, :, None]
        return jnp.sum(jnp.where(keep, starts, 0), axis=1, dtype=F32)

    corner = jnp.concatenate(
        [
            front_entries[:held, q * local_rows + k * share : q * local_rows + (k + 1) * share]
            for k in range(NP)
            for q in range(fan)
        ],
        axis=1,
    )
    kids = jnp.concatenate([chosen(my_row), chosen(jnp.bitwise_xor(my_row, rows // 2))], axis=1)
    packet = jnp.concatenate([corner, kids], axis=0)
    packets = [swapped(packet, "row", d * fan) for d in range(cols)]

    row_strip = jnp.concatenate(
        [
            front_entries[:, q * local_rows + k * share : q * local_rows + (k + 1) * share]
            for k in range(NP)
            for q in range(fan)
        ],
        axis=1,
    )
    steps = [1 << i for i in range(cols.bit_length() - 1)]
    orders = [steps, steps[::-1]]
    halves = [row_strip[None, : local_rows // 2], row_strip[None, local_rows // 2 :]]
    masks = [[0], [0]]
    for h in range(2):
        for step in orders[h][:-1]:
            halves[h] = jnp.concatenate([halves[h], swapped(halves[h], "col", step)], axis=0)
            masks[h] = masks[h] + [m ^ step for m in masks[h]]
    gathered = lax.all_gather(flipped, "row", axis=0)
    col_strip, *packets = lax.optimization_barrier((front_entries[:held].astype(BF16), *packets))
    col_strips = lax.all_gather(col_strip, "row", axis=0)
    merged = []
    for d in range(cols):
        kid = packets[d][held:, :held] + packets[d ^ (cols // 2)][held:, held:]
        half = slice_cols // 2
        merged.append(
            jnp.concatenate(
                [packets[d][:held], jnp.concatenate([kid[:half], kid[half:]], axis=1)], axis=0
            )
        )
    merged = jnp.stack(merged)
    near = jnp.stack([swapped(merged, "col", d) for d in range(cols)])
    far = swapped(near, "row", 1)

    tile_ids = jnp.arange(row_map.shape[0], dtype=jnp.int32)
    inverse_map = jnp.sum(
        jnp.where(row_map[None, :] == tile_ids[:, None], tile_ids[None, :], 0), axis=1, dtype=jnp.int32
    )
    kid_of = (inverse_map >= row_map.shape[0] // 2).astype(F32)
    group_of = jnp.repeat(tile_group, MT // TS).astype(F32)

    placed = pl.pallas_call(
        functools.partial(place_kernel, (cols, fan, tiles, slice_cols)),
        out_shape=[jax.ShapeDtypeStruct((2 * slice_cols, local_rows), BF16)] * cols,
        in_specs=[smem_spec()] * 2 + [whole_spec()],
        out_specs=[whole_spec()] * cols,
        compiler_params=params(),
        cost_estimate=pl.CostEstimate(flops=0, bytes_accessed=8 * 2**20, transcendentals=0),
        name="place_tiles",
    )(place, inverse_map, gathered)
    near, far, *placed = lax.optimization_barrier((near, far, *placed))
    kid_parts = [swapped(placed[d], "col", d) for d in range(cols)]
    square = jax.ShapeDtypeStruct((PW, PW), BF16)
    lower1, inv1_hi, inv1_lo, inv1_t_hi, inv1_t_lo, link, link_t, rest, piv_t, piv = pl.pallas_call(
        functools.partial(first_kernel, (cols, fan, share, held, tiles)),
        out_shape=[
            jax.ShapeDtypeStruct((2 * PW, PW), F32),
            square, square, square, square, square, square,
            jax.ShapeDtypeStruct((PW, PW), F32),
            jax.ShapeDtypeStruct((kid_cols, NPIV), BF16),
            jax.ShapeDtypeStruct((NPIV, kid_cols), BF16),
        ],
        in_specs=[smem_spec()] * 3 + [whole_spec()] * 2,
        out_specs=[whole_spec()] * 10,
        scratch_shapes=[
            pltpu.VMEM((NPIV, NPIV), F32),
            pltpu.VMEM((NPIV, kid_cols), F32),
            pltpu.VMEM((PW, 2 * PW), F32),
        ],
        compiler_params=params(),
        cost_estimate=pl.CostEstimate(flops=2 * 10**10, bytes_accessed=5 * 10**7, transcendentals=0),
        name="first_pivots",
    )(place, group_of, kid_of, near, far)

    rest, *arrived = lax.optimization_barrier((rest, *kid_parts, *halves))
    kid_parts, halves = arrived[:cols], arrived[cols:]
    near_kids = jnp.concatenate([part[slice_cols:] for part in kid_parts], axis=0)
    rest, near_kids = lax.optimization_barrier((rest, near_kids))
    far_kids = swapped(near_kids, "row", 1)
    others = [swapped(halves[h], "col", orders[h][-1]) for h in range(2)]
    masks = [masks[h] + [m ^ orders[h][-1] for m in masks[h]] for h in range(2)]
    lower2, inv2_hi, inv2_lo, inv2_t_hi, inv2_t_lo = pl.pallas_call(
        second_kernel,
        out_shape=[jax.ShapeDtypeStruct((PW, PW), F32), square, square, square, square],
        in_specs=[whole_spec()],
        out_specs=[whole_spec()] * 5,
        scratch_shapes=[pltpu.VMEM((PW, 2 * PW), F32)],
        compiler_params=params(),
        cost_estimate=pl.CostEstimate(flops=2 * 10**10, bytes_accessed=5 * 10**7, transcendentals=0),
        name="second_pivots",
    )(rest)

    block_rows = min(256, local_rows // 2)
    per_half = local_rows // 2 // block_rows
    wide = min(1024, local_cols)
    piece = (cols // 2, block_rows, fan * held)
    schur_block, factor_panels = pl.pallas_call(
        functools.partial(
            schur_kernel,
            (rows, cols, fan, share, held, slice_cols, block_rows, local_rows, local_cols, tiles),
            masks,
        ),
        grid=(2 * per_half,),
        out_shape=[
            jax.ShapeDtypeStruct((local_rows, local_cols), F32),
            jax.ShapeDtypeStruct((local_rows, NP * PW // cols), BF16),
        ],
        in_specs=[smem_spec()] * 3
        + [pl.BlockSpec((block_rows, local_cols), lambda i: (i, 0))]
        + [whole_spec()] * 17
        + [pl.BlockSpec((2 * slice_cols, block_rows), lambda i: (0, i))] * cols
        + [pl.BlockSpec(piece, lambda i: (0, jnp.minimum(i, per_half - 1), 0))] * 2
        + [pl.BlockSpec(piece, lambda i: (0, jnp.maximum(i - per_half, 0), 0))] * 2,
        out_specs=[
            pl.BlockSpec((block_rows, local_cols), lambda i: (i, 0)),
            pl.BlockSpec((block_rows, NP * PW // cols), lambda i: (i, 0)),
        ],
        scratch_shapes=[
            pltpu.VMEM((NPIV, local_cols), BF16),
            pltpu.VMEM((kid_cols, local_cols), BF16),
            pltpu.VMEM((NPIV, wide), F32),
            pltpu.VMEM((block_rows, NPIV), F32),
            pltpu.VMEM((cols, block_rows, fan * held), F32),
        ],
        compiler_params=params(),
        cost_estimate=pl.CostEstimate(flops=3 * 10**10, bytes_accessed=9 * 10**7, transcendentals=0),
        name="schur_update",
    )(
        place, group_of, kid_of, front_entries, col_strips, near_kids, far_kids,
        piv, piv_t, lower1, lower2, inv1_hi, inv1_lo, inv2_hi, inv2_lo, link,
        inv1_t_hi, inv1_t_lo, inv2_t_hi, inv2_t_lo, link_t, *kid_parts,
        halves[0], others[0], halves[1], others[1],
    )
    return (factor_panels, schur_block)


def solution(mesh):
    placed = (P("row", "col"), P(), P("row", "col"), P())
    return jax.shard_map(
        local,
        mesh=mesh,
        in_specs=placed,
        out_specs=(P("row", "col"), P("row", "col")),
        check_vma=False,
    )
```

```python
import functools

import jax
import jax.numpy as jnp
from jax import lax
from jax.experimental import pallas as pl
from jax.experimental.pallas import tpu as pltpu
from jax.sharding import PartitionSpec as P

PW = 256
NP = 2
TS = 128
MT = 512
NPIV = NP * PW
BLK = 32
F32 = jnp.float32
BF16 = jnp.bfloat16
VMEM_BYTES = 60 * 1024 * 1024

NN = (((1,), (0,)), ((), ()))
NT = (((1,), (1,)), ((), ()))


def dot(left, right, dims=NN, precision=None):
    return lax.dot_general(left, right, dims, precision=precision, preferred_element_type=F32)


def exact(left, right, dims=NN):
    return dot(left, right, dims, lax.Precision.HIGHEST)


def split(value):
    high = value.astype(BF16)
    return high, (value - high.astype(F32)).astype(BF16)


def swapped(value, axis, mask):
    if mask == 0:
        return value
    return lax.ppermute(value, axis, [(i, i ^ mask) for i in range(lax.axis_size(axis))])


def whole_spec():
    return pl.BlockSpec(memory_space=pltpu.VMEM)


def any_spec():
    return pl.BlockSpec(memory_space=pl.ANY)


def smem_spec():
    return pl.BlockSpec(memory_space=pltpu.SMEM)


def factor_diagonal(block):
    groups = BLK // 8
    lane = lax.broadcasted_iota(jnp.int32, (BLK, 128), 1)
    row = lax.broadcasted_iota(jnp.int32, (BLK, 128), 0)
    row8 = lax.broadcasted_iota(jnp.int32, (8, 128), 0)
    start = jnp.where(lane < BLK, block, jnp.where(lane == row + BLK, 1.0, 0.0))
    work = [start[8 * g : 8 * g + 8] for g in range(groups)]
    cols = []
    for k in range(BLK):
        base = 8 * (k // 8)
        cols.append(jnp.broadcast_to(block[base:, k : k + 1], (BLK - base, 128)))
    scale = [jnp.ones((8, 128), F32) for _ in range(groups)]
    for j in range(BLK):
        g0 = j // 8
        base = 8 * g0
        column = cols[j]
        pivot = column[j - base : j - base + 1]
        root = lax.rsqrt(pivot)
        root = root * (1.5 - 0.5 * pivot * root * root)
        factor = jnp.where(row[base:] > j, column * (root * root), 0.0)
        lead = work[g0][j - base : j - base + 1]
        for g in range(g0, groups):
            work[g] = work[g] - factor[8 * (g - g0) : 8 * (g - g0) + 8] * lead
        for k in range(j + 1, BLK):
            skip = 8 * (k // 8 - g0)
            cols[k] = cols[k] - factor[skip:] * column[k - base : k - base + 1]
        scale[g0] = jnp.where(row8 == j - base, root, scale[g0])
    return jnp.concatenate([work[g] * scale[g] for g in range(groups)], axis=0)


def factor_panel(work):
    per_tile = 128 // BLK
    row = lax.broadcasted_iota(jnp.int32, (PW, BLK), 0)
    lane = lax.broadcasted_iota(jnp.int32, (BLK, 128), 1)

    def step(b, carry):
        low = pl.multiple_of(b * BLK, BLK)
        tile = pl.multiple_of((b // per_tile) * 128, 128)
        turn = (128 - (b % per_tile) * BLK) % 128
        columns = pltpu.roll(work[:, pl.ds(tile, 128)], turn, 1)
        block = pltpu.roll(work[pl.ds(low, BLK), pl.ds(tile, 128)], turn, 1)
        done = factor_diagonal(block)
        inverse = jnp.where(lane < BLK, pltpu.roll(done, 128 - BLK, 1), 0.0)
        upper = exact(inverse[:, :BLK], work[pl.ds(low, BLK), :])
        lead = exact(columns, inverse, NT)
        lead = jnp.where(row >= low + BLK, lead, 0.0)
        work[...] = work[...] - exact(lead, upper)
        work[pl.ds(low, BLK), :] = upper
        return carry

    lax.fori_loop(0, PW // BLK, step, 0)


def pivot_values(table, stride, share, along_rows):
    shape = (NPIV, 1) if along_rows else (1, NPIV)
    block = lax.broadcasted_iota(jnp.int32, shape, 0 if along_rows else 1) % PW // share
    values = jnp.zeros(shape, F32)
    for r in range(PW // share):
        values = jnp.where(block == r, table[r * stride], values)
    return values


def tile_values(table, start, count):
    return jnp.concatenate([jnp.full((1, TS), table[start + i], F32) for i in range(count)], axis=1)


def finish_panel(work, lower, inv_hi, inv_lo, inv_t_hi, inv_t_lo):
    row = lax.broadcasted_iota(jnp.int32, (PW, PW), 0)
    col = lax.broadcasted_iota(jnp.int32, (PW, PW), 1)
    lower[:PW, :] = jnp.where(col <= row, work[:, :PW].T, 0.0)
    inverse = work[:, PW:]
    inv_hi[...], inv_lo[...] = split(inverse)
    inv_t_hi[...], inv_t_lo[...] = split(inverse.T)
    return inverse


def unit():
    row = lax.broadcasted_iota(jnp.int32, (PW, PW), 0)
    col = lax.broadcasted_iota(jnp.int32, (PW, PW), 1)
    return jnp.where(row == col, 1.0, 0.0)


def first_kernel(sizes, place, group_of, kid_of, near, far,
                 lower, inv_hi, inv_lo, inv_t_hi, inv_t_lo, link_out, link_t, rest, piv_t, piv,
                 pile, wide, work):
    cols, fan, share, held, tiles = sizes
    my_row, my_col = place[0], place[1]
    my_q, my_a = my_row % fan, my_row // fan
    col_share = PW // cols
    for dq, source in enumerate((near, far)):
        for d in range(cols):
            r = (my_a ^ d) * fan + (my_q ^ dq)
            pieces = [source[c ^ my_col, d, :held, :] for c in range(cols)]
            line = jnp.concatenate(
                [piece[:, k * col_share : (k + 1) * col_share] for k in range(NP) for piece in pieces],
                axis=1,
            )
            kids = []
            for e in range(cols):
                packed = source[e, d, held:, :]
                kids += [packed[:, :held], packed[:, held:]]
            kids = jnp.concatenate(kids, axis=0).T
            for k in range(NP):
                at = pl.ds(pl.multiple_of(k * PW + r * share, share), share)
                pile[at, :] = line[k * share : (k + 1) * share]
                wide[at, :] = kids[k * share : (k + 1) * share]
    piv[...] = wide[...].astype(BF16)
    piv_t[...] = wide[...].T.astype(BF16)
    product = dot(piv[...], piv_t[...])
    same_group = pivot_values(group_of, tiles, share, True) == pivot_values(group_of, tiles, share, False)
    same_kid = pivot_values(kid_of, tiles, share, True) == pivot_values(kid_of, tiles, share, False)
    pile[...] = jnp.where(same_group, pile[...], 0.0) + jnp.where(same_kid, product, 0.0)
    work[:, :PW] = pile[:PW, :PW]
    work[:, PW:] = unit()
    factor_panel(work)
    inverse = finish_panel(work, lower, inv_hi, inv_lo, inv_t_hi, inv_t_lo)
    link = exact(pile[PW:, :PW], inverse, NT).astype(BF16)
    link_out[...] = link
    lower[PW:, :] = link.astype(F32)
    link_t[...] = link.astype(F32).T.astype(BF16)
    rest[...] = pile[PW:, PW:] - dot(link, link, NT)


def second_kernel(rest, lower, inv_hi, inv_lo, inv_t_hi, inv_t_lo, work):
    work[:, :PW] = rest[...]
    work[:, PW:] = unit()
    factor_panel(work)
    finish_panel(work, lower, inv_hi, inv_lo, inv_t_hi, inv_t_lo)


def place_kernel(sizes, place, inverse_map, held, *outs):
    cols, fan, tiles, slice_cols = sizes
    my_row, my_col = place[0], place[1]
    my_q = my_row % fan

    def fetch(block, i):
        tile = inverse_map[block * tiles + i]
        at = pl.multiple_of((tile % tiles) * TS, TS)
        return held[tile // tiles, :, pl.ds(at, TS)]

    for i in range(tiles):
        mine = fetch(my_row, i)
        for d in range(cols):
            outs[d][:slice_cols, i * TS : (i + 1) * TS] = mine
    for d in range(cols):
        for i in range(tiles):
            outs[d][slice_cols:, i * TS : (i + 1) * TS] = fetch((my_col ^ d) * fan + my_q, i)


def solve_rows(first, second, inv1_hi, inv1_lo, inv2_hi, inv2_lo, link):
    high, low = split(first)
    head = dot(high, inv1_hi) + dot(high, inv1_lo) + dot(low, inv1_hi)
    high, low = split(second - dot(head.astype(BF16), link))
    tail = dot(high, inv2_hi) + dot(high, inv2_lo) + dot(low, inv2_hi)
    return head, tail


def solve_cols(first, second, inv1_hi, inv1_lo, inv2_hi, inv2_lo, link):
    def apply(inv_hi, inv_lo, value):
        both = dot(jnp.concatenate([inv_hi, inv_lo], axis=0), value.astype(BF16))
        return both[:PW] + both[PW:]

    head = apply(inv1_hi, inv1_lo, first)
    return head, apply(inv2_hi, inv2_lo, second - dot(link, head.astype(BF16)))


def schur_kernel(sizes, masks, place, group_of, kid_of,
                 piv, piv_t, lower1, lower2, inv1_hi, inv1_lo, inv2_hi, inv2_lo, link,
                 inv1_t_hi, inv1_t_lo, inv2_t_hi, inv2_t_lo, link_t, *refs):
    rows, cols, fan, share, held, slice_cols, block_rows, local_rows, local_cols, tiles, wide = sizes
    front, strips, near_kids, far_kids = refs[:4]
    sources = refs[4 : 4 + cols]
    halves = [refs[4 + cols : 6 + cols], refs[6 + cols : 8 + cols]]
    out, panel = refs[8 + cols : 10 + cols]
    (fronts, outs, strips_in, kids, own_t, pieces, flipped, strip, solved,
     front_sems, out_sems, strip_sems, kid_sems, own_sems, piece_sems) = refs[10 + cols :]
    my_row, my_col = place[0], place[1]
    my_q = my_row % fan
    first_tile = my_col * fan * tiles
    steps = local_rows // block_rows
    chunks = local_cols // wide
    ins, holds = fronts.shape[0], outs.shape[0]
    half_rows = local_rows // 2

    def rows_at(i):
        return pl.ds(pl.multiple_of(i * block_rows, block_rows), block_rows)

    def front_copy(i, slot):
        return pltpu.make_async_copy(front.at[rows_at(i), :], fronts.at[slot], front_sems.at[slot])

    def out_copy(i, slot):
        return pltpu.make_async_copy(outs.at[slot], out.at[rows_at(i), :], out_sems.at[slot])

    def chunk_at(n):
        return pl.ds(pl.multiple_of(n * wide, wide), wide)

    def strip_copy(n):
        return pltpu.make_async_copy(
            strips.at[:, :, chunk_at(n)], strips_in.at[:, :, chunk_at(n)], strip_sems.at[n]
        )

    kid_copies = [
        pltpu.make_async_copy(
            source,
            kids.at[:, pl.ds(pl.multiple_of((my_q ^ q) * local_rows, local_rows), local_rows)],
            kid_sems.at[q],
        )
        for q, source in enumerate((near_kids, far_kids))
    ]
    own_copies = [
        pltpu.make_async_copy(
            source.at[:slice_cols, :], own_t.at[d * slice_cols : (d + 1) * slice_cols, :], own_sems.at[d]
        )
        for d, source in enumerate(sources)
    ]
    piece_copies = [
        pltpu.make_async_copy(
            halves[half][i // (cols // 2)].at[i % (cols // 2)],
            pieces.at[my_col ^ mask, half * half_rows : (half + 1) * half_rows, :],
            piece_sems.at[half * cols + i],
        )
        for half in range(2)
        for i, mask in enumerate(masks[half])
    ]
    for copy in kid_copies:
        copy.start()
    for n in range(chunks):
        strip_copy(n).start()
    for copy in own_copies + piece_copies:
        copy.start()
    for copy in kid_copies:
        copy.wait()
    group_col = pivot_values(group_of, tiles, share, True)
    kid_col = pivot_values(kid_of, tiles, share, True)

    def solve(n, carry):
        strip_copy(n).wait()

        @pl.when(n == 0)
        def _():
            for i in range(ins):
                front_copy(i, i).start()

        at = chunk_at(n)
        for r in range(rows):
            piece = strips_in[r, :, at].astype(F32)
            for k in range(NP):
                low = k * PW + r * share
                strip[low : low + share, :] = piece[k * share : (k + 1) * share]
        tile = first_tile + n * (wide // TS)
        group_all = tile_values(group_of, tile, wide // TS)
        kid_all = tile_values(kid_of, tile, wide // TS)
        product = dot(piv[...], kids[:, at])
        full = jnp.where(group_col == group_all, strip[...], 0.0) + jnp.where(
            kid_col == kid_all, product, 0.0
        )
        head, tail = solve_cols(
            full[:PW], full[PW:], inv1_hi[...], inv1_lo[...], inv2_hi[...], inv2_lo[...], link[...]
        )
        flipped[:PW, at] = (-head).astype(BF16)
        flipped[PW:, at] = (-tail).astype(BF16)
        return carry

    lax.fori_loop(0, chunks, solve, 0)
    for copy in own_copies + piece_copies:
        copy.wait()
    col_share = PW // cols
    subs = block_rows // TS
    per_tile = 128 // col_share
    span = min(512, local_cols)
    group_row = pivot_values(group_of, tiles, share, False)
    kid_row = pivot_values(kid_of, tiles, share, False)
    lane = lax.broadcasted_iota(jnp.int32, (block_rows, 128), 1)

    def work_rows(step, carry):
        own = own_t[:, rows_at(step)].astype(F32).T.astype(BF16)
        product = dot(own, piv_t[...])
        entries = jnp.concatenate(
            [
                pieces[c, rows_at(step), k * col_share : (k + 1) * col_share]
                for k in range(NP)
                for c in range(cols)
            ],
            axis=1,
        )
        my_tile = my_row * tiles + step * subs
        parts = []
        for i in range(subs):
            part = slice(i * TS, (i + 1) * TS)
            parts.append(
                jnp.where(group_row == group_of[my_tile + i], entries[part], 0.0)
                + jnp.where(kid_row == kid_of[my_tile + i], product[part], 0.0)
            )
        full = jnp.concatenate(parts, axis=0)
        head, tail = solve_rows(
            full[:, :PW], full[:, PW:],
            inv1_t_hi[...], inv1_t_lo[...], inv2_t_hi[...], inv2_t_lo[...], link_t[...],
        )
        solved[:, :PW] = head
        solved[:, PW:] = tail

        @pl.when(step == 0)
        def _():
            at = pl.multiple_of(my_row * share, share)
            solved[:share, :PW] = lower1[pl.ds(at, share), :]
            solved[:share, PW:] = jnp.zeros((share, PW), F32)
            solved[share : 2 * share, :PW] = lower1[pl.ds(PW + at, share), :]
            solved[share : 2 * share, PW:] = lower2[pl.ds(at, share), :]

        moved_out = jnp.zeros((block_rows, 128), F32)
        for k in range(NP):
            tile = pl.multiple_of(k * PW + (my_col // per_tile) * 128, 128)
            turn = (128 + k * col_share - (my_col % per_tile) * col_share) % 128
            moved = pltpu.roll(solved[:, pl.ds(tile, 128)], turn, 1)
            moved_out = jnp.where(lane // col_share == k, moved, moved_out)
        panel[rows_at(step), :] = moved_out[:, : NP * col_share].astype(BF16)

        slot, hold = step % ins, step % holds
        front_copy(step, slot).wait()

        @pl.when(step >= holds)
        def _():
            out_copy(step - holds, hold).wait()

        lead = solved[...].astype(BF16)
        for n in range(local_cols // span):
            at = slice(n * span, (n + 1) * span)
            update = dot(lead, flipped[:, at])
            product = dot(own, kids[:, at])
            group_all = tile_values(group_of, first_tile + n * (span // TS), span // TS)
            kid_all = tile_values(kid_of, first_tile + n * (span // TS), span // TS)
            for i in range(subs):
                part = slice(i * TS, (i + 1) * TS)
                outs[hold, part, at] = (
                    jnp.where(group_all == group_of[my_tile + i], fronts[slot, part, at], 0.0)
                    + jnp.where(kid_all == kid_of[my_tile + i], product[part], 0.0)
                    + update[part]
                )
        for q in range(fan):
            outs[hold, :, q * local_rows : q * local_rows + held] = jnp.zeros((block_rows, held), F32)

        @pl.when(step == 0)
        def _():
            outs[hold, :held, :] = jnp.zeros((held, local_cols), F32)

        out_copy(step, hold).start()

        @pl.when(step + ins < steps)
        def _():
            front_copy(step + ins, slot).start()

        return carry

    lax.fori_loop(0, steps, work_rows, 0)
    for i in range(max(0, steps - holds), steps):
        out_copy(i, i % holds).wait()


def params():
    return pltpu.CompilerParams(vmem_limit_bytes=VMEM_BYTES)


def local(front_entries, tile_group, child_factor, row_map):
    rows, cols = lax.axis_size("row"), lax.axis_size("col")
    fan = rows // cols
    assert fan == 2
    local_rows, local_cols = front_entries.shape
    slice_cols = child_factor.shape[1]
    kid_cols = slice_cols * cols
    tiles = local_rows // TS
    share = PW // rows
    held = NP * share
    my_row, my_col = lax.axis_index("row"), lax.axis_index("col")
    place = jnp.stack([my_row, my_col]).astype(jnp.int32)

    flipped = child_factor.T
    own_map = lax.dynamic_slice_in_dim(row_map, my_row * tiles, tiles)
    starts = flipped.reshape(slice_cols, tiles, TS)[:, :, :held]

    def chosen(block):
        keep = (own_map == block * tiles)[None, :, None]
        return jnp.sum(jnp.where(keep, starts, 0), axis=1, dtype=F32)

    corner = jnp.concatenate(
        [
            front_entries[:held, q * local_rows + k * share : q * local_rows + (k + 1) * share]
            for k in range(NP)
            for q in range(fan)
        ],
        axis=1,
    )
    kids = jnp.concatenate([chosen(my_row), chosen(jnp.bitwise_xor(my_row, rows // 2))], axis=1)
    packet = jnp.concatenate([corner, kids], axis=0)
    packets = [swapped(packet, "row", d * fan) for d in range(cols)]

    row_strip = jnp.concatenate(
        [
            front_entries[:, q * local_rows + k * share : q * local_rows + (k + 1) * share]
            for k in range(NP)
            for q in range(fan)
        ],
        axis=1,
    )
    steps = [1 << i for i in range(cols.bit_length() - 1)]
    orders = [steps, steps[::-1]]
    halves = [row_strip[None, : local_rows // 2], row_strip[None, local_rows // 2 :]]
    masks = [[0], [0]]
    for h in range(2):
        for step in orders[h][:-2]:
            halves[h] = jnp.concatenate([halves[h], swapped(halves[h], "col", step)], axis=0)
            masks[h] = masks[h] + [m ^ step for m in masks[h]]
    others = [swapped(halves[h], "col", orders[h][-2]) for h in range(2)]
    masks = [masks[h] + [m ^ orders[h][-2] for m in masks[h]] for h in range(2)]
    gathered = lax.all_gather(flipped, "row", axis=0)
    col_strip, *packets = lax.optimization_barrier((front_entries[:held].astype(BF16), *packets))
    col_strips = lax.all_gather(col_strip, "row", axis=0)
    merged = []
    for d in range(cols):
        kid = packets[d][held:, :held] + packets[d ^ (cols // 2)][held:, held:]
        half = slice_cols // 2
        merged.append(
            jnp.concatenate(
                [packets[d][:held], jnp.concatenate([kid[:half], kid[half:]], axis=1)], axis=0
            )
        )
    merged = jnp.stack(merged)
    near = jnp.stack([swapped(merged, "col", d) for d in range(cols)])
    far = swapped(near, "row", 1)

    tile_ids = jnp.arange(row_map.shape[0], dtype=jnp.int32)
    inverse_map = jnp.sum(
        jnp.where(row_map[None, :] == tile_ids[:, None], tile_ids[None, :], 0), axis=1, dtype=jnp.int32
    )
    kid_of = (inverse_map >= row_map.shape[0] // 2).astype(F32)
    group_of = jnp.repeat(tile_group, MT // TS).astype(F32)

    placed = pl.pallas_call(
        functools.partial(place_kernel, (cols, fan, tiles, slice_cols)),
        out_shape=[jax.ShapeDtypeStruct((2 * slice_cols, local_rows), BF16)] * cols,
        in_specs=[smem_spec()] * 2 + [whole_spec()],
        out_specs=[whole_spec()] * cols,
        compiler_params=params(),
        cost_estimate=pl.CostEstimate(flops=0, bytes_accessed=8 * 2**20, transcendentals=0),
        name="place_tiles",
    )(place, inverse_map, gathered)
    near, far, *placed = lax.optimization_barrier((near, far, *placed))
    kid_parts = [swapped(placed[d], "col", d) for d in range(cols)]
    square = jax.ShapeDtypeStruct((PW, PW), BF16)
    lower1, inv1_hi, inv1_lo, inv1_t_hi, inv1_t_lo, link, link_t, rest, piv_t, piv = pl.pallas_call(
        functools.partial(first_kernel, (cols, fan, share, held, tiles)),
        out_shape=[
            jax.ShapeDtypeStruct((2 * PW, PW), F32),
            square, square, square, square, square, square,
            jax.ShapeDtypeStruct((PW, PW), F32),
            jax.ShapeDtypeStruct((kid_cols, NPIV), BF16),
            jax.ShapeDtypeStruct((NPIV, kid_cols), BF16),
        ],
        in_specs=[smem_spec()] * 3 + [whole_spec()] * 2,
        out_specs=[whole_spec()] * 10,
        scratch_shapes=[
            pltpu.VMEM((NPIV, NPIV), F32),
            pltpu.VMEM((NPIV, kid_cols), F32),
            pltpu.VMEM((PW, 2 * PW), F32),
        ],
        compiler_params=params(),
        cost_estimate=pl.CostEstimate(flops=2 * 10**10, bytes_accessed=5 * 10**7, transcendentals=0),
        name="first_pivots",
    )(place, group_of, kid_of, near, far)

    rest, *arrived = lax.optimization_barrier((rest, *halves, *others))
    halves = [jnp.concatenate([arrived[h], arrived[2 + h]], axis=0) for h in range(2)]
    *halves, rest, kid_parts = lax.optimization_barrier((*halves, rest, kid_parts))
    near_kids = jnp.concatenate([part[slice_cols:] for part in kid_parts], axis=0)
    rest, near_kids = lax.optimization_barrier((rest, near_kids))
    far_kids = swapped(near_kids, "row", 1)
    others = [swapped(halves[h], "col", orders[h][-1]) for h in range(2)]
    masks = [masks[h] + [m ^ orders[h][-1] for m in masks[h]] for h in range(2)]
    lower2, inv2_hi, inv2_lo, inv2_t_hi, inv2_t_lo = pl.pallas_call(
        second_kernel,
        out_shape=[jax.ShapeDtypeStruct((PW, PW), F32), square, square, square, square],
        in_specs=[whole_spec()],
        out_specs=[whole_spec()] * 5,
        scratch_shapes=[pltpu.VMEM((PW, 2 * PW), F32)],
        compiler_params=params(),
        cost_estimate=pl.CostEstimate(flops=2 * 10**10, bytes_accessed=5 * 10**7, transcendentals=0),
        name="second_pivots",
    )(rest)

    block_rows = min(256, local_rows)
    wide = min(512, local_cols)
    ins, holds = min(4, local_rows // block_rows), min(3, local_rows // block_rows)
    schur_block, factor_panels = pl.pallas_call(
        functools.partial(
            schur_kernel,
            (rows, cols, fan, share, held, slice_cols, block_rows, local_rows, local_cols, tiles, wide),
            masks,
        ),
        out_shape=[
            jax.ShapeDtypeStruct((local_rows, local_cols), F32),
            jax.ShapeDtypeStruct((local_rows, NP * PW // cols), BF16),
        ],
        in_specs=[smem_spec()] * 3 + [whole_spec()] * 14 + [any_spec()] * (8 + cols),
        out_specs=[any_spec(), whole_spec()],
        scratch_shapes=[
            pltpu.VMEM((ins, block_rows, local_cols), F32),
            pltpu.VMEM((holds, block_rows, local_cols), F32),
            pltpu.VMEM((rows, held, local_cols), BF16),
            pltpu.VMEM((kid_cols, local_cols), BF16),
            pltpu.VMEM((kid_cols, local_rows), BF16),
            pltpu.VMEM((cols, local_rows, fan * held), F32),
            pltpu.VMEM((NPIV, local_cols), BF16),
            pltpu.VMEM((NPIV, wide), F32),
            pltpu.VMEM((block_rows, NPIV), F32),
            pltpu.SemaphoreType.DMA((ins,)),
            pltpu.SemaphoreType.DMA((holds,)),
            pltpu.SemaphoreType.DMA((local_cols // wide,)),
            pltpu.SemaphoreType.DMA((fan,)),
            pltpu.SemaphoreType.DMA((cols,)),
            pltpu.SemaphoreType.DMA((2 * cols,)),
        ],
        compiler_params=params(),
        cost_estimate=pl.CostEstimate(flops=3 * 10**10, bytes_accessed=9 * 10**7, transcendentals=0),
        name="schur_update",
    )(
        place, group_of, kid_of,
        piv, piv_t, lower1, lower2, inv1_hi, inv1_lo, inv2_hi, inv2_lo, link,
        inv1_t_hi, inv1_t_lo, inv2_t_hi, inv2_t_lo, link_t,
        front_entries, col_strips, near_kids, far_kids, *kid_parts,
        halves[0], others[0], halves[1], others[1],
    )
    return (factor_panels, schur_block)


def solution(mesh):
    placed = (P("row", "col"), P(), P("row", "col"), P())
    return jax.shard_map(
        local,
        mesh=mesh,
        in_specs=placed,
        out_specs=(P("row", "col"), P("row", "col")),
        check_vma=False,
    )
```

```python
import functools

import jax
import jax.numpy as jnp
from jax import lax
from jax.experimental import pallas as pl
from jax.experimental.pallas import tpu as pltpu
from jax.sharding import PartitionSpec as P

PW = 256
NP = 2
TS = 128
MT = 512
NPIV = NP * PW
BLK = 32
F32 = jnp.float32
BF16 = jnp.bfloat16
VMEM_BYTES = 60 * 1024 * 1024

NN = (((1,), (0,)), ((), ()))
NT = (((1,), (1,)), ((), ()))


def dot(left, right, dims=NN, precision=None):
    return lax.dot_general(left, right, dims, precision=precision, preferred_element_type=F32)


def exact(left, right, dims=NN):
    return dot(left, right, dims, lax.Precision.HIGHEST)


def split(value):
    high = value.astype(BF16)
    return high, (value - high.astype(F32)).astype(BF16)


def swapped(value, axis, mask):
    if mask == 0:
        return value
    return lax.ppermute(value, axis, [(i, i ^ mask) for i in range(lax.axis_size(axis))])


def whole_spec():
    return pl.BlockSpec(memory_space=pltpu.VMEM)


def any_spec():
    return pl.BlockSpec(memory_space=pl.ANY)


def smem_spec():
    return pl.BlockSpec(memory_space=pltpu.SMEM)


def factor_diagonal(block):
    groups = BLK // 8
    lane = lax.broadcasted_iota(jnp.int32, (BLK, 128), 1)
    row = lax.broadcasted_iota(jnp.int32, (BLK, 128), 0)
    row8 = lax.broadcasted_iota(jnp.int32, (8, 128), 0)
    start = jnp.where(lane < BLK, block, jnp.where(lane == row + BLK, 1.0, 0.0))
    work = [start[8 * g : 8 * g + 8] for g in range(groups)]
    cols = []
    for k in range(BLK):
        base = 8 * (k // 8)
        cols.append(jnp.broadcast_to(block[base:, k : k + 1], (BLK - base, 128)))
    scale = [jnp.ones((8, 128), F32) for _ in range(groups)]

    def inverse_root(value):
        root = lax.rsqrt(value)
        return root * (1.5 - 0.5 * value * root * root)

    for j in range(0, BLK, 2):
        g0 = j // 8
        base = 8 * g0
        one, two = cols[j], cols[j + 1]
        first, cross, last = one[j - base : j - base + 1], one[j - base + 1 : j - base + 2], two[j - base + 1 : j - base + 2]
        volume = first * last - cross * cross
        root = inverse_root(volume)
        inverse = root * root
        below = row[base:] > j + 1
        lead_one = jnp.where(below, last * one - cross * two, 0.0) * inverse
        lead_two = jnp.where(below, first * two - cross * one, 0.0) * inverse
        row_one, row_two = work[g0][j - base : j - base + 1], work[g0][j - base + 1 : j - base + 2]
        for k in range(j + 2, BLK):
            skip = 8 * (k // 8 - g0)
            cols[k] = cols[k] - (
                lead_one[skip:] * one[k - base : k - base + 1] + lead_two[skip:] * two[k - base : k - base + 1]
            )
        for g in range(g0, groups):
            part = slice(8 * (g - g0), 8 * (g - g0) + 8)
            work[g] = work[g] - (lead_one[part] * row_one + lead_two[part] * row_two)
        first_root = inverse_root(first)
        ratio = cross * (first_root * first_root)
        work[g0] = work[g0] - jnp.where(row8 == j - base + 1, ratio, 0.0) * row_one
        scale[g0] = jnp.where(row8 == j - base, first_root, scale[g0])
        scale[g0] = jnp.where(row8 == j - base + 1, first * first_root * root, scale[g0])
    return jnp.concatenate([work[g] * scale[g] for g in range(groups)], axis=0)


def factor_panel(work, start, stop):
    per_tile = 128 // BLK
    row = lax.broadcasted_iota(jnp.int32, (PW, BLK), 0)
    lane = lax.broadcasted_iota(jnp.int32, (BLK, 128), 1)

    def step(b, carry):
        low = pl.multiple_of(b * BLK, BLK)
        tile = pl.multiple_of((b // per_tile) * 128, 128)
        turn = (128 - (b % per_tile) * BLK) % 128
        columns = pltpu.roll(work[:, pl.ds(tile, 128)], turn, 1)
        block = pltpu.roll(work[pl.ds(low, BLK), pl.ds(tile, 128)], turn, 1)
        done = factor_diagonal(block)
        inverse = jnp.where(lane < BLK, pltpu.roll(done, 128 - BLK, 1), 0.0)
        upper = exact(inverse[:, :BLK], work[pl.ds(low, BLK), :])
        lead = exact(columns, inverse, NT)
        lead = jnp.where(row >= low + BLK, lead, 0.0)
        work[...] = work[...] - exact(lead, upper)
        work[pl.ds(low, BLK), :] = upper
        return carry

    lax.fori_loop(start, stop, step, 0)


def diagonals(value):
    row = lax.broadcasted_iota(jnp.int32, (PW, PW), 0)
    col = lax.broadcasted_iota(jnp.int32, (PW, PW), 1)
    kept = jnp.where(row == col, value, 0.0)
    return jnp.sum(kept, axis=1, keepdims=True), jnp.sum(kept, axis=0, keepdims=True)


def start_panel(work, diag_col, diag_row, value):
    by_row, by_col = diagonals(value)
    diag_col[...] = jnp.broadcast_to(by_row, (PW, 128))
    diag_row[...] = jnp.broadcast_to(by_col, (8, PW))
    work[:, :PW] = value / jnp.sqrt(by_row) / jnp.sqrt(by_col)
    work[:, PW:] = unit()


def pivot_values(table, stride, share, along_rows):
    shape = (NPIV, 1) if along_rows else (1, NPIV)
    block = lax.broadcasted_iota(jnp.int32, shape, 0 if along_rows else 1) % PW // share
    values = jnp.zeros(shape, F32)
    for r in range(PW // share):
        values = jnp.where(block == r, table[r * stride], values)
    return values


def tile_values(table, start, count):
    return jnp.concatenate([jnp.full((1, TS), table[start + i], F32) for i in range(count)], axis=1)


def finish_panel(work, diag_col, diag_row, lower, inv_hi, inv_lo, inv_t_hi, inv_t_lo):
    row = lax.broadcasted_iota(jnp.int32, (PW, PW), 0)
    col = lax.broadcasted_iota(jnp.int32, (PW, PW), 1)
    lower[:PW, :] = jnp.where(col <= row, work[:, :PW].T, 0.0) * jnp.sqrt(diag_col[:, :1])
    inverse = work[:, PW:] / jnp.sqrt(diag_row[:1, :])
    inv_hi[...], inv_lo[...] = split(inverse)
    inv_t_hi[...], inv_t_lo[...] = split(inverse.T)
    return inverse


def unit():
    row = lax.broadcasted_iota(jnp.int32, (PW, PW), 0)
    col = lax.broadcasted_iota(jnp.int32, (PW, PW), 1)
    return jnp.where(row == col, 1.0, 0.0)


def open_kernel(sizes, place, group_of, kid_of, near, far,
                work, diag_col, diag_row, low_rows, piv_t, piv, pile, wide):
    cols, fan, share, held, tiles = sizes
    my_row, my_col = place[0], place[1]
    my_q, my_a = my_row % fan, my_row // fan
    col_share = PW // cols
    for dq, source in enumerate((near, far)):
        for d in range(cols):
            r = (my_a ^ d) * fan + (my_q ^ dq)
            pieces = [source[c ^ my_col, d, :held, :] for c in range(cols)]
            line = jnp.concatenate(
                [piece[:, k * col_share : (k + 1) * col_share] for k in range(NP) for piece in pieces],
                axis=1,
            )
            kids = []
            for e in range(cols):
                packed = source[e, d, held:, :]
                kids += [packed[:, :held], packed[:, held:]]
            kids = jnp.concatenate(kids, axis=0).T
            for k in range(NP):
                at = pl.ds(pl.multiple_of(k * PW + r * share, share), share)
                pile[at, :] = line[k * share : (k + 1) * share]
                wide[at, :] = kids[k * share : (k + 1) * share]
    piv[...] = wide[...].astype(BF16)
    piv_t[...] = wide[...].T.astype(BF16)
    product = dot(piv[...], piv_t[...])
    same_group = pivot_values(group_of, tiles, share, True) == pivot_values(group_of, tiles, share, False)
    same_kid = pivot_values(kid_of, tiles, share, True) == pivot_values(kid_of, tiles, share, False)
    pile[...] = jnp.where(same_group, pile[...], 0.0) + jnp.where(same_kid, product, 0.0)
    low_rows[...] = pile[PW:, :]
    start_panel(work, diag_col, diag_row, pile[:PW, :PW])
    factor_panel(work, 0, PW // BLK // 2)


def first_kernel(begun, diag_col, diag_row, low_rows,
                 lower, inv_hi, inv_lo, inv_t_hi, inv_t_lo, link_out, link_t, rest, work):
    work[...] = begun[...]
    factor_panel(work, PW // BLK // 2, PW // BLK)
    inverse = finish_panel(work, diag_col, diag_row, lower, inv_hi, inv_lo, inv_t_hi, inv_t_lo)
    link = exact(low_rows[:, :PW], inverse, NT).astype(BF16)
    link_out[...] = link
    lower[PW:, :] = link.astype(F32)
    link_t[...] = link.astype(F32).T.astype(BF16)
    rest[...] = low_rows[:, PW:] - dot(link, link, NT)


def second_kernel(rest, lower, inv_hi, inv_lo, inv_t_hi, inv_t_lo, work, diag_col, diag_row):
    start_panel(work, diag_col, diag_row, rest[...])
    factor_panel(work, 0, PW // BLK)
    finish_panel(work, diag_col, diag_row, lower, inv_hi, inv_lo, inv_t_hi, inv_t_lo)


def place_kernel(sizes, place, inverse_map, held, *outs):
    cols, fan, tiles, slice_cols = sizes
    my_row, my_col = place[0], place[1]
    my_q = my_row % fan

    def fetch(block, i):
        tile = inverse_map[block * tiles + i]
        at = pl.multiple_of((tile % tiles) * TS, TS)
        return held[tile // tiles, :, pl.ds(at, TS)]

    for i in range(tiles):
        mine = fetch(my_row, i)
        for d in range(cols):
            outs[d][:slice_cols, i * TS : (i + 1) * TS] = mine
    for d in range(cols):
        for i in range(tiles):
            outs[d][slice_cols:, i * TS : (i + 1) * TS] = fetch((my_col ^ d) * fan + my_q, i)


def schur_kernel(sizes, masks, place, group_of, kid_of,
                 piv, piv_t, lower1, lower2, inv1_hi, inv1_lo, inv2_hi, inv2_lo, link,
                 inv1_t_hi, inv1_t_lo, inv2_t_hi, inv2_t_lo, link_t, *refs):
    rows, cols, fan, share, held, slice_cols, block_rows, local_rows, local_cols, tiles, wide = sizes
    front, strips, near_kids, far_kids = refs[:4]
    sources = refs[4 : 4 + cols]
    halves = [refs[4 + cols : 6 + cols], refs[6 + cols : 8 + cols]]
    out, panel = refs[8 + cols : 10 + cols]
    (fronts, outs, strips_in, kids, own_t, pieces, flipped, strip, solved_even, solved_odd, own_even, own_odd,
     front_sems, out_sems, strip_sems, kid_sems, own_sems, piece_sems) = refs[10 + cols :]
    my_row, my_col = place[0], place[1]
    my_q = my_row % fan
    first_tile = my_col * fan * tiles
    steps = local_rows // block_rows
    chunks = local_cols // wide
    depth = fronts.shape[0] // 2
    half_rows = local_rows // 2

    def rows_at(i):
        return pl.ds(pl.multiple_of(i * block_rows, block_rows), block_rows)

    def front_copy(i, slot):
        return pltpu.make_async_copy(front.at[rows_at(i), :], fronts.at[slot], front_sems.at[slot])

    def out_copy(i, slot):
        return pltpu.make_async_copy(outs.at[slot], out.at[rows_at(i), :], out_sems.at[slot])

    def chunk_at(n):
        return pl.ds(pl.multiple_of(n * wide, wide), wide)

    def strip_copy(n):
        return pltpu.make_async_copy(
            strips.at[:, :, chunk_at(n)], strips_in.at[:, :, chunk_at(n)], strip_sems.at[n]
        )

    kid_copies = [
        pltpu.make_async_copy(
            source,
            kids.at[:, pl.ds(pl.multiple_of((my_q ^ q) * local_rows, local_rows), local_rows)],
            kid_sems.at[q],
        )
        for q, source in enumerate((near_kids, far_kids))
    ]
    own_copies = [
        pltpu.make_async_copy(
            source.at[:slice_cols, :], own_t.at[d * slice_cols : (d + 1) * slice_cols, :], own_sems.at[d]
        )
        for d, source in enumerate(sources)
    ]
    piece_copies = [
        pltpu.make_async_copy(
            halves[half][i // (cols // 2)].at[i % (cols // 2)],
            pieces.at[my_col ^ mask, half * half_rows : (half + 1) * half_rows, :],
            piece_sems.at[half * cols + i],
        )
        for half in range(2)
        for i, mask in enumerate(masks[half])
    ]
    for copy in kid_copies:
        copy.start()
    for n in range(chunks):
        strip_copy(n).start()
    for copy in own_copies + piece_copies:
        copy.start()
    for copy in kid_copies:
        copy.wait()
    group_col = pivot_values(group_of, tiles, share, True)
    kid_col = pivot_values(kid_of, tiles, share, True)

    def col_solve(n, pile):
        at = slice(n * wide, (n + 1) * wide)
        for r in range(rows):
            piece = strips_in[r, :, at].astype(F32)
            for k in range(NP):
                low = k * PW + r * share
                pile[low : low + share, :] = piece[k * share : (k + 1) * share]
        tile = first_tile + n * (wide // TS)
        group_all = tile_values(group_of, tile, wide // TS)
        kid_all = tile_values(kid_of, tile, wide // TS)
        product = dot(piv[...], kids[:, at])
        yield
        full = jnp.where(group_col == group_all, pile[...], 0.0) + jnp.where(
            kid_col == kid_all, product, 0.0
        )
        first, second = full[:PW].astype(BF16), full[PW:]
        yield
        both = dot(jnp.concatenate([inv1_hi[...], inv1_lo[...]], axis=0), first)
        yield
        head = (both[:PW] + both[PW:]).astype(BF16)
        flipped[:PW, at] = -head
        yield
        second = (second - dot(link[...], head)).astype(BF16)
        yield
        both = dot(jnp.concatenate([inv2_hi[...], inv2_lo[...]], axis=0), second)
        yield
        flipped[PW:, at] = (-(both[:PW] + both[PW:])).astype(BF16)

    col_share = PW // cols
    subs = block_rows // TS
    per_tile = 128 // col_share
    span = min(512, local_cols)
    group_row = pivot_values(group_of, tiles, share, False)
    kid_row = pivot_values(kid_of, tiles, share, False)
    lane = lax.broadcasted_iota(jnp.int32, (block_rows, 128), 1)

    def row_solve(step, opening, own_ref, solved):
        own = own_t[:, rows_at(step)].astype(F32).T.astype(BF16)
        own_ref[...] = own
        product = dot(own, piv_t[...])
        yield
        entries = jnp.concatenate(
            [
                pieces[c, rows_at(step), k * col_share : (k + 1) * col_share]
                for k in range(NP)
                for c in range(cols)
            ],
            axis=1,
        )
        my_tile = my_row * tiles + step * subs
        parts = []
        for i in range(subs):
            part = slice(i * TS, (i + 1) * TS)
            parts.append(
                jnp.where(group_row == group_of[my_tile + i], entries[part], 0.0)
                + jnp.where(kid_row == kid_of[my_tile + i], product[part], 0.0)
            )
        full = jnp.concatenate(parts, axis=0)
        high, low = split(full[:, :PW])
        yield
        head = dot(high, inv1_t_hi[...]) + dot(high, inv1_t_lo[...]) + dot(low, inv1_t_hi[...])
        solved[:, :PW] = head
        yield
        high, low = split(full[:, PW:] - dot(head.astype(BF16), link_t[...]))
        yield
        solved[:, PW:] = dot(high, inv2_t_hi[...]) + dot(high, inv2_t_lo[...]) + dot(low, inv2_t_hi[...])
        yield
        if opening:
            at = pl.multiple_of(my_row * share, share)
            solved[:share, :PW] = lower1[pl.ds(at, share), :]
            solved[:share, PW:] = jnp.zeros((share, PW), F32)
            solved[share : 2 * share, :PW] = lower1[pl.ds(PW + at, share), :]
            solved[share : 2 * share, PW:] = lower2[pl.ds(at, share), :]
        moved_out = jnp.zeros((block_rows, 128), F32)
        for k in range(NP):
            tile = pl.multiple_of(k * PW + (my_col // per_tile) * 128, 128)
            turn = (128 + k * col_share - (my_col % per_tile) * col_share) % 128
            moved = pltpu.roll(solved[:, pl.ds(tile, 128)], turn, 1)
            moved_out = jnp.where(lane // col_share == k, moved, moved_out)
        panel[rows_at(step), :] = moved_out[:, : NP * col_share].astype(BF16)

    def update(step, slot, own_ref, solved):
        lead, own = solved[...].astype(BF16), own_ref[...]
        my_tile = my_row * tiles + step * subs
        for n in range(local_cols // span):
            at = slice(n * span, (n + 1) * span)
            change = dot(lead, flipped[:, at])
            product = dot(own, kids[:, at])
            group_all = tile_values(group_of, first_tile + n * (span // TS), span // TS)
            kid_all = tile_values(kid_of, first_tile + n * (span // TS), span // TS)
            for i in range(subs):
                part = slice(i * TS, (i + 1) * TS)
                outs[slot, part, at] = (
                    jnp.where(group_all == group_of[my_tile + i], fronts[slot, part, at], 0.0)
                    + jnp.where(kid_all == kid_of[my_tile + i], product[part], 0.0)
                    + change[part]
                )
            yield

    def together(*parts):
        parts = list(parts)
        while parts:
            for part in list(parts):
                try:
                    next(part)
                except StopIteration:
                    parts.remove(part)

    for n in range(0, chunks, 2):
        pair = range(n, min(n + 2, chunks))
        for m in pair:
            strip_copy(m).wait()
        if n == 0:
            for i in range(2 * depth):
                front_copy(i, i).start()
        together(*[col_solve(m, strip.at[m - n]) for m in pair])
    for copy in own_copies + piece_copies:
        copy.wait()
    together(row_solve(0, True, own_even, solved_even))

    def two_blocks(pair, carry):
        for odd in range(2):
            step = 2 * pair + odd
            slot = 2 * lax.rem(pair, depth) + odd
            front_copy(step, slot).wait()

            @pl.when(pair >= depth)
            def _():
                out_copy(step - 2 * depth, slot).wait()

            if odd:
                mine, later = (own_odd, solved_odd), (own_even, solved_even)
            else:
                mine, later = (own_even, solved_even), (own_odd, solved_odd)
            together(update(step, slot, *mine), row_solve(jnp.minimum(step + 1, steps - 1), False, *later))
            for q in range(fan):
                outs[slot, :, q * local_rows : q * local_rows + held] = jnp.zeros((block_rows, held), F32)
            if not odd:

                @pl.when(pair == 0)
                def _():
                    outs[slot, :held, :] = jnp.zeros((held, local_cols), F32)

            out_copy(step, slot).start()

            @pl.when(pair + depth < steps // 2)
            def _():
                front_copy(step + 2 * depth, slot).start()

        return carry

    lax.fori_loop(0, steps // 2, two_blocks, 0)
    for i in range(steps - 2 * depth, steps):
        out_copy(i, i % (2 * depth)).wait()


def params():
    return pltpu.CompilerParams(vmem_limit_bytes=VMEM_BYTES)


def local(front_entries, tile_group, child_factor, row_map):
    rows, cols = lax.axis_size("row"), lax.axis_size("col")
    fan = rows // cols
    assert fan == 2
    local_rows, local_cols = front_entries.shape
    slice_cols = child_factor.shape[1]
    kid_cols = slice_cols * cols
    tiles = local_rows // TS
    share = PW // rows
    held = NP * share
    my_row, my_col = lax.axis_index("row"), lax.axis_index("col")
    place = jnp.stack([my_row, my_col]).astype(jnp.int32)

    flipped = child_factor.T
    own_map = lax.dynamic_slice_in_dim(row_map, my_row * tiles, tiles)
    starts = flipped.reshape(slice_cols, tiles, TS)[:, :, :held]

    def chosen(block):
        keep = (own_map == block * tiles)[None, :, None]
        return jnp.sum(jnp.where(keep, starts, 0), axis=1, dtype=F32)

    corner = jnp.concatenate(
        [
            front_entries[:held, q * local_rows + k * share : q * local_rows + (k + 1) * share]
            for k in range(NP)
            for q in range(fan)
        ],
        axis=1,
    )
    kids = jnp.concatenate([chosen(my_row), chosen(jnp.bitwise_xor(my_row, rows // 2))], axis=1)
    packet = jnp.concatenate([corner, kids], axis=0)
    packets = [swapped(packet, "row", d * fan) for d in range(cols)]

    row_strip = jnp.concatenate(
        [
            front_entries[:, q * local_rows + k * share : q * local_rows + (k + 1) * share]
            for k in range(NP)
            for q in range(fan)
        ],
        axis=1,
    )
    steps = [1 << i for i in range(cols.bit_length() - 1)]
    orders = [steps, steps[::-1]]
    halves = [row_strip[None, : local_rows // 2], row_strip[None, local_rows // 2 :]]
    masks = [[0], [0]]
    for h in range(2):
        for step in orders[h][:-2]:
            halves[h] = jnp.concatenate([halves[h], swapped(halves[h], "col", step)], axis=0)
            masks[h] = masks[h] + [m ^ step for m in masks[h]]
    others = [swapped(halves[h], "col", orders[h][-2]) for h in range(2)]
    masks = [masks[h] + [m ^ orders[h][-2] for m in masks[h]] for h in range(2)]
    gathered = lax.all_gather(flipped, "row", axis=0)
    col_strip, *packets = lax.optimization_barrier((front_entries[:held].astype(BF16), *packets))
    col_strips = lax.all_gather(col_strip, "row", axis=0)
    merged = []
    for d in range(cols):
        kid = packets[d][held:, :held] + packets[d ^ (cols // 2)][held:, held:]
        half = slice_cols // 2
        merged.append(
            jnp.concatenate(
                [packets[d][:held], jnp.concatenate([kid[:half], kid[half:]], axis=1)], axis=0
            )
        )
    merged = jnp.stack(merged)
    near = jnp.stack([swapped(merged, "col", d) for d in range(cols)])
    far = swapped(near, "row", 1)

    tile_ids = jnp.arange(row_map.shape[0], dtype=jnp.int32)
    inverse_map = jnp.sum(
        jnp.where(row_map[None, :] == tile_ids[:, None], tile_ids[None, :], 0), axis=1, dtype=jnp.int32
    )
    kid_of = (inverse_map >= row_map.shape[0] // 2).astype(F32)
    group_of = jnp.repeat(tile_group, MT // TS).astype(F32)

    half_cost = pl.CostEstimate(flops=10**10, bytes_accessed=3 * 10**7, transcendentals=0)
    work_shape = jax.ShapeDtypeStruct((PW, 2 * PW), F32)
    begun, diag_col, diag_row, low_rows, piv_t, piv = pl.pallas_call(
        functools.partial(open_kernel, (cols, fan, share, held, tiles)),
        out_shape=[
            work_shape,
            jax.ShapeDtypeStruct((PW, 128), F32),
            jax.ShapeDtypeStruct((8, PW), F32),
            jax.ShapeDtypeStruct((PW, NPIV), F32),
            jax.ShapeDtypeStruct((kid_cols, NPIV), BF16),
            jax.ShapeDtypeStruct((NPIV, kid_cols), BF16),
        ],
        in_specs=[smem_spec()] * 3 + [whole_spec()] * 2,
        out_specs=[whole_spec()] * 6,
        scratch_shapes=[pltpu.VMEM((NPIV, NPIV), F32), pltpu.VMEM((NPIV, kid_cols), F32)],
        compiler_params=params(),
        cost_estimate=half_cost,
        name="open_pivots",
    )(place, group_of, kid_of, near, far)

    begun, gathered = lax.optimization_barrier((begun, gathered))
    placed = pl.pallas_call(
        functools.partial(place_kernel, (cols, fan, tiles, slice_cols)),
        out_shape=[jax.ShapeDtypeStruct((2 * slice_cols, local_rows), BF16)] * cols,
        in_specs=[smem_spec()] * 2 + [whole_spec()],
        out_specs=[whole_spec()] * cols,
        compiler_params=params(),
        cost_estimate=pl.CostEstimate(flops=0, bytes_accessed=8 * 2**20, transcendentals=0),
        name="place_tiles",
    )(place, inverse_map, gathered)
    begun, *placed = lax.optimization_barrier((begun, *placed))
    kid_parts = [swapped(placed[d], "col", d) for d in range(cols)]
    square = jax.ShapeDtypeStruct((PW, PW), BF16)
    lower1, inv1_hi, inv1_lo, inv1_t_hi, inv1_t_lo, link, link_t, rest = pl.pallas_call(
        first_kernel,
        out_shape=[
            jax.ShapeDtypeStruct((2 * PW, PW), F32),
            square, square, square, square, square, square,
            jax.ShapeDtypeStruct((PW, PW), F32),
        ],
        in_specs=[whole_spec()] * 4,
        out_specs=[whole_spec()] * 8,
        scratch_shapes=[pltpu.VMEM((PW, 2 * PW), F32)],
        compiler_params=params(),
        cost_estimate=half_cost,
        name="first_pivots",
    )(begun, diag_col, diag_row, low_rows)

    rest, *arrived = lax.optimization_barrier((rest, *halves, *others))
    halves = [jnp.concatenate([arrived[h], arrived[2 + h]], axis=0) for h in range(2)]
    *halves, rest, kid_parts = lax.optimization_barrier((*halves, rest, kid_parts))
    near_kids = jnp.concatenate([part[slice_cols:] for part in kid_parts], axis=0)
    rest, near_kids = lax.optimization_barrier((rest, near_kids))
    far_kids = swapped(near_kids, "row", 1)
    others = [swapped(halves[h], "col", orders[h][-1]) for h in range(2)]
    masks = [masks[h] + [m ^ orders[h][-1] for m in masks[h]] for h in range(2)]
    lower2, inv2_hi, inv2_lo, inv2_t_hi, inv2_t_lo = pl.pallas_call(
        second_kernel,
        out_shape=[jax.ShapeDtypeStruct((PW, PW), F32), square, square, square, square],
        in_specs=[whole_spec()],
        out_specs=[whole_spec()] * 5,
        scratch_shapes=[
            pltpu.VMEM((PW, 2 * PW), F32),
            pltpu.VMEM((PW, 128), F32),
            pltpu.VMEM((8, PW), F32),
        ],
        compiler_params=params(),
        cost_estimate=pl.CostEstimate(flops=2 * 10**10, bytes_accessed=5 * 10**7, transcendentals=0),
        name="second_pivots",
    )(rest)

    block_rows = min(256, local_rows)
    wide = min(512, local_cols)
    depth = min(2, local_rows // block_rows // 2)
    schur_block, factor_panels = pl.pallas_call(
        functools.partial(
            schur_kernel,
            (rows, cols, fan, share, held, slice_cols, block_rows, local_rows, local_cols, tiles, wide),
            masks,
        ),
        out_shape=[
            jax.ShapeDtypeStruct((local_rows, local_cols), F32),
            jax.ShapeDtypeStruct((local_rows, NP * PW // cols), BF16),
        ],
        in_specs=[smem_spec()] * 3 + [whole_spec()] * 14 + [any_spec()] * (8 + cols),
        out_specs=[any_spec(), whole_spec()],
        scratch_shapes=[
            pltpu.VMEM((2 * depth, block_rows, local_cols), F32),
            pltpu.VMEM((2 * depth, block_rows, local_cols), F32),
            pltpu.VMEM((rows, held, local_cols), BF16),
            pltpu.VMEM((kid_cols, local_cols), BF16),
            pltpu.VMEM((kid_cols, local_rows), BF16),
            pltpu.VMEM((cols, local_rows, fan * held), F32),
            pltpu.VMEM((NPIV, local_cols), BF16),
            pltpu.VMEM((2, NPIV, wide), F32),
            pltpu.VMEM((block_rows, NPIV), F32),
            pltpu.VMEM((block_rows, NPIV), F32),
            pltpu.VMEM((block_rows, kid_cols), BF16),
            pltpu.VMEM((block_rows, kid_cols), BF16),
            pltpu.SemaphoreType.DMA((2 * depth,)),
            pltpu.SemaphoreType.DMA((2 * depth,)),
            pltpu.SemaphoreType.DMA((local_cols // wide,)),
            pltpu.SemaphoreType.DMA((fan,)),
            pltpu.SemaphoreType.DMA((cols,)),
            pltpu.SemaphoreType.DMA((2 * cols,)),
        ],
        compiler_params=params(),
        cost_estimate=pl.CostEstimate(flops=3 * 10**10, bytes_accessed=9 * 10**7, transcendentals=0),
        name="schur_update",
    )(
        place, group_of, kid_of,
        piv, piv_t, lower1, lower2, inv1_hi, inv1_lo, inv2_hi, inv2_lo, link,
        inv1_t_hi, inv1_t_lo, inv2_t_hi, inv2_t_lo, link_t,
        front_entries, col_strips, near_kids, far_kids, *kid_parts,
        halves[0], others[0], halves[1], others[1],
    )
    return (factor_panels, schur_block)


def solution(mesh):
    placed = (P("row", "col"), P(), P("row", "col"), P())
    return jax.shard_map(
        local,
        mesh=mesh,
        in_specs=placed,
        out_specs=(P("row", "col"), P("row", "col")),
        check_vma=False,
    )
```

```python
import functools

import jax
import jax.numpy as jnp
from jax import lax
from jax.experimental import pallas as pl
from jax.experimental.pallas import tpu as pltpu
from jax.sharding import PartitionSpec as P

PW = 256
NP = 2
TS = 128
MT = 512
NPIV = NP * PW
BLK = 32
F32 = jnp.float32
BF16 = jnp.bfloat16
VMEM_BYTES = 60 * 1024 * 1024

NN = (((1,), (0,)), ((), ()))
NT = (((1,), (1,)), ((), ()))
TN = (((0,), (0,)), ((), ()))


def dot(left, right, dims=NN, precision=None):
    return lax.dot_general(left, right, dims, precision=precision, preferred_element_type=F32)


def exact(left, right, dims=NN):
    return dot(left, right, dims, lax.Precision.HIGHEST)


def split(value):
    high = value.astype(BF16)
    return high, (value - high.astype(F32)).astype(BF16)


def swapped(value, axis, mask):
    if mask == 0:
        return value
    return lax.ppermute(value, axis, [(i, i ^ mask) for i in range(lax.axis_size(axis))])


def whole_spec():
    return pl.BlockSpec(memory_space=pltpu.VMEM)


def any_spec():
    return pl.BlockSpec(memory_space=pl.ANY)


def smem_spec():
    return pl.BlockSpec(memory_space=pltpu.SMEM)


def factor_diagonal(block):
    groups = BLK // 8
    lane = lax.broadcasted_iota(jnp.int32, (BLK, 128), 1)
    row = lax.broadcasted_iota(jnp.int32, (BLK, 128), 0)
    row8 = lax.broadcasted_iota(jnp.int32, (8, 128), 0)
    start = jnp.where(lane < BLK, block, jnp.where(lane == row + BLK, 1.0, 0.0))
    work = [start[8 * g : 8 * g + 8] for g in range(groups)]
    cols = []
    for k in range(BLK):
        base = 8 * (k // 8)
        cols.append(jnp.broadcast_to(block[base:, k : k + 1], (BLK - base, 128)))
    scale = [jnp.ones((8, 128), F32) for _ in range(groups)]

    def inverse_root(value):
        root = lax.rsqrt(value)
        return root * (1.5 - 0.5 * value * root * root)

    for j in range(0, BLK, 2):
        g0 = j // 8
        base = 8 * g0
        one, two = cols[j], cols[j + 1]
        first, cross, last = one[j - base : j - base + 1], one[j - base + 1 : j - base + 2], two[j - base + 1 : j - base + 2]
        volume = first * last - cross * cross
        root = inverse_root(volume)
        inverse = root * root
        below = row[base:] > j + 1
        lead_one = jnp.where(below, last * one - cross * two, 0.0) * inverse
        lead_two = jnp.where(below, first * two - cross * one, 0.0) * inverse
        row_one, row_two = work[g0][j - base : j - base + 1], work[g0][j - base + 1 : j - base + 2]
        for k in range(j + 2, BLK):
            skip = 8 * (k // 8 - g0)
            cols[k] = cols[k] - (
                lead_one[skip:] * one[k - base : k - base + 1] + lead_two[skip:] * two[k - base : k - base + 1]
            )
        for g in range(g0, groups):
            part = slice(8 * (g - g0), 8 * (g - g0) + 8)
            work[g] = work[g] - (lead_one[part] * row_one + lead_two[part] * row_two)
        first_root = inverse_root(first)
        ratio = cross * (first_root * first_root)
        work[g0] = work[g0] - jnp.where(row8 == j - base + 1, ratio, 0.0) * row_one
        scale[g0] = jnp.where(row8 == j - base, first_root, scale[g0])
        scale[g0] = jnp.where(row8 == j - base + 1, first * first_root * root, scale[g0])
    return jnp.concatenate([work[g] * scale[g] for g in range(groups)], axis=0)


def factor_panel(work, upper_out):
    per_tile = 128 // BLK
    row = lax.broadcasted_iota(jnp.int32, (BLK, PW), 0)
    lane = lax.broadcasted_iota(jnp.int32, (BLK, PW), 1)
    all_lane = lax.broadcasted_iota(jnp.int32, (PW, PW), 1)

    def step(b, carry):
        low = pl.multiple_of(b * BLK, BLK)
        tile = pl.multiple_of((b // per_tile) * 128, 128)
        shift = (b % per_tile) * BLK
        block = pltpu.roll(work[pl.ds(low, BLK), pl.ds(tile, 128)], (128 - shift) % 128, 1)
        done = factor_diagonal(block)
        inverse = pltpu.roll(done, 128 - BLK, 1)[:, :BLK]
        inside = (lane >= low) & (lane < low + BLK)
        lines = jnp.where(inside, jnp.where(lane == row + low, 1.0, 0.0), work[pl.ds(low, BLK), :])
        upper = exact(inverse, lines)
        placed = pltpu.roll(done, shift, 1)
        corner = jnp.concatenate([placed] * (PW // 128), axis=1)
        upper_out[pl.ds(low, BLK), :] = jnp.where(inside, corner, upper)
        lead = jnp.where(lane >= low + BLK, upper, 0.0)
        kept = jnp.where((all_lane >= low) & (all_lane < low + BLK), 0.0, work[...])
        work[...] = kept - exact(lead, upper, TN)
        work[pl.ds(low, BLK), :] = upper
        return carry

    lax.fori_loop(0, PW // BLK, step, 0)


def diagonals(value):
    row = lax.broadcasted_iota(jnp.int32, (PW, PW), 0)
    col = lax.broadcasted_iota(jnp.int32, (PW, PW), 1)
    kept = jnp.where(row == col, value, 0.0)
    return jnp.sum(kept, axis=1, keepdims=True), jnp.sum(kept, axis=0, keepdims=True)


def start_panel(work, diag_col, diag_row, value):
    by_row, by_col = diagonals(value)
    diag_col[...] = jnp.broadcast_to(by_row, (PW, 128))
    diag_row[...] = jnp.broadcast_to(by_col, (8, PW))
    work[...] = value / jnp.sqrt(by_row) / jnp.sqrt(by_col)


def pivot_values(table, stride, share, along_rows):
    shape = (NPIV, 1) if along_rows else (1, NPIV)
    block = lax.broadcasted_iota(jnp.int32, shape, 0 if along_rows else 1) % PW // share
    values = jnp.zeros(shape, F32)
    for r in range(PW // share):
        values = jnp.where(block == r, table[r * stride], values)
    return values


def tile_values(table, start, count):
    return jnp.concatenate([jnp.full((1, TS), table[start + i], F32) for i in range(count)], axis=1)


def finish_panel(work, upper, diag_col, diag_row, lower, inv_hi, inv_lo, inv_t_hi, inv_t_lo):
    row = lax.broadcasted_iota(jnp.int32, (PW, PW), 0)
    col = lax.broadcasted_iota(jnp.int32, (PW, PW), 1)
    lower[:PW, :] = jnp.where(col <= row, upper[...].T, 0.0) * jnp.sqrt(diag_col[:, :1])
    inverse = jnp.where(col <= row, work[...], 0.0) / jnp.sqrt(diag_row[:1, :])
    inv_hi[...], inv_lo[...] = split(inverse)
    inv_t_hi[...], inv_t_lo[...] = split(inverse.T)
    return inverse


def first_kernel(sizes, place, group_of, kid_of, near, far,
                 lower, inv_hi, inv_lo, inv_t_hi, inv_t_lo, link_out, link_t, rest, piv_t, piv,
                 pile, wide, work, upper, diag_col, diag_row):
    cols, fan, share, held, tiles = sizes
    my_row, my_col = place[0], place[1]
    my_q, my_a = my_row % fan, my_row // fan
    col_share = PW // cols
    for dq, source in enumerate((near, far)):
        for d in range(cols):
            r = (my_a ^ d) * fan + (my_q ^ dq)
            pieces = [source[c ^ my_col, d, :held, :] for c in range(cols)]
            line = jnp.concatenate(
                [piece[:, k * col_share : (k + 1) * col_share] for k in range(NP) for piece in pieces],
                axis=1,
            )
            kids = []
            for e in range(cols):
                packed = source[e, d, held:, :]
                kids += [packed[:, :held], packed[:, held:]]
            kids = jnp.concatenate(kids, axis=0).T
            for k in range(NP):
                at = pl.ds(pl.multiple_of(k * PW + r * share, share), share)
                pile[at, :] = line[k * share : (k + 1) * share]
                wide[at, :] = kids[k * share : (k + 1) * share]
    piv[...] = wide[...].astype(BF16)
    piv_t[...] = wide[...].T.astype(BF16)
    product = dot(piv[...], piv_t[...])
    same_group = pivot_values(group_of, tiles, share, True) == pivot_values(group_of, tiles, share, False)
    same_kid = pivot_values(kid_of, tiles, share, True) == pivot_values(kid_of, tiles, share, False)
    pile[...] = jnp.where(same_group, pile[...], 0.0) + jnp.where(same_kid, product, 0.0)
    start_panel(work, diag_col, diag_row, pile[:PW, :PW])
    factor_panel(work, upper)
    inverse = finish_panel(work, upper, diag_col, diag_row, lower, inv_hi, inv_lo, inv_t_hi, inv_t_lo)
    link = exact(pile[PW:, :PW], inverse, NT).astype(BF16)
    link_out[...] = link
    lower[PW:, :] = link.astype(F32)
    link_t[...] = link.astype(F32).T.astype(BF16)
    rest[...] = pile[PW:, PW:] - dot(link, link, NT)


def second_kernel(rest, lower, inv_hi, inv_lo, inv_t_hi, inv_t_lo, work, upper, diag_col, diag_row):
    start_panel(work, diag_col, diag_row, rest[...])
    factor_panel(work, upper)
    finish_panel(work, upper, diag_col, diag_row, lower, inv_hi, inv_lo, inv_t_hi, inv_t_lo)


def place_kernel(sizes, place, inverse_map, held, *outs):
    cols, fan, tiles, slice_cols = sizes
    my_row, my_col = place[0], place[1]
    my_q = my_row % fan

    def fetch(block, i):
        tile = inverse_map[block * tiles + i]
        at = pl.multiple_of((tile % tiles) * TS, TS)
        return held[tile // tiles, :, pl.ds(at, TS)]

    for i in range(tiles):
        mine = fetch(my_row, i)
        for d in range(cols):
            outs[d][:slice_cols, i * TS : (i + 1) * TS] = mine
    for d in range(cols):
        for i in range(tiles):
            outs[d][slice_cols:, i * TS : (i + 1) * TS] = fetch((my_col ^ d) * fan + my_q, i)


def together(*parts):
    parts = list(parts)
    while parts:
        for part in list(parts):
            try:
                next(part)
            except StopIteration:
                parts.remove(part)


def col_kernel(sizes, place, group_of, kid_of, strips, near_kids, far_kids,
               piv, inv1_hi, inv1_lo, inv2_hi, inv2_lo, link, out, strip, kids):
    rows, fan, share, block_cols, local_rows, tiles, wide = sizes
    my_row, my_col = place[0], place[1]
    my_q = my_row % fan
    j = pl.program_id(0)
    q = (j * block_cols) // local_rows
    group_col = pivot_values(group_of, tiles, share, True)
    kid_col = pivot_values(kid_of, tiles, share, True)

    @pl.when(q == my_q)
    def _():
        kids[...] = near_kids[...]

    @pl.when(q != my_q)
    def _():
        kids[...] = far_kids[...]

    def col_solve(n, pile):
        at = slice(n * wide, (n + 1) * wide)
        for r in range(rows):
            piece = strips[r, :, at].astype(F32)
            for k in range(NP):
                low = k * PW + r * share
                pile[low : low + share, :] = piece[k * share : (k + 1) * share]
        tile = my_col * fan * tiles + (j * block_cols + n * wide) // TS
        group_all = tile_values(group_of, tile, wide // TS)
        kid_all = tile_values(kid_of, tile, wide // TS)
        product = dot(piv[...], kids[:, at])
        yield
        full = jnp.where(group_col == group_all, pile[...], 0.0) + jnp.where(
            kid_col == kid_all, product, 0.0
        )
        first, second = full[:PW].astype(BF16), full[PW:]
        yield
        both = dot(jnp.concatenate([inv1_hi[...], inv1_lo[...]], axis=0), first)
        yield
        head = (both[:PW] + both[PW:]).astype(BF16)
        out[:PW, at] = -head
        yield
        second = (second - dot(link[...], head)).astype(BF16)
        yield
        both = dot(jnp.concatenate([inv2_hi[...], inv2_lo[...]], axis=0), second)
        yield
        out[PW:, at] = (-(both[:PW] + both[PW:])).astype(BF16)

    together(*[col_solve(n, strip.at[n]) for n in range(block_cols // wide)])


def schur_kernel(sizes, masks, place, group_of, kid_of,
                 piv_t, lower1, lower2, inv1_t_hi, inv1_t_lo, inv2_t_hi, inv2_t_lo, link_t, *refs):
    cols, fan, share, held, slice_cols, block_rows, local_rows, local_cols, tiles = sizes
    front, solved_cols, near_kids, far_kids = refs[:4]
    sources = refs[4 : 4 + cols]
    quarters = refs[4 + cols : 12 + cols]
    out, panel = refs[12 + cols : 14 + cols]
    (fronts, outs, kids, own_t, pieces, flipped, solved_even, solved_odd, own_even, own_odd,
     front_sems, out_sems, flip_sem, kid_sems, own_sems, piece_sems) = refs[14 + cols :]
    my_row, my_col = place[0], place[1]
    my_q = my_row % fan
    first_tile = my_col * fan * tiles
    steps = local_rows // block_rows
    depth = fronts.shape[0] // 2
    quarter_rows = local_rows // 4

    def rows_at(i):
        return pl.ds(pl.multiple_of(i * block_rows, block_rows), block_rows)

    def front_copy(i, slot):
        return pltpu.make_async_copy(front.at[rows_at(i), :], fronts.at[slot], front_sems.at[slot])

    def out_copy(i, slot):
        return pltpu.make_async_copy(outs.at[slot], out.at[rows_at(i), :], out_sems.at[slot])

    kid_copies = [
        pltpu.make_async_copy(
            source,
            kids.at[:, pl.ds(pl.multiple_of((my_q ^ q) * local_rows, local_rows), local_rows)],
            kid_sems.at[q],
        )
        for q, source in enumerate((near_kids, far_kids))
    ]
    flip_copy = pltpu.make_async_copy(solved_cols, flipped, flip_sem)
    own_copies = [
        pltpu.make_async_copy(
            source.at[:slice_cols, :], own_t.at[d * slice_cols : (d + 1) * slice_cols, :], own_sems.at[d]
        )
        for d, source in enumerate(sources)
    ]
    piece_copies = [
        pltpu.make_async_copy(
            quarters[2 * quarter + i // (cols // 2)].at[i % (cols // 2)],
            pieces.at[my_col ^ mask, quarter * quarter_rows : (quarter + 1) * quarter_rows, :],
            piece_sems.at[quarter * cols + i],
        )
        for quarter in range(4)
        for i, mask in enumerate(masks[quarter // 2])
    ]
    for copy in own_copies + piece_copies + [flip_copy] + kid_copies:
        copy.start()
    for i in range(2 * depth):
        front_copy(i, i).start()
    for copy in own_copies + piece_copies:
        copy.wait()
    col_share = PW // cols
    subs = block_rows // TS
    per_tile = 128 // col_share
    span = min(512, local_cols)
    group_row = pivot_values(group_of, tiles, share, False)
    kid_row = pivot_values(kid_of, tiles, share, False)
    lane = lax.broadcasted_iota(jnp.int32, (block_rows, 128), 1)

    def row_solve(step, opening, own_ref, solved):
        own = own_t[:, rows_at(step)].astype(F32).T.astype(BF16)
        own_ref[...] = own
        product = dot(own, piv_t[...])
        yield
        entries = jnp.concatenate(
            [
                pieces[c, rows_at(step), k * col_share : (k + 1) * col_share]
                for k in range(NP)
                for c in range(cols)
            ],
            axis=1,
        )
        my_tile = my_row * tiles + step * subs
        parts = []
        for i in range(subs):
            part = slice(i * TS, (i + 1) * TS)
            parts.append(
                jnp.where(group_row == group_of[my_tile + i], entries[part], 0.0)
                + jnp.where(kid_row == kid_of[my_tile + i], product[part], 0.0)
            )
        full = jnp.concatenate(parts, axis=0)
        high, low = split(full[:, :PW])
        yield
        head = dot(high, inv1_t_hi[...]) + dot(high, inv1_t_lo[...]) + dot(low, inv1_t_hi[...])
        solved[:, :PW] = head
        yield
        high, low = split(full[:, PW:] - dot(head.astype(BF16), link_t[...]))
        yield
        solved[:, PW:] = dot(high, inv2_t_hi[...]) + dot(high, inv2_t_lo[...]) + dot(low, inv2_t_hi[...])
        yield
        if opening:
            at = pl.multiple_of(my_row * share, share)
            solved[:share, :PW] = lower1[pl.ds(at, share), :]
            solved[:share, PW:] = jnp.zeros((share, PW), F32)
            solved[share : 2 * share, :PW] = lower1[pl.ds(PW + at, share), :]
            solved[share : 2 * share, PW:] = lower2[pl.ds(at, share), :]
        moved_out = jnp.zeros((block_rows, 128), F32)
        for k in range(NP):
            tile = pl.multiple_of(k * PW + (my_col // per_tile) * 128, 128)
            turn = (128 + k * col_share - (my_col % per_tile) * col_share) % 128
            moved = pltpu.roll(solved[:, pl.ds(tile, 128)], turn, 1)
            moved_out = jnp.where(lane // col_share == k, moved, moved_out)
        panel[rows_at(step), :] = moved_out[:, : NP * col_share].astype(BF16)

    def update(step, slot, own_ref, solved):
        lead, own = solved[...].astype(BF16), own_ref[...]
        my_tile = my_row * tiles + step * subs
        for n in range(local_cols // span):
            at = slice(n * span, (n + 1) * span)
            change = dot(lead, flipped[:, at])
            product = dot(own, kids[:, at])
            group_all = tile_values(group_of, first_tile + n * (span // TS), span // TS)
            kid_all = tile_values(kid_of, first_tile + n * (span // TS), span // TS)
            for i in range(subs):
                part = slice(i * TS, (i + 1) * TS)
                outs[slot, part, at] = (
                    jnp.where(group_all == group_of[my_tile + i], fronts[slot, part, at], 0.0)
                    + jnp.where(kid_all == kid_of[my_tile + i], product[part], 0.0)
                    + change[part]
                )
            yield

    together(row_solve(0, True, own_even, solved_even))
    for copy in [flip_copy] + kid_copies:
        copy.wait()

    def two_blocks(pair, carry):
        for odd in range(2):
            step = 2 * pair + odd
            slot = 2 * lax.rem(pair, depth) + odd
            front_copy(step, slot).wait()

            @pl.when(pair >= depth)
            def _():
                out_copy(step - 2 * depth, slot).wait()

            if odd:
                mine, later = (own_odd, solved_odd), (own_even, solved_even)
            else:
                mine, later = (own_even, solved_even), (own_odd, solved_odd)
            together(update(step, slot, *mine), row_solve(jnp.minimum(step + 1, steps - 1), False, *later))
            for q in range(fan):
                outs[slot, :, q * local_rows : q * local_rows + held] = jnp.zeros((block_rows, held), F32)
            if not odd:

                @pl.when(pair == 0)
                def _():
                    outs[slot, :held, :] = jnp.zeros((held, local_cols), F32)

            out_copy(step, slot).start()

            @pl.when(pair + depth < steps // 2)
            def _():
                front_copy(step + 2 * depth, slot).start()

        return carry

    lax.fori_loop(0, steps // 2, two_blocks, 0)
    for i in range(steps - 2 * depth, steps):
        out_copy(i, i % (2 * depth)).wait()


def params():
    return pltpu.CompilerParams(vmem_limit_bytes=VMEM_BYTES)


def local(front_entries, tile_group, child_factor, row_map):
    rows, cols = lax.axis_size("row"), lax.axis_size("col")
    fan = rows // cols
    assert fan == 2
    local_rows, local_cols = front_entries.shape
    slice_cols = child_factor.shape[1]
    kid_cols = slice_cols * cols
    tiles = local_rows // TS
    share = PW // rows
    held = NP * share
    my_row, my_col = lax.axis_index("row"), lax.axis_index("col")
    place = jnp.stack([my_row, my_col]).astype(jnp.int32)

    flipped = child_factor.T
    own_map = lax.dynamic_slice_in_dim(row_map, my_row * tiles, tiles)
    starts = flipped.reshape(slice_cols, tiles, TS)[:, :, :held]

    def chosen(block):
        keep = (own_map == block * tiles)[None, :, None]
        return jnp.sum(jnp.where(keep, starts, 0), axis=1, dtype=F32)

    corner = jnp.concatenate(
        [
            front_entries[:held, q * local_rows + k * share : q * local_rows + (k + 1) * share]
            for k in range(NP)
            for q in range(fan)
        ],
        axis=1,
    )
    kids = jnp.concatenate([chosen(my_row), chosen(jnp.bitwise_xor(my_row, rows // 2))], axis=1)
    packet = jnp.concatenate([corner, kids], axis=0)
    packets = [swapped(packet, "row", d * fan) for d in range(cols)]

    row_strip = jnp.concatenate(
        [
            front_entries[:, q * local_rows + k * share : q * local_rows + (k + 1) * share]
            for k in range(NP)
            for q in range(fan)
        ],
        axis=1,
    )
    gathered = lax.all_gather(flipped, "row", axis=0)
    col_strip, row_strip, *packets = lax.optimization_barrier(
        (front_entries[:held].astype(BF16), row_strip, *packets)
    )
    col_strips = lax.all_gather(col_strip, "row", axis=0)
    steps = [1 << i for i in range(cols.bit_length() - 1)]
    orders = [steps, steps[::-1]]
    halves = [row_strip[None, : local_rows // 2], row_strip[None, local_rows // 2 :]]
    masks = [[0], [0]]
    for h in range(2):
        for step in orders[h][:-2]:
            halves[h] = jnp.concatenate([halves[h], swapped(halves[h], "col", step)], axis=0)
            masks[h] = masks[h] + [m ^ step for m in masks[h]]
    others = [swapped(halves[h], "col", orders[h][-2]) for h in range(2)]
    masks = [masks[h] + [m ^ orders[h][-2] for m in masks[h]] for h in range(2)]
    merged = []
    for d in range(cols):
        kid = packets[d][held:, :held] + packets[d ^ (cols // 2)][held:, held:]
        half = slice_cols // 2
        merged.append(
            jnp.concatenate(
                [packets[d][:held], jnp.concatenate([kid[:half], kid[half:]], axis=1)], axis=0
            )
        )
    merged = jnp.stack(merged)
    near = jnp.stack([swapped(merged, "col", d) for d in range(cols)])
    far = swapped(near, "row", 1)

    tile_ids = jnp.arange(row_map.shape[0], dtype=jnp.int32)
    inverse_map = jnp.sum(
        jnp.where(row_map[None, :] == tile_ids[:, None], tile_ids[None, :], 0), axis=1, dtype=jnp.int32
    )
    kid_of = (inverse_map >= row_map.shape[0] // 2).astype(F32)
    group_of = jnp.repeat(tile_group, MT // TS).astype(F32)

    placed = pl.pallas_call(
        functools.partial(place_kernel, (cols, fan, tiles, slice_cols)),
        out_shape=[jax.ShapeDtypeStruct((2 * slice_cols, local_rows), BF16)] * cols,
        in_specs=[smem_spec()] * 2 + [whole_spec()],
        out_specs=[whole_spec()] * cols,
        compiler_params=params(),
        cost_estimate=pl.CostEstimate(flops=0, bytes_accessed=2**16, transcendentals=0),
        name="place_tiles",
    )(place, inverse_map, gathered)
    near, far, *placed = lax.optimization_barrier((near, far, *placed))
    kid_parts = [swapped(placed[d], "col", d) for d in range(cols)]

    middle = local_rows // 4

    def joined(part):
        return [
            jnp.concatenate([value[h][:, part * middle : (part + 1) * middle] for value in (halves, others)])
            for h in range(2)
        ]

    def last_step(value):
        return [swapped(value[h], "col", orders[h][-1]) for h in range(2)]

    early = joined(0)
    early_far = last_step(early)
    masks = [masks[h] + [m ^ orders[h][-1] for m in masks[h]] for h in range(2)]

    square = jax.ShapeDtypeStruct((PW, PW), BF16)
    pivot_scratch = [
        pltpu.VMEM((PW, PW), F32),
        pltpu.VMEM((PW, PW), F32),
        pltpu.VMEM((PW, 128), F32),
        pltpu.VMEM((8, PW), F32),
    ]
    pivot_cost = pl.CostEstimate(flops=2 * 10**10, bytes_accessed=5 * 10**7, transcendentals=0)
    lower1, inv1_hi, inv1_lo, inv1_t_hi, inv1_t_lo, link, link_t, rest, piv_t, piv = pl.pallas_call(
        functools.partial(first_kernel, (cols, fan, share, held, tiles)),
        out_shape=[
            jax.ShapeDtypeStruct((2 * PW, PW), F32),
            square, square, square, square, square, square,
            jax.ShapeDtypeStruct((PW, PW), F32),
            jax.ShapeDtypeStruct((kid_cols, NPIV), BF16),
            jax.ShapeDtypeStruct((NPIV, kid_cols), BF16),
        ],
        in_specs=[smem_spec()] * 3 + [whole_spec()] * 2,
        out_specs=[whole_spec()] * 10,
        scratch_shapes=[pltpu.VMEM((NPIV, NPIV), F32), pltpu.VMEM((NPIV, kid_cols), F32)] + pivot_scratch,
        compiler_params=params(),
        cost_estimate=pl.CostEstimate(flops=4*10**9, bytes_accessed=10**6, transcendentals=0),
        name="first_pivots",
    )(place, group_of, kid_of, near, far)
    rest, *early_far = lax.optimization_barrier((rest, *early_far))
    lower2, inv2_hi, inv2_lo, inv2_t_hi, inv2_t_lo = pl.pallas_call(
        second_kernel,
        out_shape=[jax.ShapeDtypeStruct((PW, PW), F32), square, square, square, square],
        in_specs=[whole_spec()],
        out_specs=[whole_spec()] * 5,
        scratch_shapes=pivot_scratch,
        compiler_params=params(),
        cost_estimate=pivot_cost,
        name="second_pivots",
    )(rest)

    lower2, kid_parts, *others = lax.optimization_barrier((lower2, kid_parts, *others))
    near_kids = jnp.concatenate([part[slice_cols:] for part in kid_parts], axis=0)
    far_kids = swapped(near_kids, "row", 1)
    late = joined(1)
    late_far = last_step(late)

    block_cols = min(1024, local_rows)
    per_block = local_rows // block_cols
    wide = min(512, block_cols)
    solved_cols = pl.pallas_call(
        functools.partial(col_kernel, (rows, fan, share, block_cols, local_rows, tiles, wide)),
        grid=(local_cols // block_cols,),
        out_shape=jax.ShapeDtypeStruct((NPIV, local_cols), BF16),
        in_specs=[smem_spec()] * 3
        + [
            pl.BlockSpec((rows, held, block_cols), lambda j: (0, 0, j)),
            pl.BlockSpec((kid_cols, block_cols), lambda j: (0, j % per_block)),
            pl.BlockSpec((kid_cols, block_cols), lambda j: (0, j % per_block)),
        ]
        + [whole_spec()] * 6,
        out_specs=pl.BlockSpec((NPIV, block_cols), lambda j: (0, j)),
        scratch_shapes=[
            pltpu.VMEM((block_cols // wide, NPIV, wide), F32),
            pltpu.VMEM((kid_cols, block_cols), BF16),
        ],
        compiler_params=params(),
        cost_estimate=pl.CostEstimate(flops=10**10, bytes_accessed=3 * 10**7, transcendentals=0),
        name="col_factors",
    )(
        place, group_of, kid_of, col_strips, near_kids, far_kids,
        piv, inv1_hi, inv1_lo, inv2_hi, inv2_lo, link,
    )

    block_rows = min(256, local_rows)
    depth = min(2, local_rows // block_rows // 2)
    solved_cols, *late_far = lax.optimization_barrier((solved_cols, *late_far))
    schur_block, factor_panels = pl.pallas_call(
        functools.partial(
            schur_kernel,
            (cols, fan, share, held, slice_cols, block_rows, local_rows, local_cols, tiles),
            masks,
        ),
        out_shape=[
            jax.ShapeDtypeStruct((local_rows, local_cols), F32),
            jax.ShapeDtypeStruct((local_rows, NP * PW // cols), BF16),
        ],
        in_specs=[smem_spec()] * 3 + [whole_spec()] * 8 + [any_spec()] * (12 + cols),
        out_specs=[any_spec(), whole_spec()],
        scratch_shapes=[
            pltpu.VMEM((2 * depth, block_rows, local_cols), F32),
            pltpu.VMEM((2 * depth, block_rows, local_cols), F32),
            pltpu.VMEM((kid_cols, local_cols), BF16),
            pltpu.VMEM((kid_cols, local_rows), BF16),
            pltpu.VMEM((cols, local_rows, fan * held), F32),
            pltpu.VMEM((NPIV, local_cols), BF16),
            pltpu.VMEM((block_rows, NPIV), F32),
            pltpu.VMEM((block_rows, NPIV), F32),
            pltpu.VMEM((block_rows, kid_cols), BF16),
            pltpu.VMEM((block_rows, kid_cols), BF16),
            pltpu.SemaphoreType.DMA((2 * depth,)),
            pltpu.SemaphoreType.DMA((2 * depth,)),
            pltpu.SemaphoreType.DMA,
            pltpu.SemaphoreType.DMA((fan,)),
            pltpu.SemaphoreType.DMA((cols,)),
            pltpu.SemaphoreType.DMA((4 * cols,)),
        ],
        compiler_params=params(),
        cost_estimate=pl.CostEstimate(flops=3 * 10**10, bytes_accessed=9 * 10**7, transcendentals=0),
        name="schur_update",
    )(
        place, group_of, kid_of, piv_t, lower1, lower2,
        inv1_t_hi, inv1_t_lo, inv2_t_hi, inv2_t_lo, link_t,
        front_entries, solved_cols, near_kids, far_kids, *kid_parts,
        early[0], early_far[0], late[0], late_far[0], early[1], early_far[1], late[1], late_far[1],
    )
    return (factor_panels, schur_block)


def solution(mesh):
    placed = (P("row", "col"), P(), P("row", "col"), P())
    return jax.shard_map(
        local,
        mesh=mesh,
        in_specs=placed,
        out_specs=(P("row", "col"), P("row", "col")),
        check_vma=False,
    )
```

```python
import functools

import jax
import jax.numpy as jnp
from jax import lax
from jax.experimental import pallas as pl
from jax.experimental.pallas import tpu as pltpu
from jax.sharding import PartitionSpec as P

PW = 256
NP = 2
TS = 128
MT = 512
NPIV = NP * PW
BLK = 32
F32 = jnp.float32
BF16 = jnp.bfloat16
VMEM_BYTES = 60 * 1024 * 1024

NN = (((1,), (0,)), ((), ()))
NT = (((1,), (1,)), ((), ()))
TN = (((0,), (0,)), ((), ()))


def dot(left, right, dims=NN, precision=None):
    return lax.dot_general(left, right, dims, precision=precision, preferred_element_type=F32)


def exact(left, right, dims=NN):
    return dot(left, right, dims, lax.Precision.HIGHEST)


def split(value):
    high = value.astype(BF16)
    return high, (value - high.astype(F32)).astype(BF16)


def swapped(value, axis, mask):
    if mask == 0:
        return value
    return lax.ppermute(value, axis, [(i, i ^ mask) for i in range(lax.axis_size(axis))])


def whole_spec():
    return pl.BlockSpec(memory_space=pltpu.VMEM)


def any_spec():
    return pl.BlockSpec(memory_space=pl.ANY)


def smem_spec():
    return pl.BlockSpec(memory_space=pltpu.SMEM)


def factor_diagonal(block):
    groups = BLK // 8
    lane = lax.broadcasted_iota(jnp.int32, (BLK, 128), 1)
    row = lax.broadcasted_iota(jnp.int32, (BLK, 128), 0)
    row8 = lax.broadcasted_iota(jnp.int32, (8, 128), 0)
    start = jnp.where(lane < BLK, block, jnp.where(lane == row + BLK, 1.0, 0.0))
    work = [start[8 * g : 8 * g + 8] for g in range(groups)]
    cols = []
    for k in range(BLK):
        base = 8 * (k // 8)
        cols.append(jnp.broadcast_to(block[base:, k : k + 1], (BLK - base, 128)))
    scale = [jnp.ones((8, 128), F32) for _ in range(groups)]

    def inverse_root(value):
        root = lax.rsqrt(value)
        return root * (1.5 - 0.5 * value * root * root)

    for j in range(0, BLK, 2):
        g0 = j // 8
        base = 8 * g0
        one, two = cols[j], cols[j + 1]
        first, cross, last = one[j - base : j - base + 1], one[j - base + 1 : j - base + 2], two[j - base + 1 : j - base + 2]
        volume = first * last - cross * cross
        root = inverse_root(volume)
        inverse = root * root
        below = row[base:] > j + 1
        lead_one = jnp.where(below, last * one - cross * two, 0.0) * inverse
        lead_two = jnp.where(below, first * two - cross * one, 0.0) * inverse
        row_one, row_two = work[g0][j - base : j - base + 1], work[g0][j - base + 1 : j - base + 2]
        for k in range(j + 2, BLK):
            skip = 8 * (k // 8 - g0)
            cols[k] = cols[k] - (
                lead_one[skip:] * one[k - base : k - base + 1] + lead_two[skip:] * two[k - base : k - base + 1]
            )
        for g in range(g0, groups):
            part = slice(8 * (g - g0), 8 * (g - g0) + 8)
            work[g] = work[g] - (lead_one[part] * row_one + lead_two[part] * row_two)
        first_root = inverse_root(first)
        ratio = cross * (first_root * first_root)
        work[g0] = work[g0] - jnp.where(row8 == j - base + 1, ratio, 0.0) * row_one
        scale[g0] = jnp.where(row8 == j - base, first_root, scale[g0])
        scale[g0] = jnp.where(row8 == j - base + 1, first * first_root * root, scale[g0])
    return jnp.concatenate([work[g] * scale[g] for g in range(groups)], axis=0)


def factor_panel(work, upper_out, start, stop):
    per_tile = 128 // BLK
    row = lax.broadcasted_iota(jnp.int32, (BLK, PW), 0)
    lane = lax.broadcasted_iota(jnp.int32, (BLK, PW), 1)
    all_lane = lax.broadcasted_iota(jnp.int32, (PW, PW), 1)

    def step(b, carry):
        low = pl.multiple_of(b * BLK, BLK)
        tile = pl.multiple_of((b // per_tile) * 128, 128)
        shift = (b % per_tile) * BLK
        block = pltpu.roll(work[pl.ds(low, BLK), pl.ds(tile, 128)], (128 - shift) % 128, 1)
        done = factor_diagonal(block)
        inverse = pltpu.roll(done, 128 - BLK, 1)[:, :BLK]
        inside = (lane >= low) & (lane < low + BLK)
        lines = jnp.where(inside, jnp.where(lane == row + low, 1.0, 0.0), work[pl.ds(low, BLK), :])
        upper = exact(inverse, lines)
        placed = pltpu.roll(done, shift, 1)
        corner = jnp.concatenate([placed] * (PW // 128), axis=1)
        upper_out[pl.ds(low, BLK), :] = jnp.where(inside, corner, upper)
        lead = jnp.where(lane >= low + BLK, upper, 0.0)
        kept = jnp.where((all_lane >= low) & (all_lane < low + BLK), 0.0, work[...])
        work[...] = kept - exact(lead, upper, TN)
        work[pl.ds(low, BLK), :] = upper
        return carry

    lax.fori_loop(start, stop, step, 0)


def diagonals(value):
    row = lax.broadcasted_iota(jnp.int32, (PW, PW), 0)
    col = lax.broadcasted_iota(jnp.int32, (PW, PW), 1)
    kept = jnp.where(row == col, value, 0.0)
    return jnp.sum(kept, axis=1, keepdims=True), jnp.sum(kept, axis=0, keepdims=True)


def start_panel(work, diag_col, diag_row, value):
    by_row, by_col = diagonals(value)
    diag_col[...] = jnp.broadcast_to(by_row, (PW, 128))
    diag_row[...] = jnp.broadcast_to(by_col, (8, PW))
    work[...] = value / jnp.sqrt(by_row) / jnp.sqrt(by_col)


def pivot_values(table, stride, share, along_rows):
    shape = (NPIV, 1) if along_rows else (1, NPIV)
    block = lax.broadcasted_iota(jnp.int32, shape, 0 if along_rows else 1) % PW // share
    values = jnp.zeros(shape, F32)
    for r in range(PW // share):
        values = jnp.where(block == r, table[r * stride], values)
    return values


def tile_values(table, start, count):
    return jnp.concatenate([jnp.full((1, TS), table[start + i], F32) for i in range(count)], axis=1)


def finish_panel(work, upper, diag_col, diag_row, lower, inv_hi, inv_lo, inv_t_hi, inv_t_lo):
    row = lax.broadcasted_iota(jnp.int32, (PW, PW), 0)
    col = lax.broadcasted_iota(jnp.int32, (PW, PW), 1)
    lower[:PW, :] = jnp.where(col <= row, upper[...].T, 0.0) * jnp.sqrt(diag_col[:, :1])
    inverse = jnp.where(col <= row, work[...], 0.0) / jnp.sqrt(diag_row[:1, :])
    inv_hi[...], inv_lo[...] = split(inverse)
    inv_t_hi[...], inv_t_lo[...] = split(inverse.T)
    return inverse


def open_kernel(sizes, place, group_of, kid_of, near, far,
                work, upper, diag_col, diag_row, low_rows, piv_t, piv, pile, wide):
    cols, fan, share, held, tiles = sizes
    my_row, my_col = place[0], place[1]
    my_q, my_a = my_row % fan, my_row // fan
    col_share = PW // cols
    for dq, source in enumerate((near, far)):
        for d in range(cols):
            r = (my_a ^ d) * fan + (my_q ^ dq)
            pieces = [source[c ^ my_col, d, :held, :] for c in range(cols)]
            line = jnp.concatenate(
                [piece[:, k * col_share : (k + 1) * col_share] for k in range(NP) for piece in pieces],
                axis=1,
            )
            kids = []
            for e in range(cols):
                packed = source[e, d, held:, :]
                kids += [packed[:, :held], packed[:, held:]]
            kids = jnp.concatenate(kids, axis=0).T
            for k in range(NP):
                at = pl.ds(pl.multiple_of(k * PW + r * share, share), share)
                pile[at, :] = line[k * share : (k + 1) * share]
                wide[at, :] = kids[k * share : (k + 1) * share]
    piv[...] = wide[...].astype(BF16)
    piv_t[...] = wide[...].T.astype(BF16)
    product = dot(piv[...], piv_t[...])
    same_group = pivot_values(group_of, tiles, share, True) == pivot_values(group_of, tiles, share, False)
    same_kid = pivot_values(kid_of, tiles, share, True) == pivot_values(kid_of, tiles, share, False)
    pile[...] = jnp.where(same_group, pile[...], 0.0) + jnp.where(same_kid, product, 0.0)
    low_rows[...] = pile[PW:, :]
    upper[...] = jnp.zeros_like(upper)
    start_panel(work, diag_col, diag_row, pile[:PW, :PW])
    factor_panel(work, upper, 0, PW // BLK // 2)


def first_kernel(begun, begun_upper, diag_col, diag_row, low_rows,
                 lower, inv_hi, inv_lo, inv_t_hi, inv_t_lo, link_out, link_t, rest, work, upper):
    work[...] = begun[...]
    upper[...] = begun_upper[...]
    factor_panel(work, upper, PW // BLK // 2, PW // BLK)
    inverse = finish_panel(work, upper, diag_col, diag_row, lower, inv_hi, inv_lo, inv_t_hi, inv_t_lo)
    link = exact(low_rows[:, :PW], inverse, NT).astype(BF16)
    link_out[...] = link
    lower[PW:, :] = link.astype(F32)
    link_t[...] = link.astype(F32).T.astype(BF16)
    rest[...] = low_rows[:, PW:] - dot(link, link, NT)


def second_kernel(rest, lower, inv_hi, inv_lo, inv_t_hi, inv_t_lo, work, upper, diag_col, diag_row):
    start_panel(work, diag_col, diag_row, rest[...])
    factor_panel(work, upper, 0, PW // BLK)
    finish_panel(work, upper, diag_col, diag_row, lower, inv_hi, inv_lo, inv_t_hi, inv_t_lo)


def place_kernel(sizes, place, inverse_map, held, *outs):
    cols, fan, tiles, slice_cols = sizes
    my_row, my_col = place[0], place[1]
    my_q = my_row % fan

    def fetch(block, i):
        tile = inverse_map[block * tiles + i]
        at = pl.multiple_of((tile % tiles) * TS, TS)
        return held[tile // tiles, :, pl.ds(at, TS)]

    for i in range(tiles):
        mine = fetch(my_row, i)
        for d in range(cols):
            outs[d][:slice_cols, i * TS : (i + 1) * TS] = mine
    for d in range(cols):
        for i in range(tiles):
            outs[d][slice_cols:, i * TS : (i + 1) * TS] = fetch((my_col ^ d) * fan + my_q, i)


def together(*parts):
    parts = list(parts)
    while parts:
        for part in list(parts):
            try:
                next(part)
            except StopIteration:
                parts.remove(part)


def col_kernel(sizes, place, group_of, kid_of, strips, near_kids, far_kids,
               piv, inv1_hi, inv1_lo, inv2_hi, inv2_lo, link, out, strip, kids):
    rows, fan, share, block_cols, local_rows, tiles, wide = sizes
    my_row, my_col = place[0], place[1]
    my_q = my_row % fan
    j = pl.program_id(0)
    q = (j * block_cols) // local_rows
    group_col = pivot_values(group_of, tiles, share, True)
    kid_col = pivot_values(kid_of, tiles, share, True)

    @pl.when(q == my_q)
    def _():
        kids[...] = near_kids[...]

    @pl.when(q != my_q)
    def _():
        kids[...] = far_kids[...]

    def col_solve(n, pile):
        at = slice(n * wide, (n + 1) * wide)
        for r in range(rows):
            piece = strips[r, :, at].astype(F32)
            for k in range(NP):
                low = k * PW + r * share
                pile[low : low + share, :] = piece[k * share : (k + 1) * share]
        tile = my_col * fan * tiles + (j * block_cols + n * wide) // TS
        group_all = tile_values(group_of, tile, wide // TS)
        kid_all = tile_values(kid_of, tile, wide // TS)
        product = dot(piv[...], kids[:, at])
        yield
        full = jnp.where(group_col == group_all, pile[...], 0.0) + jnp.where(
            kid_col == kid_all, product, 0.0
        )
        first, second = full[:PW].astype(BF16), full[PW:]
        yield
        both = dot(jnp.concatenate([inv1_hi[...], inv1_lo[...]], axis=0), first)
        yield
        head = (both[:PW] + both[PW:]).astype(BF16)
        out[:PW, at] = -head
        yield
        second = (second - dot(link[...], head)).astype(BF16)
        yield
        both = dot(jnp.concatenate([inv2_hi[...], inv2_lo[...]], axis=0), second)
        yield
        out[PW:, at] = (-(both[:PW] + both[PW:])).astype(BF16)

    together(*[col_solve(n, strip.at[n]) for n in range(block_cols // wide)])


def schur_kernel(sizes, masks, place, group_of, kid_of,
                 piv_t, lower1, lower2, inv1_t_hi, inv1_t_lo, inv2_t_hi, inv2_t_lo, link_t, *refs):
    cols, fan, share, held, slice_cols, block_rows, local_rows, local_cols, tiles = sizes
    front, solved_cols, near_kids, far_kids = refs[:4]
    sources = refs[4 : 4 + cols]
    quarters = refs[4 + cols : 12 + cols]
    out, panel = refs[12 + cols : 14 + cols]
    (fronts, outs, kids, own_t, pieces, flipped, solved_even, solved_odd, own_even, own_odd,
     front_sems, out_sems, flip_sem, kid_sems, own_sems, piece_sems) = refs[14 + cols :]
    my_row, my_col = place[0], place[1]
    my_q = my_row % fan
    first_tile = my_col * fan * tiles
    steps = local_rows // block_rows
    depth = fronts.shape[0] // 2
    quarter_rows = local_rows // 4

    def rows_at(i):
        return pl.ds(pl.multiple_of(i * block_rows, block_rows), block_rows)

    def front_copy(i, slot):
        return pltpu.make_async_copy(front.at[rows_at(i), :], fronts.at[slot], front_sems.at[slot])

    def out_copy(i, slot):
        return pltpu.make_async_copy(outs.at[slot], out.at[rows_at(i), :], out_sems.at[slot])

    kid_copies = [
        pltpu.make_async_copy(
            source,
            kids.at[:, pl.ds(pl.multiple_of((my_q ^ q) * local_rows, local_rows), local_rows)],
            kid_sems.at[q],
        )
        for q, source in enumerate((near_kids, far_kids))
    ]
    flip_copy = pltpu.make_async_copy(solved_cols, flipped, flip_sem)
    own_copies = [
        pltpu.make_async_copy(
            source.at[:slice_cols, :], own_t.at[d * slice_cols : (d + 1) * slice_cols, :], own_sems.at[d]
        )
        for d, source in enumerate(sources)
    ]
    piece_copies = [
        pltpu.make_async_copy(
            quarters[2 * quarter + i // (cols // 2)].at[i % (cols // 2)],
            pieces.at[my_col ^ mask, quarter * quarter_rows : (quarter + 1) * quarter_rows, :],
            piece_sems.at[quarter * cols + i],
        )
        for quarter in range(4)
        for i, mask in enumerate(masks[quarter // 2])
    ]
    for copy in own_copies + piece_copies + [flip_copy] + kid_copies:
        copy.start()
    for i in range(2 * depth):
        front_copy(i, i).start()
    for copy in own_copies + piece_copies:
        copy.wait()
    col_share = PW // cols
    subs = block_rows // TS
    per_tile = 128 // col_share
    span = min(512, local_cols)
    group_row = pivot_values(group_of, tiles, share, False)
    kid_row = pivot_values(kid_of, tiles, share, False)
    lane = lax.broadcasted_iota(jnp.int32, (block_rows, 128), 1)

    def row_solve(step, opening, own_ref, solved):
        own = own_t[:, rows_at(step)].astype(F32).T.astype(BF16)
        own_ref[...] = own
        product = dot(own, piv_t[...])
        yield
        entries = jnp.concatenate(
            [
                pieces[c, rows_at(step), k * col_share : (k + 1) * col_share]
                for k in range(NP)
                for c in range(cols)
            ],
            axis=1,
        )
        my_tile = my_row * tiles + step * subs
        parts = []
        for i in range(subs):
            part = slice(i * TS, (i + 1) * TS)
            parts.append(
                jnp.where(group_row == group_of[my_tile + i], entries[part], 0.0)
                + jnp.where(kid_row == kid_of[my_tile + i], product[part], 0.0)
            )
        full = jnp.concatenate(parts, axis=0)
        high, low = split(full[:, :PW])
        yield
        head = dot(high, inv1_t_hi[...]) + dot(high, inv1_t_lo[...]) + dot(low, inv1_t_hi[...])
        solved[:, :PW] = head
        yield
        high, low = split(full[:, PW:] - dot(head.astype(BF16), link_t[...]))
        yield
        solved[:, PW:] = dot(high, inv2_t_hi[...]) + dot(high, inv2_t_lo[...]) + dot(low, inv2_t_hi[...])
        yield
        if opening:
            at = pl.multiple_of(my_row * share, share)
            solved[:share, :PW] = lower1[pl.ds(at, share), :]
            solved[:share, PW:] = jnp.zeros((share, PW), F32)
            solved[share : 2 * share, :PW] = lower1[pl.ds(PW + at, share), :]
            solved[share : 2 * share, PW:] = lower2[pl.ds(at, share), :]
        moved_out = jnp.zeros((block_rows, 128), F32)
        for k in range(NP):
            tile = pl.multiple_of(k * PW + (my_col // per_tile) * 128, 128)
            turn = (128 + k * col_share - (my_col % per_tile) * col_share) % 128
            moved = pltpu.roll(solved[:, pl.ds(tile, 128)], turn, 1)
            moved_out = jnp.where(lane // col_share == k, moved, moved_out)
        panel[rows_at(step), :] = moved_out[:, : NP * col_share].astype(BF16)

    def update(step, slot, own_ref, solved):
        lead, own = solved[...].astype(BF16), own_ref[...]
        my_tile = my_row * tiles + step * subs
        for n in range(local_cols // span):
            at = slice(n * span, (n + 1) * span)
            change = dot(lead, flipped[:, at])
            product = dot(own, kids[:, at])
            group_all = tile_values(group_of, first_tile + n * (span // TS), span // TS)
            kid_all = tile_values(kid_of, first_tile + n * (span // TS), span // TS)
            for i in range(subs):
                part = slice(i * TS, (i + 1) * TS)
                outs[slot, part, at] = (
                    jnp.where(group_all == group_of[my_tile + i], fronts[slot, part, at], 0.0)
                    + jnp.where(kid_all == kid_of[my_tile + i], product[part], 0.0)
                    + change[part]
                )
            yield

    together(row_solve(0, True, own_even, solved_even))
    for copy in [flip_copy] + kid_copies:
        copy.wait()

    def two_blocks(pair, carry):
        for odd in range(2):
            step = 2 * pair + odd
            slot = 2 * lax.rem(pair, depth) + odd
            front_copy(step, slot).wait()

            @pl.when(pair >= depth)
            def _():
                out_copy(step - 2 * depth, slot).wait()

            if odd:
                mine, later = (own_odd, solved_odd), (own_even, solved_even)
            else:
                mine, later = (own_even, solved_even), (own_odd, solved_odd)
            together(update(step, slot, *mine), row_solve(jnp.minimum(step + 1, steps - 1), False, *later))
            for q in range(fan):
                outs[slot, :, q * local_rows : q * local_rows + held] = jnp.zeros((block_rows, held), F32)
            if not odd:

                @pl.when(pair == 0)
                def _():
                    outs[slot, :held, :] = jnp.zeros((held, local_cols), F32)

            out_copy(step, slot).start()

            @pl.when(pair + depth < steps // 2)
            def _():
                front_copy(step + 2 * depth, slot).start()

        return carry

    lax.fori_loop(0, steps // 2, two_blocks, 0)
    for i in range(steps - 2 * depth, steps):
        out_copy(i, i % (2 * depth)).wait()


def params():
    return pltpu.CompilerParams(vmem_limit_bytes=VMEM_BYTES)


def local(front_entries, tile_group, child_factor, row_map):
    rows, cols = lax.axis_size("row"), lax.axis_size("col")
    fan = rows // cols
    assert fan == 2
    local_rows, local_cols = front_entries.shape
    slice_cols = child_factor.shape[1]
    kid_cols = slice_cols * cols
    tiles = local_rows // TS
    share = PW // rows
    held = NP * share
    my_row, my_col = lax.axis_index("row"), lax.axis_index("col")
    place = jnp.stack([my_row, my_col]).astype(jnp.int32)

    flipped = child_factor.T
    own_map = lax.dynamic_slice_in_dim(row_map, my_row * tiles, tiles)
    starts = flipped.reshape(slice_cols, tiles, TS)[:, :, :held]

    def chosen(block):
        keep = (own_map == block * tiles)[None, :, None]
        return jnp.sum(jnp.where(keep, starts, 0), axis=1, dtype=F32)

    corner = jnp.concatenate(
        [
            front_entries[:held, q * local_rows + k * share : q * local_rows + (k + 1) * share]
            for k in range(NP)
            for q in range(fan)
        ],
        axis=1,
    )
    kids = jnp.concatenate([chosen(my_row), chosen(jnp.bitwise_xor(my_row, rows // 2))], axis=1)
    packet = jnp.concatenate([corner, kids], axis=0)
    packets = [swapped(packet, "row", d * fan) for d in range(cols)]

    row_strip = jnp.concatenate(
        [
            front_entries[:, q * local_rows + k * share : q * local_rows + (k + 1) * share]
            for k in range(NP)
            for q in range(fan)
        ],
        axis=1,
    )
    gathered = lax.all_gather(flipped, "row", axis=0)
    steps = [1 << i for i in range(cols.bit_length() - 1)]
    orders = [steps, steps[::-1]]
    halves = [row_strip[None, : local_rows // 2], row_strip[None, local_rows // 2 :]]
    masks = [[0], [0]]
    for h in range(2):
        for step in orders[h][:-2]:
            halves[h] = jnp.concatenate([halves[h], swapped(halves[h], "col", step)], axis=0)
            masks[h] = masks[h] + [m ^ step for m in masks[h]]
    others = [swapped(halves[h], "col", orders[h][-2]) for h in range(2)]
    masks = [masks[h] + [m ^ orders[h][-2] for m in masks[h]] for h in range(2)]
    merged = []
    for d in range(cols):
        kid = packets[d][held:, :held] + packets[d ^ (cols // 2)][held:, held:]
        half = slice_cols // 2
        merged.append(
            jnp.concatenate(
                [packets[d][:held], jnp.concatenate([kid[:half], kid[half:]], axis=1)], axis=0
            )
        )
    merged = jnp.stack(merged)
    near = jnp.stack([swapped(merged, "col", d) for d in range(cols)])
    col_strip, near = lax.optimization_barrier((front_entries[:held].astype(BF16), near))
    col_strips = lax.all_gather(col_strip, "row", axis=0)
    far = swapped(near, "row", 1)

    tile_ids = jnp.arange(row_map.shape[0], dtype=jnp.int32)
    inverse_map = jnp.sum(
        jnp.where(row_map[None, :] == tile_ids[:, None], tile_ids[None, :], 0), axis=1, dtype=jnp.int32
    )
    kid_of = (inverse_map >= row_map.shape[0] // 2).astype(F32)
    group_of = jnp.repeat(tile_group, MT // TS).astype(F32)

    state = jax.ShapeDtypeStruct((PW, PW), F32)
    state_scratch = [pltpu.VMEM((PW, PW), F32), pltpu.VMEM((PW, PW), F32)]
    diag_scratch = [pltpu.VMEM((PW, 128), F32), pltpu.VMEM((8, PW), F32)]
    begun, begun_upper, diag_col, diag_row, low_rows, piv_t, piv = pl.pallas_call(
        functools.partial(open_kernel, (cols, fan, share, held, tiles)),
        out_shape=[
            state, state,
            jax.ShapeDtypeStruct((PW, 128), F32),
            jax.ShapeDtypeStruct((8, PW), F32),
            jax.ShapeDtypeStruct((PW, NPIV), F32),
            jax.ShapeDtypeStruct((kid_cols, NPIV), BF16),
            jax.ShapeDtypeStruct((NPIV, kid_cols), BF16),
        ],
        in_specs=[smem_spec()] * 3 + [whole_spec()] * 2,
        out_specs=[whole_spec()] * 7,
        scratch_shapes=[pltpu.VMEM((NPIV, NPIV), F32), pltpu.VMEM((NPIV, kid_cols), F32)],
        compiler_params=params(),
        cost_estimate=pl.CostEstimate(flops=10**10, bytes_accessed=3 * 10**7, transcendentals=0),
        name="open_pivots",
    )(place, group_of, kid_of, near, far)

    middle = local_rows // 4

    def joined(part):
        return [
            jnp.concatenate([value[h][:, part * middle : (part + 1) * middle] for value in (halves, others)])
            for h in range(2)
        ]

    def last_step(value):
        return [swapped(value[h], "col", orders[h][-1]) for h in range(2)]

    begun, gathered, others[0], others[1] = lax.optimization_barrier((begun, gathered, *others))
    early = joined(0)
    early_far = last_step(early)
    masks = [masks[h] + [m ^ orders[h][-1] for m in masks[h]] for h in range(2)]

    placed = pl.pallas_call(
        functools.partial(place_kernel, (cols, fan, tiles, slice_cols)),
        out_shape=[jax.ShapeDtypeStruct((2 * slice_cols, local_rows), BF16)] * cols,
        in_specs=[smem_spec()] * 2 + [whole_spec()],
        out_specs=[whole_spec()] * cols,
        compiler_params=params(),
        cost_estimate=pl.CostEstimate(flops=0, bytes_accessed=2**16, transcendentals=0),
        name="place_tiles",
    )(place, inverse_map, gathered)
    begun, *placed = lax.optimization_barrier((begun, *placed))
    kid_parts = [swapped(placed[d], "col", d) for d in range(cols)]

    square = jax.ShapeDtypeStruct((PW, PW), BF16)
    lower1, inv1_hi, inv1_lo, inv1_t_hi, inv1_t_lo, link, link_t, rest = pl.pallas_call(
        first_kernel,
        out_shape=[
            jax.ShapeDtypeStruct((2 * PW, PW), F32),
            square, square, square, square, square, square, state,
        ],
        in_specs=[whole_spec()] * 5,
        out_specs=[whole_spec()] * 8,
        scratch_shapes=state_scratch,
        compiler_params=params(),
        cost_estimate=pl.CostEstimate(flops=10**9, bytes_accessed=10**6, transcendentals=0),
        name="first_pivots",
    )(begun, begun_upper, diag_col, diag_row, low_rows)
    lower2, inv2_hi, inv2_lo, inv2_t_hi, inv2_t_lo = pl.pallas_call(
        second_kernel,
        out_shape=[jax.ShapeDtypeStruct((PW, PW), F32), square, square, square, square],
        in_specs=[whole_spec()],
        out_specs=[whole_spec()] * 5,
        scratch_shapes=state_scratch + diag_scratch,
        compiler_params=params(),
        cost_estimate=pl.CostEstimate(flops=2 * 10**9, bytes_accessed=10**6, transcendentals=0),
        name="second_pivots",
    )(rest)

    lower2, kid_parts, early_far, *others = lax.optimization_barrier((lower2, kid_parts, early_far, *others))
    near_kids = jnp.concatenate([part[slice_cols:] for part in kid_parts], axis=0)
    far_kids = swapped(near_kids, "row", 1)
    late = joined(1)
    late_far = last_step(late)

    block_cols = min(1024, local_rows)
    per_block = local_rows // block_cols
    wide = min(512, block_cols)
    solved_cols = pl.pallas_call(
        functools.partial(col_kernel, (rows, fan, share, block_cols, local_rows, tiles, wide)),
        grid=(local_cols // block_cols,),
        out_shape=jax.ShapeDtypeStruct((NPIV, local_cols), BF16),
        in_specs=[smem_spec()] * 3
        + [
            pl.BlockSpec((rows, held, block_cols), lambda j: (0, 0, j)),
            pl.BlockSpec((kid_cols, block_cols), lambda j: (0, j % per_block)),
            pl.BlockSpec((kid_cols, block_cols), lambda j: (0, j % per_block)),
        ]
        + [whole_spec()] * 6,
        out_specs=pl.BlockSpec((NPIV, block_cols), lambda j: (0, j)),
        scratch_shapes=[
            pltpu.VMEM((block_cols // wide, NPIV, wide), F32),
            pltpu.VMEM((kid_cols, block_cols), BF16),
        ],
        compiler_params=params(),
        cost_estimate=pl.CostEstimate(flops=10**10, bytes_accessed=3 * 10**7, transcendentals=0),
        name="col_factors",
    )(
        place, group_of, kid_of, col_strips, near_kids, far_kids,
        piv, inv1_hi, inv1_lo, inv2_hi, inv2_lo, link,
    )

    block_rows = min(512, local_rows // 2)
    depth = 1
    solved_cols, *late_far = lax.optimization_barrier((solved_cols, *late_far))
    schur_block, factor_panels = pl.pallas_call(
        functools.partial(
            schur_kernel,
            (cols, fan, share, held, slice_cols, block_rows, local_rows, local_cols, tiles),
            masks,
        ),
        out_shape=[
            jax.ShapeDtypeStruct((local_rows, local_cols), F32),
            jax.ShapeDtypeStruct((local_rows, NP * PW // cols), BF16),
        ],
        in_specs=[smem_spec()] * 3 + [whole_spec()] * 8 + [any_spec()] * (12 + cols),
        out_specs=[any_spec(), whole_spec()],
        scratch_shapes=[
            pltpu.VMEM((2 * depth, block_rows, local_cols), F32),
            pltpu.VMEM((2 * depth, block_rows, local_cols), F32),
            pltpu.VMEM((kid_cols, local_cols), BF16),
            pltpu.VMEM((kid_cols, local_rows), BF16),
            pltpu.VMEM((cols, local_rows, fan * held), F32),
            pltpu.VMEM((NPIV, local_cols), BF16),
            pltpu.VMEM((block_rows, NPIV), F32),
            pltpu.VMEM((block_rows, NPIV), F32),
            pltpu.VMEM((block_rows, kid_cols), BF16),
            pltpu.VMEM((block_rows, kid_cols), BF16),
            pltpu.SemaphoreType.DMA((2 * depth,)),
            pltpu.SemaphoreType.DMA((2 * depth,)),
            pltpu.SemaphoreType.DMA,
            pltpu.SemaphoreType.DMA((fan,)),
            pltpu.SemaphoreType.DMA((cols,)),
            pltpu.SemaphoreType.DMA((4 * cols,)),
        ],
        compiler_params=params(),
        cost_estimate=pl.CostEstimate(flops=3 * 10**10, bytes_accessed=9 * 10**7, transcendentals=0),
        name="schur_update",
    )(
        place, group_of, kid_of, piv_t, lower1, lower2,
        inv1_t_hi, inv1_t_lo, inv2_t_hi, inv2_t_lo, link_t,
        front_entries, solved_cols, near_kids, far_kids, *kid_parts,
        early[0], early_far[0], late[0], late_far[0], early[1], early_far[1], late[1], late_far[1],
    )
    return (factor_panels, schur_block)


def solution(mesh):
    placed = (P("row", "col"), P(), P("row", "col"), P())
    return jax.shard_map(
        local,
        mesh=mesh,
        in_specs=placed,
        out_specs=(P("row", "col"), P("row", "col")),
        check_vma=False,
    )
```

```python
import functools

import jax
import jax.numpy as jnp
from jax import lax
from jax.experimental import pallas as pl
from jax.experimental.pallas import tpu as pltpu
from jax.sharding import PartitionSpec as P

PW = 256
NP = 2
TS = 128
MT = 512
NPIV = NP * PW
BLK = 32
F32 = jnp.float32
BF16 = jnp.bfloat16
VMEM_BYTES = 60 * 1024 * 1024

NN = (((1,), (0,)), ((), ()))
NT = (((1,), (1,)), ((), ()))
TN = (((0,), (0,)), ((), ()))


def dot(left, right, dims=NN, precision=None):
    return lax.dot_general(left, right, dims, precision=precision, preferred_element_type=F32)


def exact(left, right, dims=NN):
    return dot(left, right, dims, lax.Precision.HIGHEST)


def split(value):
    high = value.astype(BF16)
    return high, (value - high.astype(F32)).astype(BF16)


def swapped(value, axis, mask):
    if mask == 0:
        return value
    return lax.ppermute(value, axis, [(i, i ^ mask) for i in range(lax.axis_size(axis))])


def whole_spec():
    return pl.BlockSpec(memory_space=pltpu.VMEM)


def any_spec():
    return pl.BlockSpec(memory_space=pl.ANY)


def smem_spec():
    return pl.BlockSpec(memory_space=pltpu.SMEM)


def factor_diagonal(block):
    groups = BLK // 8
    lane = lax.broadcasted_iota(jnp.int32, (BLK, 128), 1)
    row = lax.broadcasted_iota(jnp.int32, (BLK, 128), 0)
    row8 = lax.broadcasted_iota(jnp.int32, (8, 128), 0)
    start = jnp.where(lane < BLK, block, jnp.where(lane == row + BLK, 1.0, 0.0))
    work = [start[8 * g : 8 * g + 8] for g in range(groups)]
    cols = []
    for k in range(BLK):
        base = 8 * (k // 8)
        cols.append(jnp.broadcast_to(block[base:, k : k + 1], (BLK - base, 128)))
    scale = [jnp.ones((8, 128), F32) for _ in range(groups)]

    def inverse_root(value):
        root = lax.rsqrt(value)
        return root * (1.5 - 0.5 * value * root * root)

    for j in range(0, BLK, 2):
        g0 = j // 8
        base = 8 * g0
        one, two = cols[j], cols[j + 1]
        first, cross, last = one[j - base : j - base + 1], one[j - base + 1 : j - base + 2], two[j - base + 1 : j - base + 2]
        volume = first * last - cross * cross
        root = inverse_root(volume)
        inverse = root * root
        below = row[base:] > j + 1
        lead_one = jnp.where(below, last * one - cross * two, 0.0) * inverse
        lead_two = jnp.where(below, first * two - cross * one, 0.0) * inverse
        row_one, row_two = work[g0][j - base : j - base + 1], work[g0][j - base + 1 : j - base + 2]
        for k in range(j + 2, BLK):
            skip = 8 * (k // 8 - g0)
            cols[k] = cols[k] - (
                lead_one[skip:] * one[k - base : k - base + 1] + lead_two[skip:] * two[k - base : k - base + 1]
            )
        for g in range(g0, groups):
            part = slice(8 * (g - g0), 8 * (g - g0) + 8)
            work[g] = work[g] - (lead_one[part] * row_one + lead_two[part] * row_two)
        first_root = inverse_root(first)
        ratio = cross * (first_root * first_root)
        work[g0] = work[g0] - jnp.where(row8 == j - base + 1, ratio, 0.0) * row_one
        scale[g0] = jnp.where(row8 == j - base, first_root, scale[g0])
        scale[g0] = jnp.where(row8 == j - base + 1, first * first_root * root, scale[g0])
    return jnp.concatenate([work[g] * scale[g] for g in range(groups)], axis=0)


def factor_panel(work, upper_out, start, stop):
    per_tile = 128 // BLK
    row = lax.broadcasted_iota(jnp.int32, (BLK, PW), 0)
    lane = lax.broadcasted_iota(jnp.int32, (BLK, PW), 1)
    all_lane = lax.broadcasted_iota(jnp.int32, (PW, PW), 1)

    def step(b, carry):
        low = pl.multiple_of(b * BLK, BLK)
        tile = pl.multiple_of((b // per_tile) * 128, 128)
        shift = (b % per_tile) * BLK
        block = pltpu.roll(work[pl.ds(low, BLK), pl.ds(tile, 128)], (128 - shift) % 128, 1)
        done = factor_diagonal(block)
        inverse = pltpu.roll(done, 128 - BLK, 1)[:, :BLK]
        inside = (lane >= low) & (lane < low + BLK)
        lines = jnp.where(inside, jnp.where(lane == row + low, 1.0, 0.0), work[pl.ds(low, BLK), :])
        upper = exact(inverse, lines)
        placed = pltpu.roll(done, shift, 1)
        corner = jnp.concatenate([placed] * (PW // 128), axis=1)
        upper_out[pl.ds(low, BLK), :] = jnp.where(inside, corner, upper)
        lead = jnp.where(lane >= low + BLK, upper, 0.0)
        kept = jnp.where((all_lane >= low) & (all_lane < low + BLK), 0.0, work[...])
        work[...] = kept - exact(lead, upper, TN)
        work[pl.ds(low, BLK), :] = upper
        return carry

    lax.fori_loop(start, stop, step, 0)


def diagonals(value):
    row = lax.broadcasted_iota(jnp.int32, (PW, PW), 0)
    col = lax.broadcasted_iota(jnp.int32, (PW, PW), 1)
    kept = jnp.where(row == col, value, 0.0)
    return jnp.sum(kept, axis=1, keepdims=True), jnp.sum(kept, axis=0, keepdims=True)


def start_panel(work, diag_col, diag_row, value):
    by_row, by_col = diagonals(value)
    diag_col[...] = jnp.broadcast_to(by_row, (PW, 128))
    diag_row[...] = jnp.broadcast_to(by_col, (8, PW))
    work[...] = value / jnp.sqrt(by_row) / jnp.sqrt(by_col)


def pivot_values(table, stride, share, along_rows):
    shape = (NPIV, 1) if along_rows else (1, NPIV)
    block = lax.broadcasted_iota(jnp.int32, shape, 0 if along_rows else 1) % PW // share
    values = jnp.zeros(shape, F32)
    for r in range(PW // share):
        values = jnp.where(block == r, table[r * stride], values)
    return values


def tile_values(table, start, count):
    return jnp.concatenate([jnp.full((1, TS), table[start + i], F32) for i in range(count)], axis=1)


def finish_panel(work, upper, diag_col, diag_row, lower, inv_hi, inv_lo, inv_t_hi, inv_t_lo):
    row = lax.broadcasted_iota(jnp.int32, (PW, PW), 0)
    col = lax.broadcasted_iota(jnp.int32, (PW, PW), 1)
    lower[:PW, :] = jnp.where(col <= row, upper[...].T, 0.0) * jnp.sqrt(diag_col[:, :1])
    inverse = jnp.where(col <= row, work[...], 0.0) / jnp.sqrt(diag_row[:1, :])
    inv_hi[...], inv_lo[...] = split(inverse)
    inv_t_hi[...], inv_t_lo[...] = split(inverse.T)
    return inverse


def open_kernel(sizes, place, group_of, kid_of, near, far,
                work, upper, diag_col, diag_row, low_rows, piv_t, piv, pile, wide):
    cols, fan, share, held, tiles = sizes
    my_row, my_col = place[0], place[1]
    my_q, my_a = my_row % fan, my_row // fan
    col_share = PW // cols
    for dq, source in enumerate((near, far)):
        for d in range(cols):
            r = (my_a ^ d) * fan + (my_q ^ dq)
            pieces = [source[c ^ my_col, d, :held, :] for c in range(cols)]
            line = jnp.concatenate(
                [piece[:, k * col_share : (k + 1) * col_share] for k in range(NP) for piece in pieces],
                axis=1,
            )
            kids = []
            for e in range(cols):
                packed = source[e, d, held:, :]
                kids += [packed[:, :held], packed[:, held:]]
            kids = jnp.concatenate(kids, axis=0).T
            for k in range(NP):
                at = pl.ds(pl.multiple_of(k * PW + r * share, share), share)
                pile[at, :] = line[k * share : (k + 1) * share]
                wide[at, :] = kids[k * share : (k + 1) * share]
    piv[...] = wide[...].astype(BF16)
    piv_t[...] = wide[...].T.astype(BF16)
    product = dot(piv[...], piv_t[...])
    same_group = pivot_values(group_of, tiles, share, True) == pivot_values(group_of, tiles, share, False)
    same_kid = pivot_values(kid_of, tiles, share, True) == pivot_values(kid_of, tiles, share, False)
    pile[...] = jnp.where(same_group, pile[...], 0.0) + jnp.where(same_kid, product, 0.0)
    low_rows[...] = pile[PW:, :]
    upper[...] = jnp.zeros_like(upper)
    start_panel(work, diag_col, diag_row, pile[:PW, :PW])
    factor_panel(work, upper, 0, PW // BLK // 2)


def first_kernel(begun, begun_upper, diag_col, diag_row, low_rows,
                 lower, inv_hi, inv_lo, inv_t_hi, inv_t_lo, link_out, link_t, rest, work, upper):
    work[...] = begun[...]
    upper[...] = begun_upper[...]
    factor_panel(work, upper, PW // BLK // 2, PW // BLK)
    inverse = finish_panel(work, upper, diag_col, diag_row, lower, inv_hi, inv_lo, inv_t_hi, inv_t_lo)
    link = exact(low_rows[:, :PW], inverse, NT).astype(BF16)
    link_out[...] = link
    lower[PW:, :] = link.astype(F32)
    link_t[...] = link.astype(F32).T.astype(BF16)
    rest[...] = low_rows[:, PW:] - dot(link, link, NT)


def second_kernel(rest, lower, inv_hi, inv_lo, inv_t_hi, inv_t_lo, work, upper, diag_col, diag_row):
    start_panel(work, diag_col, diag_row, rest[...])
    factor_panel(work, upper, 0, PW // BLK)
    finish_panel(work, upper, diag_col, diag_row, lower, inv_hi, inv_lo, inv_t_hi, inv_t_lo)


def place_kernel(sizes, place, inverse_map, held, *outs):
    cols, fan, tiles, slice_cols = sizes
    my_row, my_col = place[0], place[1]
    my_q = my_row % fan

    def fetch(block, i):
        tile = inverse_map[block * tiles + i]
        at = pl.multiple_of((tile % tiles) * TS, TS)
        return held[tile // tiles, :, pl.ds(at, TS)]

    for i in range(tiles):
        mine = fetch(my_row, i)
        for d in range(cols):
            outs[d][:slice_cols, i * TS : (i + 1) * TS] = mine
    for d in range(cols):
        for i in range(tiles):
            outs[d][slice_cols:, i * TS : (i + 1) * TS] = fetch((my_col ^ d) * fan + my_q, i)


def schur_kernel(sizes, masks, place, group_of, kid_of,
                 piv, piv_t, lower1, lower2, inv1_hi, inv1_lo, inv2_hi, inv2_lo, link,
                 inv1_t_hi, inv1_t_lo, inv2_t_hi, inv2_t_lo, link_t, *refs):
    rows, cols, fan, share, held, slice_cols, block_rows, local_rows, local_cols, tiles, wide = sizes
    front, strips, near_kids, far_kids = refs[:4]
    sources = refs[4 : 4 + cols]
    halves = [refs[4 + cols : 4 + 2 * cols], refs[4 + 2 * cols : 4 + 3 * cols]]
    out, panel = refs[4 + 3 * cols : 6 + 3 * cols]
    (fronts, outs, strips_in, kids, own_t, pieces, flipped, strip, solved_even, solved_odd, own_even, own_odd,
     front_sems, out_sems, strip_sems, kid_sems, own_sems, piece_sems) = refs[6 + 3 * cols :]
    my_row, my_col = place[0], place[1]
    my_q = my_row % fan
    first_tile = my_col * fan * tiles
    steps = local_rows // block_rows
    chunks = local_cols // wide
    depth = fronts.shape[0] // 2
    half_rows = local_rows // 2

    def rows_at(i):
        return pl.ds(pl.multiple_of(i * block_rows, block_rows), block_rows)

    def front_copy(i, slot):
        return pltpu.make_async_copy(front.at[rows_at(i), :], fronts.at[slot], front_sems.at[slot])

    def out_copy(i, slot):
        return pltpu.make_async_copy(outs.at[slot], out.at[rows_at(i), :], out_sems.at[slot])

    def chunk_at(n):
        return pl.ds(pl.multiple_of(n * wide, wide), wide)

    def strip_copy(n):
        return pltpu.make_async_copy(
            strips.at[:, :, chunk_at(n)], strips_in.at[:, :, chunk_at(n)], strip_sems.at[n]
        )

    kid_copies = [
        pltpu.make_async_copy(
            source,
            kids.at[:, pl.ds(pl.multiple_of((my_q ^ q) * local_rows, local_rows), local_rows)],
            kid_sems.at[q],
        )
        for q, source in enumerate((near_kids, far_kids))
    ]
    own_copies = [
        pltpu.make_async_copy(
            source.at[:slice_cols, :], own_t.at[d * slice_cols : (d + 1) * slice_cols, :], own_sems.at[d]
        )
        for d, source in enumerate(sources)
    ]
    piece_copies = [
        pltpu.make_async_copy(
            halves[half][i],
            pieces.at[my_col ^ mask, half * half_rows : (half + 1) * half_rows, :],
            piece_sems.at[half * cols + i],
        )
        for half in range(2)
        for i, mask in enumerate(masks[half])
    ]
    for copy in kid_copies:
        copy.start()
    for n in range(chunks):
        strip_copy(n).start()
    for copy in own_copies + piece_copies:
        copy.start()
    for copy in kid_copies:
        copy.wait()
    group_col = pivot_values(group_of, tiles, share, True)
    kid_col = pivot_values(kid_of, tiles, share, True)

    def col_solve(n, pile):
        at = slice(n * wide, (n + 1) * wide)
        for r in range(rows):
            piece = strips_in[r, :, at].astype(F32)
            for k in range(NP):
                low = k * PW + r * share
                pile[low : low + share, :] = piece[k * share : (k + 1) * share]
        tile = first_tile + n * (wide // TS)
        group_all = tile_values(group_of, tile, wide // TS)
        kid_all = tile_values(kid_of, tile, wide // TS)
        product = dot(piv[...], kids[:, at])
        yield
        full = jnp.where(group_col == group_all, pile[...], 0.0) + jnp.where(
            kid_col == kid_all, product, 0.0
        )
        first, second = full[:PW].astype(BF16), full[PW:]
        yield
        both = dot(jnp.concatenate([inv1_hi[...], inv1_lo[...]], axis=0), first)
        yield
        head = (both[:PW] + both[PW:]).astype(BF16)
        flipped[:PW, at] = -head
        yield
        second = (second - dot(link[...], head)).astype(BF16)
        yield
        both = dot(jnp.concatenate([inv2_hi[...], inv2_lo[...]], axis=0), second)
        yield
        flipped[PW:, at] = (-(both[:PW] + both[PW:])).astype(BF16)

    col_share = PW // cols
    subs = block_rows // TS
    per_tile = 128 // col_share
    span = min(512, local_cols)
    group_row = pivot_values(group_of, tiles, share, False)
    kid_row = pivot_values(kid_of, tiles, share, False)
    lane = lax.broadcasted_iota(jnp.int32, (block_rows, 128), 1)

    def row_solve(step, opening, own_ref, solved):
        own = own_t[:, rows_at(step)].astype(F32).T.astype(BF16)
        own_ref[...] = own
        product = dot(own, piv_t[...])
        yield
        entries = jnp.concatenate(
            [
                pieces[c, rows_at(step), k * col_share : (k + 1) * col_share]
                for k in range(NP)
                for c in range(cols)
            ],
            axis=1,
        )
        my_tile = my_row * tiles + step * subs
        parts = []
        for i in range(subs):
            part = slice(i * TS, (i + 1) * TS)
            parts.append(
                jnp.where(group_row == group_of[my_tile + i], entries[part], 0.0)
                + jnp.where(kid_row == kid_of[my_tile + i], product[part], 0.0)
            )
        full = jnp.concatenate(parts, axis=0)
        high, low = split(full[:, :PW])
        yield
        head = dot(high, inv1_t_hi[...]) + dot(high, inv1_t_lo[...]) + dot(low, inv1_t_hi[...])
        solved[:, :PW] = head
        yield
        high, low = split(full[:, PW:] - dot(head.astype(BF16), link_t[...]))
        yield
        solved[:, PW:] = dot(high, inv2_t_hi[...]) + dot(high, inv2_t_lo[...]) + dot(low, inv2_t_hi[...])
        yield
        if opening:
            at = pl.multiple_of(my_row * share, share)
            solved[:share, :PW] = lower1[pl.ds(at, share), :]
            solved[:share, PW:] = jnp.zeros((share, PW), F32)
            solved[share : 2 * share, :PW] = lower1[pl.ds(PW + at, share), :]
            solved[share : 2 * share, PW:] = lower2[pl.ds(at, share), :]
        moved_out = jnp.zeros((block_rows, 128), F32)
        for k in range(NP):
            tile = pl.multiple_of(k * PW + (my_col // per_tile) * 128, 128)
            turn = (128 + k * col_share - (my_col % per_tile) * col_share) % 128
            moved = pltpu.roll(solved[:, pl.ds(tile, 128)], turn, 1)
            moved_out = jnp.where(lane // col_share == k, moved, moved_out)
        panel[rows_at(step), :] = moved_out[:, : NP * col_share].astype(BF16)

    def update(step, slot, own_ref, solved):
        lead, own = solved[...].astype(BF16), own_ref[...]
        my_tile = my_row * tiles + step * subs
        for n in range(local_cols // span):
            at = slice(n * span, (n + 1) * span)
            change = dot(lead, flipped[:, at])
            product = dot(own, kids[:, at])
            group_all = tile_values(group_of, first_tile + n * (span // TS), span // TS)
            kid_all = tile_values(kid_of, first_tile + n * (span // TS), span // TS)
            for i in range(subs):
                part = slice(i * TS, (i + 1) * TS)
                outs[slot, part, at] = (
                    jnp.where(group_all == group_of[my_tile + i], fronts[slot, part, at], 0.0)
                    + jnp.where(kid_all == kid_of[my_tile + i], product[part], 0.0)
                    + change[part]
                )
            yield

    def together(*parts):
        parts = list(parts)
        while parts:
            for part in list(parts):
                try:
                    next(part)
                except StopIteration:
                    parts.remove(part)

    for n in range(0, chunks, 2):
        pair = range(n, min(n + 2, chunks))
        for m in pair:
            strip_copy(m).wait()
        if n == 0:
            for i in range(2 * depth):
                front_copy(i, i).start()
        together(*[col_solve(m, strip.at[m - n]) for m in pair])
    for copy in own_copies + piece_copies:
        copy.wait()
    together(row_solve(0, True, own_even, solved_even))

    def two_blocks(pair, carry):
        for odd in range(2):
            step = 2 * pair + odd
            slot = 2 * lax.rem(pair, depth) + odd
            front_copy(step, slot).wait()

            @pl.when(pair >= depth)
            def _():
                out_copy(step - 2 * depth, slot).wait()

            if odd:
                mine, later = (own_odd, solved_odd), (own_even, solved_even)
            else:
                mine, later = (own_even, solved_even), (own_odd, solved_odd)
            together(update(step, slot, *mine), row_solve(jnp.minimum(step + 1, steps - 1), False, *later))
            for q in range(fan):
                outs[slot, :, q * local_rows : q * local_rows + held] = jnp.zeros((block_rows, held), F32)
            if not odd:

                @pl.when(pair == 0)
                def _():
                    outs[slot, :held, :] = jnp.zeros((held, local_cols), F32)

            out_copy(step, slot).start()

            @pl.when(pair + depth < steps // 2)
            def _():
                front_copy(step + 2 * depth, slot).start()

        return carry

    lax.fori_loop(0, steps // 2, two_blocks, 0)
    for i in range(steps - 2 * depth, steps):
        out_copy(i, i % (2 * depth)).wait()


def params():
    return pltpu.CompilerParams(vmem_limit_bytes=VMEM_BYTES)


def local(front_entries, tile_group, child_factor, row_map):
    rows, cols = lax.axis_size("row"), lax.axis_size("col")
    fan = rows // cols
    assert fan == 2
    local_rows, local_cols = front_entries.shape
    slice_cols = child_factor.shape[1]
    kid_cols = slice_cols * cols
    tiles = local_rows // TS
    share = PW // rows
    held = NP * share
    my_row, my_col = lax.axis_index("row"), lax.axis_index("col")
    place = jnp.stack([my_row, my_col]).astype(jnp.int32)

    flipped = child_factor.T
    own_map = lax.dynamic_slice_in_dim(row_map, my_row * tiles, tiles)
    starts = flipped.reshape(slice_cols, tiles, TS)[:, :, :held]

    def chosen(block):
        keep = (own_map == block * tiles)[None, :, None]
        return jnp.sum(jnp.where(keep, starts, 0), axis=1, dtype=F32)

    corner = jnp.concatenate(
        [
            front_entries[:held, q * local_rows + k * share : q * local_rows + (k + 1) * share]
            for k in range(NP)
            for q in range(fan)
        ],
        axis=1,
    )
    kids = jnp.concatenate([chosen(my_row), chosen(jnp.bitwise_xor(my_row, rows // 2))], axis=1)
    packet = jnp.concatenate([corner, kids], axis=0)
    packets = [swapped(packet, "row", d * fan) for d in range(cols)]

    row_strip = jnp.concatenate(
        [
            front_entries[:, q * local_rows + k * share : q * local_rows + (k + 1) * share]
            for k in range(NP)
            for q in range(fan)
        ],
        axis=1,
    )
    gathered = lax.all_gather(flipped, "row", axis=0)
    col_strip, row_strip, *packets = lax.optimization_barrier(
        (front_entries[:held].astype(BF16), row_strip, *packets)
    )
    col_strips = lax.all_gather(col_strip, "row", axis=0)
    steps = [1 << i for i in range(cols.bit_length() - 1)]
    orders = [steps, steps[::-1]]
    halves = [[row_strip[: local_rows // 2]], [row_strip[local_rows // 2 :]]]
    masks = [[0], [0]]

    def pass_on(halves, count, own_only):
        for h in range(2):
            for step in orders[h][:count]:
                for piece, mask in list(zip(halves[h], masks[h])):
                    if mask ^ step not in masks[h] and (mask == 0 or not own_only):
                        halves[h].append(swapped(piece, "col", step))
                        masks[h].append(mask ^ step)

    pass_on(halves, 1, True)
    merged = []
    for d in range(cols):
        kid = packets[d][held:, :held] + packets[d ^ (cols // 2)][held:, held:]
        half = slice_cols // 2
        merged.append(
            jnp.concatenate(
                [packets[d][:held], jnp.concatenate([kid[:half], kid[half:]], axis=1)], axis=0
            )
        )
    merged = jnp.stack(merged)
    near = jnp.stack([swapped(merged, "col", d) for d in range(cols)])
    far = swapped(near, "row", 1)

    tile_ids = jnp.arange(row_map.shape[0], dtype=jnp.int32)
    inverse_map = jnp.sum(
        jnp.where(row_map[None, :] == tile_ids[:, None], tile_ids[None, :], 0), axis=1, dtype=jnp.int32
    )
    kid_of = (inverse_map >= row_map.shape[0] // 2).astype(F32)
    group_of = jnp.repeat(tile_group, MT // TS).astype(F32)

    state = jax.ShapeDtypeStruct((PW, PW), F32)
    state_scratch = [pltpu.VMEM((PW, PW), F32), pltpu.VMEM((PW, PW), F32)]
    diag_scratch = [pltpu.VMEM((PW, 128), F32), pltpu.VMEM((8, PW), F32)]
    begun, begun_upper, diag_col, diag_row, low_rows, piv_t, piv = pl.pallas_call(
        functools.partial(open_kernel, (cols, fan, share, held, tiles)),
        out_shape=[
            state, state,
            jax.ShapeDtypeStruct((PW, 128), F32),
            jax.ShapeDtypeStruct((8, PW), F32),
            jax.ShapeDtypeStruct((PW, NPIV), F32),
            jax.ShapeDtypeStruct((kid_cols, NPIV), BF16),
            jax.ShapeDtypeStruct((NPIV, kid_cols), BF16),
        ],
        in_specs=[smem_spec()] * 3 + [whole_spec()] * 2,
        out_specs=[whole_spec()] * 7,
        scratch_shapes=[pltpu.VMEM((NPIV, NPIV), F32), pltpu.VMEM((NPIV, kid_cols), F32)],
        compiler_params=params(),
        cost_estimate=pl.CostEstimate(flops=10**10, bytes_accessed=3 * 10**7, transcendentals=0),
        name="open_pivots",
    )(place, group_of, kid_of, near, far)

    begun, gathered, halves[0][0], halves[1][0] = lax.optimization_barrier(
        (begun, gathered, halves[0][0], halves[1][0])
    )
    pass_on(halves, cols, True)
    placed = pl.pallas_call(
        functools.partial(place_kernel, (cols, fan, tiles, slice_cols)),
        out_shape=[jax.ShapeDtypeStruct((2 * slice_cols, local_rows), BF16)] * cols,
        in_specs=[smem_spec()] * 2 + [whole_spec()],
        out_specs=[whole_spec()] * cols,
        compiler_params=params(),
        cost_estimate=pl.CostEstimate(flops=0, bytes_accessed=2**16, transcendentals=0),
        name="place_tiles",
    )(place, inverse_map, gathered)
    begun, *placed = lax.optimization_barrier((begun, *placed))
    kid_parts = [swapped(placed[d], "col", d) for d in range(cols)]

    square = jax.ShapeDtypeStruct((PW, PW), BF16)
    lower1, inv1_hi, inv1_lo, inv1_t_hi, inv1_t_lo, link, link_t, rest = pl.pallas_call(
        first_kernel,
        out_shape=[
            jax.ShapeDtypeStruct((2 * PW, PW), F32),
            square, square, square, square, square, square, state,
        ],
        in_specs=[whole_spec()] * 5,
        out_specs=[whole_spec()] * 8,
        scratch_shapes=state_scratch,
        compiler_params=params(),
        cost_estimate=pl.CostEstimate(flops=10**9, bytes_accessed=10**6, transcendentals=0),
        name="first_pivots",
    )(begun, begun_upper, diag_col, diag_row, low_rows)
    lower2, inv2_hi, inv2_lo, inv2_t_hi, inv2_t_lo = pl.pallas_call(
        second_kernel,
        out_shape=[jax.ShapeDtypeStruct((PW, PW), F32), square, square, square, square],
        in_specs=[whole_spec()],
        out_specs=[whole_spec()] * 5,
        scratch_shapes=state_scratch + diag_scratch,
        compiler_params=params(),
        cost_estimate=pl.CostEstimate(flops=2 * 10**9, bytes_accessed=10**6, transcendentals=0),
        name="second_pivots",
    )(rest)

    lower2, kid_parts, halves = lax.optimization_barrier((lower2, kid_parts, halves))
    near_kids = jnp.concatenate([part[slice_cols:] for part in kid_parts], axis=0)
    far_kids = swapped(near_kids, "row", 1)
    pass_on(halves, cols, False)

    block_rows = min(256, local_rows)
    wide = min(512, local_cols)
    depth = min(2, local_rows // block_rows // 2)
    schur_block, factor_panels = pl.pallas_call(
        functools.partial(
            schur_kernel,
            (rows, cols, fan, share, held, slice_cols, block_rows, local_rows, local_cols, tiles, wide),
            masks,
        ),
        out_shape=[
            jax.ShapeDtypeStruct((local_rows, local_cols), F32),
            jax.ShapeDtypeStruct((local_rows, NP * PW // cols), BF16),
        ],
        in_specs=[smem_spec()] * 3 + [whole_spec()] * 14 + [any_spec()] * (4 + 3 * cols),
        out_specs=[any_spec(), whole_spec()],
        scratch_shapes=[
            pltpu.VMEM((2 * depth, block_rows, local_cols), F32),
            pltpu.VMEM((2 * depth, block_rows, local_cols), F32),
            pltpu.VMEM((rows, held, local_cols), BF16),
            pltpu.VMEM((kid_cols, local_cols), BF16),
            pltpu.VMEM((kid_cols, local_rows), BF16),
            pltpu.VMEM((cols, local_rows, fan * held), F32),
            pltpu.VMEM((NPIV, local_cols), BF16),
            pltpu.VMEM((2, NPIV, wide), F32),
            pltpu.VMEM((block_rows, NPIV), F32),
            pltpu.VMEM((block_rows, NPIV), F32),
            pltpu.VMEM((block_rows, kid_cols), BF16),
            pltpu.VMEM((block_rows, kid_cols), BF16),
            pltpu.SemaphoreType.DMA((2 * depth,)),
            pltpu.SemaphoreType.DMA((2 * depth,)),
            pltpu.SemaphoreType.DMA((local_cols // wide,)),
            pltpu.SemaphoreType.DMA((fan,)),
            pltpu.SemaphoreType.DMA((cols,)),
            pltpu.SemaphoreType.DMA((2 * cols,)),
        ],
        compiler_params=params(),
        cost_estimate=pl.CostEstimate(flops=3 * 10**10, bytes_accessed=9 * 10**7, transcendentals=0),
        name="schur_update",
    )(
        place, group_of, kid_of,
        piv, piv_t, lower1, lower2, inv1_hi, inv1_lo, inv2_hi, inv2_lo, link,
        inv1_t_hi, inv1_t_lo, inv2_t_hi, inv2_t_lo, link_t,
        front_entries, col_strips, near_kids, far_kids, *kid_parts,
        *halves[0], *halves[1],
    )
    return (factor_panels, schur_block)


def solution(mesh):
    placed = (P("row", "col"), P(), P("row", "col"), P())
    return jax.shard_map(
        local,
        mesh=mesh,
        in_specs=placed,
        out_specs=(P("row", "col"), P("row", "col")),
        check_vma=False,
    )
```

```python
import functools

import jax
import jax.numpy as jnp
from jax import lax
from jax.experimental import pallas as pl
from jax.experimental.pallas import tpu as pltpu
from jax.sharding import PartitionSpec as P

PW = 256
NP = 2
TS = 128
MT = 512
NPIV = NP * PW
BLK = 32
F32 = jnp.float32
BF16 = jnp.bfloat16
VMEM_BYTES = 60 * 1024 * 1024

NN = (((1,), (0,)), ((), ()))
NT = (((1,), (1,)), ((), ()))
TN = (((0,), (0,)), ((), ()))


def dot(left, right, dims=NN, precision=None):
    return lax.dot_general(left, right, dims, precision=precision, preferred_element_type=F32)


def exact(left, right, dims=NN):
    return dot(left, right, dims, lax.Precision.HIGHEST)


def split(value):
    high = value.astype(BF16)
    return high, (value - high.astype(F32)).astype(BF16)


def swapped(value, axis, mask):
    if mask == 0:
        return value
    return lax.ppermute(value, axis, [(i, i ^ mask) for i in range(lax.axis_size(axis))])


def whole_spec():
    return pl.BlockSpec(memory_space=pltpu.VMEM)


def any_spec():
    return pl.BlockSpec(memory_space=pl.ANY)


def smem_spec():
    return pl.BlockSpec(memory_space=pltpu.SMEM)


def factor_diagonal(block):
    groups = BLK // 8
    lane = lax.broadcasted_iota(jnp.int32, (BLK, 128), 1)
    row = lax.broadcasted_iota(jnp.int32, (BLK, 128), 0)
    row8 = lax.broadcasted_iota(jnp.int32, (8, 128), 0)
    start = jnp.where(lane < BLK, block, jnp.where(lane == row + BLK, 1.0, 0.0))
    work = [start[8 * g : 8 * g + 8] for g in range(groups)]
    cols = []
    for k in range(BLK):
        base = 8 * (k // 8)
        cols.append(jnp.broadcast_to(block[base:, k : k + 1], (BLK - base, 128)))
    scale = [jnp.ones((8, 128), F32) for _ in range(groups)]

    def inverse_root(value):
        root = lax.rsqrt(value)
        return root * (1.5 - 0.5 * value * root * root)

    for j in range(0, BLK, 2):
        g0 = j // 8
        base = 8 * g0
        one, two = cols[j], cols[j + 1]
        first, cross, last = one[j - base : j - base + 1], one[j - base + 1 : j - base + 2], two[j - base + 1 : j - base + 2]
        volume = first * last - cross * cross
        root = inverse_root(volume)
        inverse = root * root
        below = row[base:] > j + 1
        lead_one = jnp.where(below, last * one - cross * two, 0.0) * inverse
        lead_two = jnp.where(below, first * two - cross * one, 0.0) * inverse
        row_one, row_two = work[g0][j - base : j - base + 1], work[g0][j - base + 1 : j - base + 2]
        for k in range(j + 2, BLK):
            skip = 8 * (k // 8 - g0)
            cols[k] = cols[k] - (
                lead_one[skip:] * one[k - base : k - base + 1] + lead_two[skip:] * two[k - base : k - base + 1]
            )
        for g in range(g0, groups):
            part = slice(8 * (g - g0), 8 * (g - g0) + 8)
            work[g] = work[g] - (lead_one[part] * row_one + lead_two[part] * row_two)
        first_root = inverse_root(first)
        ratio = cross * (first_root * first_root)
        work[g0] = work[g0] - jnp.where(row8 == j - base + 1, ratio, 0.0) * row_one
        scale[g0] = jnp.where(row8 == j - base, first_root, scale[g0])
        scale[g0] = jnp.where(row8 == j - base + 1, first * first_root * root, scale[g0])
    return jnp.concatenate([work[g] * scale[g] for g in range(groups)], axis=0)


def factor_panel(work, upper_out, start, stop):
    per_tile = 128 // BLK
    row = lax.broadcasted_iota(jnp.int32, (BLK, PW), 0)
    lane = lax.broadcasted_iota(jnp.int32, (BLK, PW), 1)
    all_lane = lax.broadcasted_iota(jnp.int32, (PW, PW), 1)

    def step(b, carry):
        low = pl.multiple_of(b * BLK, BLK)
        tile = pl.multiple_of((b // per_tile) * 128, 128)
        shift = (b % per_tile) * BLK
        block = pltpu.roll(work[pl.ds(low, BLK), pl.ds(tile, 128)], (128 - shift) % 128, 1)
        done = factor_diagonal(block)
        inverse = pltpu.roll(done, 128 - BLK, 1)[:, :BLK]
        inside = (lane >= low) & (lane < low + BLK)
        lines = jnp.where(inside, jnp.where(lane == row + low, 1.0, 0.0), work[pl.ds(low, BLK), :])
        upper = exact(inverse, lines)
        placed = pltpu.roll(done, shift, 1)
        corner = jnp.concatenate([placed] * (PW // 128), axis=1)
        upper_out[pl.ds(low, BLK), :] = jnp.where(inside, corner, upper)
        lead = jnp.where(lane >= low + BLK, upper, 0.0)
        kept = jnp.where((all_lane >= low) & (all_lane < low + BLK), 0.0, work[...])
        work[...] = kept - exact(lead, upper, TN)
        work[pl.ds(low, BLK), :] = upper
        return carry

    lax.fori_loop(start, stop, step, 0)


def diagonals(value):
    row = lax.broadcasted_iota(jnp.int32, (PW, PW), 0)
    col = lax.broadcasted_iota(jnp.int32, (PW, PW), 1)
    kept = jnp.where(row == col, value, 0.0)
    return jnp.sum(kept, axis=1, keepdims=True), jnp.sum(kept, axis=0, keepdims=True)


def start_panel(work, diag_col, diag_row, value):
    by_row, by_col = diagonals(value)
    diag_col[...] = jnp.broadcast_to(by_row, (PW, 128))
    diag_row[...] = jnp.broadcast_to(by_col, (8, PW))
    work[...] = value / jnp.sqrt(by_row) / jnp.sqrt(by_col)


def pivot_values(table, stride, share, along_rows):
    shape = (NPIV, 1) if along_rows else (1, NPIV)
    block = lax.broadcasted_iota(jnp.int32, shape, 0 if along_rows else 1) % PW // share
    values = jnp.zeros(shape, F32)
    for r in range(PW // share):
        values = jnp.where(block == r, table[r * stride], values)
    return values


def tile_values(table, start, count):
    return jnp.concatenate([jnp.full((1, TS), table[start + i], F32) for i in range(count)], axis=1)


def finish_panel(work, upper, diag_col, diag_row, lower, inv_hi, inv_lo, inv_t_hi, inv_t_lo):
    row = lax.broadcasted_iota(jnp.int32, (PW, PW), 0)
    col = lax.broadcasted_iota(jnp.int32, (PW, PW), 1)
    lower[:PW, :] = jnp.where(col <= row, upper[...].T, 0.0) * jnp.sqrt(diag_col[:, :1])
    inverse = jnp.where(col <= row, work[...], 0.0) / jnp.sqrt(diag_row[:1, :])
    inv_hi[...], inv_lo[...] = split(inverse)
    inv_t_hi[...], inv_t_lo[...] = split(inverse.T)
    return inverse


def open_kernel(sizes, place, group_of, kid_of, near, far,
                work, upper, diag_col, diag_row, low_rows, piv_t, piv, pile, wide):
    cols, fan, share, held, tiles = sizes
    my_row, my_col = place[0], place[1]
    my_q, my_a = my_row % fan, my_row // fan
    col_share = PW // cols
    for dq, source in enumerate((near, far)):
        for d in range(cols):
            r = (my_a ^ d) * fan + (my_q ^ dq)
            pieces = [source[c ^ my_col, d, :held, :] for c in range(cols)]
            line = jnp.concatenate(
                [piece[:, k * col_share : (k + 1) * col_share] for k in range(NP) for piece in pieces],
                axis=1,
            )
            kids = []
            for e in range(cols):
                packed = source[e, d, held:, :]
                kids += [packed[:, :held], packed[:, held:]]
            kids = jnp.concatenate(kids, axis=0).T
            for k in range(NP):
                at = pl.ds(pl.multiple_of(k * PW + r * share, share), share)
                pile[at, :] = line[k * share : (k + 1) * share]
                wide[at, :] = kids[k * share : (k + 1) * share]
    piv[...] = wide[...].astype(BF16)
    piv_t[...] = wide[...].T.astype(BF16)
    product = dot(piv[...], piv_t[...])
    same_group = pivot_values(group_of, tiles, share, True) == pivot_values(group_of, tiles, share, False)
    same_kid = pivot_values(kid_of, tiles, share, True) == pivot_values(kid_of, tiles, share, False)
    pile[...] = jnp.where(same_group, pile[...], 0.0) + jnp.where(same_kid, product, 0.0)
    low_rows[...] = pile[PW:, :]
    upper[...] = jnp.zeros_like(upper)
    start_panel(work, diag_col, diag_row, pile[:PW, :PW])
    factor_panel(work, upper, 0, PW // BLK // 2)


def first_kernel(begun, begun_upper, diag_col, diag_row, low_rows,
                 lower, inv_hi, inv_lo, inv_t_hi, inv_t_lo, link_out, link_t, rest, work, upper):
    work[...] = begun[...]
    upper[...] = begun_upper[...]
    factor_panel(work, upper, PW // BLK // 2, PW // BLK)
    inverse = finish_panel(work, upper, diag_col, diag_row, lower, inv_hi, inv_lo, inv_t_hi, inv_t_lo)
    link = exact(low_rows[:, :PW], inverse, NT).astype(BF16)
    link_out[...] = link
    lower[PW:, :] = link.astype(F32)
    link_t[...] = link.astype(F32).T.astype(BF16)
    rest[...] = low_rows[:, PW:] - dot(link, link, NT)


def second_kernel(rest, lower, inv_hi, inv_lo, inv_t_hi, inv_t_lo, work, upper, diag_col, diag_row):
    start_panel(work, diag_col, diag_row, rest[...])
    factor_panel(work, upper, 0, PW // BLK)
    finish_panel(work, upper, diag_col, diag_row, lower, inv_hi, inv_lo, inv_t_hi, inv_t_lo)


def place_kernel(sizes, place, inverse_map, held, *outs):
    cols, fan, tiles, slice_cols = sizes
    my_row, my_col = place[0], place[1]
    my_q = my_row % fan

    def fetch(block, i):
        tile = inverse_map[block * tiles + i]
        at = pl.multiple_of((tile % tiles) * TS, TS)
        return held[tile // tiles, :, pl.ds(at, TS)]

    for i in range(tiles):
        mine = fetch(my_row, i)
        for d in range(cols):
            outs[d][:slice_cols, i * TS : (i + 1) * TS] = mine
    for d in range(cols):
        for i in range(tiles):
            outs[d][slice_cols:, i * TS : (i + 1) * TS] = fetch((my_col ^ d) * fan + my_q, i)


def together(*parts):
    parts = list(parts)
    while parts:
        for part in list(parts):
            try:
                next(part)
            except StopIteration:
                parts.remove(part)


def col_kernel(sizes, place, group_of, kid_of, strips, near_kids, far_kids,
               piv, inv1_hi, inv1_lo, inv2_hi, inv2_lo, link, out, strip, kids):
    rows, fan, share, block_cols, local_rows, tiles, wide = sizes
    my_row, my_col = place[0], place[1]
    my_q = my_row % fan
    j = pl.program_id(0)
    q = (j * block_cols) // local_rows
    group_col = pivot_values(group_of, tiles, share, True)
    kid_col = pivot_values(kid_of, tiles, share, True)

    @pl.when(q == my_q)
    def _():
        kids[...] = near_kids[...]

    @pl.when(q != my_q)
    def _():
        kids[...] = far_kids[...]

    def col_solve(n, pile):
        at = slice(n * wide, (n + 1) * wide)
        for r in range(rows):
            piece = strips[r, :, at].astype(F32)
            for k in range(NP):
                low = k * PW + r * share
                pile[low : low + share, :] = piece[k * share : (k + 1) * share]
        tile = my_col * fan * tiles + (j * block_cols + n * wide) // TS
        group_all = tile_values(group_of, tile, wide // TS)
        kid_all = tile_values(kid_of, tile, wide // TS)
        product = dot(piv[...], kids[:, at])
        yield
        full = jnp.where(group_col == group_all, pile[...], 0.0) + jnp.where(
            kid_col == kid_all, product, 0.0
        )
        first, second = full[:PW].astype(BF16), full[PW:]
        yield
        both = dot(jnp.concatenate([inv1_hi[...], inv1_lo[...]], axis=0), first)
        yield
        head = (both[:PW] + both[PW:]).astype(BF16)
        out[:PW, at] = -head
        yield
        second = (second - dot(link[...], head)).astype(BF16)
        yield
        both = dot(jnp.concatenate([inv2_hi[...], inv2_lo[...]], axis=0), second)
        yield
        out[PW:, at] = (-(both[:PW] + both[PW:])).astype(BF16)

    together(*[col_solve(n, strip.at[n]) for n in range(block_cols // wide)])


def schur_kernel(sizes, masks, place, group_of, kid_of,
                 piv_t, lower1, lower2, inv1_t_hi, inv1_t_lo, inv2_t_hi, inv2_t_lo, link_t, *refs):
    cols, fan, share, held, slice_cols, block_rows, local_rows, local_cols, tiles = sizes
    front, solved_cols, near_kids, far_kids = refs[:4]
    sources = refs[4 : 4 + cols]
    halves = [refs[4 + cols : 4 + 2 * cols], refs[4 + 2 * cols : 4 + 3 * cols]]
    out, panel = refs[4 + 3 * cols : 6 + 3 * cols]
    (fronts, outs, kids, own_t, pieces, flipped, solved_even, solved_odd, own_even, own_odd,
     front_sems, out_sems, flip_sem, kid_sems, own_sems, piece_sems) = refs[6 + 3 * cols :]
    my_row, my_col = place[0], place[1]
    my_q = my_row % fan
    first_tile = my_col * fan * tiles
    steps = local_rows // block_rows
    depth = fronts.shape[0] // 2
    half_rows = local_rows // 2

    def rows_at(i):
        return pl.ds(pl.multiple_of(i * block_rows, block_rows), block_rows)

    def front_copy(i, slot):
        return pltpu.make_async_copy(front.at[rows_at(i), :], fronts.at[slot], front_sems.at[slot])

    def out_copy(i, slot):
        return pltpu.make_async_copy(outs.at[slot], out.at[rows_at(i), :], out_sems.at[slot])

    kid_copies = [
        pltpu.make_async_copy(
            source,
            kids.at[:, pl.ds(pl.multiple_of((my_q ^ q) * local_rows, local_rows), local_rows)],
            kid_sems.at[q],
        )
        for q, source in enumerate((near_kids, far_kids))
    ]
    flip_copy = pltpu.make_async_copy(solved_cols, flipped, flip_sem)
    own_copies = [
        pltpu.make_async_copy(
            source.at[:slice_cols, :], own_t.at[d * slice_cols : (d + 1) * slice_cols, :], own_sems.at[d]
        )
        for d, source in enumerate(sources)
    ]
    piece_copies = [
        pltpu.make_async_copy(
            halves[half][i],
            pieces.at[my_col ^ mask, half * half_rows : (half + 1) * half_rows, :],
            piece_sems.at[half * cols + i],
        )
        for half in range(2)
        for i, mask in enumerate(masks[half])
    ]
    for copy in own_copies + piece_copies + [flip_copy] + kid_copies:
        copy.start()
    front_copy(0, 0).start()
    for copy in own_copies + piece_copies:
        copy.wait()
    col_share = PW // cols
    subs = block_rows // TS
    per_tile = 128 // col_share
    span = min(512, local_cols)
    group_row = pivot_values(group_of, tiles, share, False)
    kid_row = pivot_values(kid_of, tiles, share, False)
    lane = lax.broadcasted_iota(jnp.int32, (block_rows, 128), 1)

    def row_solve(step, opening, own_ref, solved):
        own = own_t[:, rows_at(step)].astype(F32).T.astype(BF16)
        own_ref[...] = own
        product = dot(own, piv_t[...])
        yield
        entries = jnp.concatenate(
            [
                pieces[c, rows_at(step), k * col_share : (k + 1) * col_share]
                for k in range(NP)
                for c in range(cols)
            ],
            axis=1,
        )
        my_tile = my_row * tiles + step * subs
        parts = []
        for i in range(subs):
            part = slice(i * TS, (i + 1) * TS)
            parts.append(
                jnp.where(group_row == group_of[my_tile + i], entries[part], 0.0)
                + jnp.where(kid_row == kid_of[my_tile + i], product[part], 0.0)
            )
        full = jnp.concatenate(parts, axis=0)
        high, low = split(full[:, :PW])
        yield
        head = dot(high, inv1_t_hi[...]) + dot(high, inv1_t_lo[...]) + dot(low, inv1_t_hi[...])
        solved[:, :PW] = head
        yield
        high, low = split(full[:, PW:] - dot(head.astype(BF16), link_t[...]))
        yield
        solved[:, PW:] = dot(high, inv2_t_hi[...]) + dot(high, inv2_t_lo[...]) + dot(low, inv2_t_hi[...])
        yield
        if opening:
            at = pl.multiple_of(my_row * share, share)
            solved[:share, :PW] = lower1[pl.ds(at, share), :]
            solved[:share, PW:] = jnp.zeros((share, PW), F32)
            solved[share : 2 * share, :PW] = lower1[pl.ds(PW + at, share), :]
            solved[share : 2 * share, PW:] = lower2[pl.ds(at, share), :]
        moved_out = jnp.zeros((block_rows, 128), F32)
        for k in range(NP):
            tile = pl.multiple_of(k * PW + (my_col // per_tile) * 128, 128)
            turn = (128 + k * col_share - (my_col % per_tile) * col_share) % 128
            moved = pltpu.roll(solved[:, pl.ds(tile, 128)], turn, 1)
            moved_out = jnp.where(lane // col_share == k, moved, moved_out)
        panel[rows_at(step), :] = moved_out[:, : NP * col_share].astype(BF16)

    def update(step, slot, own_ref, solved):
        lead, own = solved[...].astype(BF16), own_ref[...]
        my_tile = my_row * tiles + step * subs
        for n in range(local_cols // span):
            at = slice(n * span, (n + 1) * span)
            change = dot(lead, flipped[:, at])
            product = dot(own, kids[:, at])
            group_all = tile_values(group_of, first_tile + n * (span // TS), span // TS)
            kid_all = tile_values(kid_of, first_tile + n * (span // TS), span // TS)
            for i in range(subs):
                part = slice(i * TS, (i + 1) * TS)
                outs[slot, part, at] = (
                    jnp.where(group_all == group_of[my_tile + i], fronts[slot, part, at], 0.0)
                    + jnp.where(kid_all == kid_of[my_tile + i], product[part], 0.0)
                    + change[part]
                )
            yield

    together(row_solve(0, True, own_even, solved_even))
    for copy in [flip_copy] + kid_copies:
        copy.wait()
    for i in range(1, 2 * depth):
        front_copy(i, i).start()

    def two_blocks(pair, carry):
        for odd in range(2):
            step = 2 * pair + odd
            slot = 2 * lax.rem(pair, depth) + odd
            front_copy(step, slot).wait()

            @pl.when(pair >= depth)
            def _():
                out_copy(step - 2 * depth, slot).wait()

            if odd:
                mine, later = (own_odd, solved_odd), (own_even, solved_even)
            else:
                mine, later = (own_even, solved_even), (own_odd, solved_odd)
            together(update(step, slot, *mine), row_solve(jnp.minimum(step + 1, steps - 1), False, *later))
            for q in range(fan):
                outs[slot, :, q * local_rows : q * local_rows + held] = jnp.zeros((block_rows, held), F32)
            if not odd:

                @pl.when(pair == 0)
                def _():
                    outs[slot, :held, :] = jnp.zeros((held, local_cols), F32)

            out_copy(step, slot).start()

            @pl.when(pair + depth < steps // 2)
            def _():
                front_copy(step + 2 * depth, slot).start()

        return carry

    lax.fori_loop(0, steps // 2, two_blocks, 0)
    for i in range(steps - 2 * depth, steps):
        out_copy(i, i % (2 * depth)).wait()


def params():
    return pltpu.CompilerParams(vmem_limit_bytes=VMEM_BYTES)


def local(front_entries, tile_group, child_factor, row_map):
    rows, cols = lax.axis_size("row"), lax.axis_size("col")
    fan = rows // cols
    assert fan == 2
    local_rows, local_cols = front_entries.shape
    slice_cols = child_factor.shape[1]
    kid_cols = slice_cols * cols
    tiles = local_rows // TS
    share = PW // rows
    held = NP * share
    my_row, my_col = lax.axis_index("row"), lax.axis_index("col")
    place = jnp.stack([my_row, my_col]).astype(jnp.int32)

    flipped = child_factor.T
    own_map = lax.dynamic_slice_in_dim(row_map, my_row * tiles, tiles)
    starts = flipped.reshape(slice_cols, tiles, TS)[:, :, :held]

    def chosen(block):
        keep = (own_map == block * tiles)[None, :, None]
        return jnp.sum(jnp.where(keep, starts, 0), axis=1, dtype=F32)

    corner = jnp.concatenate(
        [
            front_entries[:held, q * local_rows + k * share : q * local_rows + (k + 1) * share]
            for k in range(NP)
            for q in range(fan)
        ],
        axis=1,
    )
    kids = jnp.concatenate([chosen(my_row), chosen(jnp.bitwise_xor(my_row, rows // 2))], axis=1)
    packet = jnp.concatenate([corner, kids], axis=0)
    packets = [swapped(packet, "row", d * fan) for d in range(cols)]

    row_strip = jnp.concatenate(
        [
            front_entries[:, q * local_rows + k * share : q * local_rows + (k + 1) * share]
            for k in range(NP)
            for q in range(fan)
        ],
        axis=1,
    )
    gathered = lax.all_gather(flipped, "row", axis=0)
    col_strip, row_strip, *packets = lax.optimization_barrier(
        (front_entries[:held].astype(BF16), row_strip, *packets)
    )
    col_strips = lax.all_gather(col_strip, "row", axis=0)
    steps = [1 << i for i in range(cols.bit_length() - 1)]
    orders = [steps, steps[::-1]]
    halves = [[row_strip[: local_rows // 2]], [row_strip[local_rows // 2 :]]]
    masks = [[0], [0]]

    def pass_on(halves, count, own_only):
        for h in range(2):
            for step in orders[h][:count]:
                for piece, mask in list(zip(halves[h], masks[h])):
                    if mask ^ step not in masks[h] and (mask == 0 or not own_only):
                        halves[h].append(swapped(piece, "col", step))
                        masks[h].append(mask ^ step)

    pass_on(halves, 1, True)
    merged = []
    for d in range(cols):
        kid = packets[d][held:, :held] + packets[d ^ (cols // 2)][held:, held:]
        half = slice_cols // 2
        merged.append(
            jnp.concatenate(
                [packets[d][:held], jnp.concatenate([kid[:half], kid[half:]], axis=1)], axis=0
            )
        )
    merged = jnp.stack(merged)
    near = jnp.stack([swapped(merged, "col", d) for d in range(cols)])
    far = swapped(near, "row", 1)

    tile_ids = jnp.arange(row_map.shape[0], dtype=jnp.int32)
    inverse_map = jnp.sum(
        jnp.where(row_map[None, :] == tile_ids[:, None], tile_ids[None, :], 0), axis=1, dtype=jnp.int32
    )
    kid_of = (inverse_map >= row_map.shape[0] // 2).astype(F32)
    group_of = jnp.repeat(tile_group, MT // TS).astype(F32)

    state = jax.ShapeDtypeStruct((PW, PW), F32)
    state_scratch = [pltpu.VMEM((PW, PW), F32), pltpu.VMEM((PW, PW), F32)]
    diag_scratch = [pltpu.VMEM((PW, 128), F32), pltpu.VMEM((8, PW), F32)]
    begun, begun_upper, diag_col, diag_row, low_rows, piv_t, piv = pl.pallas_call(
        functools.partial(open_kernel, (cols, fan, share, held, tiles)),
        out_shape=[
            state, state,
            jax.ShapeDtypeStruct((PW, 128), F32),
            jax.ShapeDtypeStruct((8, PW), F32),
            jax.ShapeDtypeStruct((PW, NPIV), F32),
            jax.ShapeDtypeStruct((kid_cols, NPIV), BF16),
            jax.ShapeDtypeStruct((NPIV, kid_cols), BF16),
        ],
        in_specs=[smem_spec()] * 3 + [whole_spec()] * 2,
        out_specs=[whole_spec()] * 7,
        scratch_shapes=[pltpu.VMEM((NPIV, NPIV), F32), pltpu.VMEM((NPIV, kid_cols), F32)],
        compiler_params=params(),
        cost_estimate=pl.CostEstimate(flops=10**10, bytes_accessed=3 * 10**7, transcendentals=0),
        name="open_pivots",
    )(place, group_of, kid_of, near, far)

    begun, gathered, halves[0][0], halves[1][0] = lax.optimization_barrier(
        (begun, gathered, halves[0][0], halves[1][0])
    )
    pass_on(halves, cols, True)
    placed = pl.pallas_call(
        functools.partial(place_kernel, (cols, fan, tiles, slice_cols)),
        out_shape=[jax.ShapeDtypeStruct((2 * slice_cols, local_rows), BF16)] * cols,
        in_specs=[smem_spec()] * 2 + [whole_spec()],
        out_specs=[whole_spec()] * cols,
        compiler_params=params(),
        cost_estimate=pl.CostEstimate(flops=0, bytes_accessed=2**16, transcendentals=0),
        name="place_tiles",
    )(place, inverse_map, gathered)
    begun, *placed = lax.optimization_barrier((begun, *placed))
    kid_parts = [swapped(placed[d], "col", d) for d in range(cols)]

    square = jax.ShapeDtypeStruct((PW, PW), BF16)
    lower1, inv1_hi, inv1_lo, inv1_t_hi, inv1_t_lo, link, link_t, rest = pl.pallas_call(
        first_kernel,
        out_shape=[
            jax.ShapeDtypeStruct((2 * PW, PW), F32),
            square, square, square, square, square, square, state,
        ],
        in_specs=[whole_spec()] * 5,
        out_specs=[whole_spec()] * 8,
        scratch_shapes=state_scratch,
        compiler_params=params(),
        cost_estimate=pl.CostEstimate(flops=10**9, bytes_accessed=10**6, transcendentals=0),
        name="first_pivots",
    )(begun, begun_upper, diag_col, diag_row, low_rows)
    lower2, inv2_hi, inv2_lo, inv2_t_hi, inv2_t_lo = pl.pallas_call(
        second_kernel,
        out_shape=[jax.ShapeDtypeStruct((PW, PW), F32), square, square, square, square],
        in_specs=[whole_spec()],
        out_specs=[whole_spec()] * 5,
        scratch_shapes=state_scratch + diag_scratch,
        compiler_params=params(),
        cost_estimate=pl.CostEstimate(flops=2 * 10**9, bytes_accessed=10**6, transcendentals=0),
        name="second_pivots",
    )(rest)

    lower2, kid_parts, halves = lax.optimization_barrier((lower2, kid_parts, halves))
    near_kids = jnp.concatenate([part[slice_cols:] for part in kid_parts], axis=0)
    far_kids = swapped(near_kids, "row", 1)
    pass_on(halves, cols, False)

    block_cols = min(1024, local_rows)
    per_block = local_rows // block_cols
    wide = min(512, block_cols)
    solved_cols = pl.pallas_call(
        functools.partial(col_kernel, (rows, fan, share, block_cols, local_rows, tiles, wide)),
        grid=(local_cols // block_cols,),
        out_shape=jax.ShapeDtypeStruct((NPIV, local_cols), BF16),
        in_specs=[smem_spec()] * 3
        + [
            pl.BlockSpec((rows, held, block_cols), lambda j: (0, 0, j)),
            pl.BlockSpec((kid_cols, block_cols), lambda j: (0, j % per_block)),
            pl.BlockSpec((kid_cols, block_cols), lambda j: (0, j % per_block)),
        ]
        + [whole_spec()] * 6,
        out_specs=pl.BlockSpec((NPIV, block_cols), lambda j: (0, j)),
        scratch_shapes=[
            pltpu.VMEM((block_cols // wide, NPIV, wide), F32),
            pltpu.VMEM((kid_cols, block_cols), BF16),
        ],
        compiler_params=params(),
        cost_estimate=pl.CostEstimate(flops=10**10, bytes_accessed=3 * 10**7, transcendentals=0),
        name="col_factors",
    )(
        place, group_of, kid_of, col_strips, near_kids, far_kids,
        piv, inv1_hi, inv1_lo, inv2_hi, inv2_lo, link,
    )

    block_rows = min(256, local_rows)
    depth = min(2, local_rows // block_rows // 2)
    schur_block, factor_panels = pl.pallas_call(
        functools.partial(
            schur_kernel,
            (cols, fan, share, held, slice_cols, block_rows, local_rows, local_cols, tiles),
            masks,
        ),
        out_shape=[
            jax.ShapeDtypeStruct((local_rows, local_cols), F32),
            jax.ShapeDtypeStruct((local_rows, NP * PW // cols), BF16),
        ],
        in_specs=[smem_spec()] * 3 + [whole_spec()] * 8 + [any_spec()] * (4 + 3 * cols),
        out_specs=[any_spec(), whole_spec()],
        scratch_shapes=[
            pltpu.VMEM((2 * depth, block_rows, local_cols), F32),
            pltpu.VMEM((2 * depth, block_rows, local_cols), F32),
            pltpu.VMEM((kid_cols, local_cols), BF16),
            pltpu.VMEM((kid_cols, local_rows), BF16),
            pltpu.VMEM((cols, local_rows, fan * held), F32),
            pltpu.VMEM((NPIV, local_cols), BF16),
            pltpu.VMEM((block_rows, NPIV), F32),
            pltpu.VMEM((block_rows, NPIV), F32),
            pltpu.VMEM((block_rows, kid_cols), BF16),
            pltpu.VMEM((block_rows, kid_cols), BF16),
            pltpu.SemaphoreType.DMA((2 * depth,)),
            pltpu.SemaphoreType.DMA((2 * depth,)),
            pltpu.SemaphoreType.DMA,
            pltpu.SemaphoreType.DMA((fan,)),
            pltpu.SemaphoreType.DMA((cols,)),
            pltpu.SemaphoreType.DMA((2 * cols,)),
        ],
        compiler_params=params(),
        cost_estimate=pl.CostEstimate(flops=3 * 10**10, bytes_accessed=9 * 10**7, transcendentals=0),
        name="schur_update",
    )(
        place, group_of, kid_of, piv_t, lower1, lower2,
        inv1_t_hi, inv1_t_lo, inv2_t_hi, inv2_t_lo, link_t,
        front_entries, solved_cols, near_kids, far_kids, *kid_parts,
        *halves[0], *halves[1],
    )
    return (factor_panels, schur_block)


def solution(mesh):
    placed = (P("row", "col"), P(), P("row", "col"), P())
    return jax.shard_map(
        local,
        mesh=mesh,
        in_specs=placed,
        out_specs=(P("row", "col"), P("row", "col")),
        check_vma=False,
    )
```

```python
import functools

import jax
import jax.numpy as jnp
from jax import lax
from jax.experimental import pallas as pl
from jax.experimental.pallas import tpu as pltpu
from jax.sharding import PartitionSpec as P

PW = 256
NP = 2
TS = 128
MT = 512
NPIV = NP * PW
BLK = 32
F32 = jnp.float32
BF16 = jnp.bfloat16
VMEM_BYTES = 60 * 1024 * 1024

NN = (((1,), (0,)), ((), ()))
NT = (((1,), (1,)), ((), ()))
TN = (((0,), (0,)), ((), ()))


def dot(left, right, dims=NN, precision=None):
    return lax.dot_general(left, right, dims, precision=precision, preferred_element_type=F32)


def exact(left, right, dims=NN):
    return dot(left, right, dims, lax.Precision.HIGHEST)


def split(value):
    high = value.astype(BF16)
    return high, (value - high.astype(F32)).astype(BF16)


def swapped(value, axis, mask):
    if mask == 0:
        return value
    return lax.ppermute(value, axis, [(i, i ^ mask) for i in range(lax.axis_size(axis))])


def whole_spec():
    return pl.BlockSpec(memory_space=pltpu.VMEM)


def any_spec():
    return pl.BlockSpec(memory_space=pl.ANY)


def smem_spec():
    return pl.BlockSpec(memory_space=pltpu.SMEM)


def factor_diagonal(block):
    groups = BLK // 8
    lane = lax.broadcasted_iota(jnp.int32, (BLK, 128), 1)
    row = lax.broadcasted_iota(jnp.int32, (BLK, 128), 0)
    row8 = lax.broadcasted_iota(jnp.int32, (8, 128), 0)
    start = jnp.where(lane < BLK, block, jnp.where(lane == row + BLK, 1.0, 0.0))
    work = [start[8 * g : 8 * g + 8] for g in range(groups)]
    cols = []
    for k in range(BLK):
        base = 8 * (k // 8)
        cols.append(jnp.broadcast_to(block[base:, k : k + 1], (BLK - base, 128)))
    scale = [jnp.ones((8, 128), F32) for _ in range(groups)]

    def inverse_root(value):
        root = lax.rsqrt(value)
        return root * (1.5 - 0.5 * value * root * root)

    for j in range(0, BLK, 2):
        g0 = j // 8
        base = 8 * g0
        one, two = cols[j], cols[j + 1]
        first, cross, last = one[j - base : j - base + 1], one[j - base + 1 : j - base + 2], two[j - base + 1 : j - base + 2]
        volume = first * last - cross * cross
        root = inverse_root(volume)
        inverse = root * root
        below = row[base:] > j + 1
        lead_one = jnp.where(below, last * one - cross * two, 0.0) * inverse
        lead_two = jnp.where(below, first * two - cross * one, 0.0) * inverse
        row_one, row_two = work[g0][j - base : j - base + 1], work[g0][j - base + 1 : j - base + 2]
        for k in range(j + 2, BLK):
            skip = 8 * (k // 8 - g0)
            cols[k] = cols[k] - (
                lead_one[skip:] * one[k - base : k - base + 1] + lead_two[skip:] * two[k - base : k - base + 1]
            )
        for g in range(g0, groups):
            part = slice(8 * (g - g0), 8 * (g - g0) + 8)
            work[g] = work[g] - (lead_one[part] * row_one + lead_two[part] * row_two)
        first_root = inverse_root(first)
        ratio = cross * (first_root * first_root)
        work[g0] = work[g0] - jnp.where(row8 == j - base + 1, ratio, 0.0) * row_one
        scale[g0] = jnp.where(row8 == j - base, first_root, scale[g0])
        scale[g0] = jnp.where(row8 == j - base + 1, first * first_root * root, scale[g0])
    return jnp.concatenate([work[g] * scale[g] for g in range(groups)], axis=0)


def factor_panel(work, upper_out, start, stop):
    per_tile = 128 // BLK
    row = lax.broadcasted_iota(jnp.int32, (BLK, PW), 0)
    lane = lax.broadcasted_iota(jnp.int32, (BLK, PW), 1)
    all_lane = lax.broadcasted_iota(jnp.int32, (PW, PW), 1)

    def step(b, carry):
        low = pl.multiple_of(b * BLK, BLK)
        tile = pl.multiple_of((b // per_tile) * 128, 128)
        shift = (b % per_tile) * BLK
        block = pltpu.roll(work[pl.ds(low, BLK), pl.ds(tile, 128)], (128 - shift) % 128, 1)
        done = factor_diagonal(block)
        inverse = pltpu.roll(done, 128 - BLK, 1)[:, :BLK]
        inside = (lane >= low) & (lane < low + BLK)
        lines = jnp.where(inside, jnp.where(lane == row + low, 1.0, 0.0), work[pl.ds(low, BLK), :])
        upper = exact(inverse, lines)
        placed = pltpu.roll(done, shift, 1)
        corner = jnp.concatenate([placed] * (PW // 128), axis=1)
        upper_out[pl.ds(low, BLK), :] = jnp.where(inside, corner, upper)
        lead = jnp.where(lane >= low + BLK, upper, 0.0)
        kept = jnp.where((all_lane >= low) & (all_lane < low + BLK), 0.0, work[...])
        work[...] = kept - exact(lead, upper, TN)
        work[pl.ds(low, BLK), :] = upper
        return carry

    lax.fori_loop(start, stop, step, 0)


def diagonals(value):
    row = lax.broadcasted_iota(jnp.int32, (PW, PW), 0)
    col = lax.broadcasted_iota(jnp.int32, (PW, PW), 1)
    kept = jnp.where(row == col, value, 0.0)
    return jnp.sum(kept, axis=1, keepdims=True), jnp.sum(kept, axis=0, keepdims=True)


def start_panel(work, diag_col, diag_row, value):
    by_row, by_col = diagonals(value)
    diag_col[...] = jnp.broadcast_to(by_row, (PW, 128))
    diag_row[...] = jnp.broadcast_to(by_col, (8, PW))
    work[...] = value / jnp.sqrt(by_row) / jnp.sqrt(by_col)


def pivot_values(table, stride, share, along_rows):
    shape = (NPIV, 1) if along_rows else (1, NPIV)
    block = lax.broadcasted_iota(jnp.int32, shape, 0 if along_rows else 1) % PW // share
    values = jnp.zeros(shape, F32)
    for r in range(PW // share):
        values = jnp.where(block == r, table[r * stride], values)
    return values


def tile_values(table, start, count):
    return jnp.concatenate([jnp.full((1, TS), table[start + i], F32) for i in range(count)], axis=1)


def finish_panel(work, upper, diag_col, diag_row, lower, inv_hi, inv_lo, inv_t_hi, inv_t_lo):
    row = lax.broadcasted_iota(jnp.int32, (PW, PW), 0)
    col = lax.broadcasted_iota(jnp.int32, (PW, PW), 1)
    lower[:PW, :] = jnp.where(col <= row, upper[...].T, 0.0) * jnp.sqrt(diag_col[:, :1])
    inverse = jnp.where(col <= row, work[...], 0.0) / jnp.sqrt(diag_row[:1, :])
    inv_hi[...], inv_lo[...] = split(inverse)
    inv_t_hi[...], inv_t_lo[...] = split(inverse.T)
    return inverse


def open_kernel(sizes, place, group_of, kid_of, near, far,
                work, upper, diag_col, diag_row, low_rows, piv_t, piv, pile, wide):
    cols, fan, share, held, tiles = sizes
    my_row, my_col = place[0], place[1]
    my_q, my_a = my_row % fan, my_row // fan
    col_share = PW // cols
    for dq, source in enumerate((near, far)):
        for d in range(cols):
            r = (my_a ^ d) * fan + (my_q ^ dq)
            pieces = [source[c ^ my_col, d, :held, :] for c in range(cols)]
            line = jnp.concatenate(
                [piece[:, k * col_share : (k + 1) * col_share] for k in range(NP) for piece in pieces],
                axis=1,
            )
            kids = []
            for e in range(cols):
                packed = source[e, d, held:, :]
                kids += [packed[:, :held], packed[:, held:]]
            kids = jnp.concatenate(kids, axis=0).T
            for k in range(NP):
                at = pl.ds(pl.multiple_of(k * PW + r * share, share), share)
                pile[at, :] = line[k * share : (k + 1) * share]
                wide[at, :] = kids[k * share : (k + 1) * share]
    piv[...] = wide[...].astype(BF16)
    piv_t[...] = wide[...].T.astype(BF16)
    product = dot(piv[...], piv_t[...])
    same_group = pivot_values(group_of, tiles, share, True) == pivot_values(group_of, tiles, share, False)
    same_kid = pivot_values(kid_of, tiles, share, True) == pivot_values(kid_of, tiles, share, False)
    pile[...] = jnp.where(same_group, pile[...], 0.0) + jnp.where(same_kid, product, 0.0)
    low_rows[...] = pile[PW:, :]
    upper[...] = jnp.zeros_like(upper)
    start_panel(work, diag_col, diag_row, pile[:PW, :PW])
    factor_panel(work, upper, 0, PW // BLK // 2)


def first_kernel(begun, begun_upper, diag_col, diag_row, low_rows,
                 lower, inv_hi, inv_lo, inv_t_hi, inv_t_lo, link_out, link_t, rest, work, upper):
    work[...] = begun[...]
    upper[...] = begun_upper[...]
    factor_panel(work, upper, PW // BLK // 2, PW // BLK)
    inverse = finish_panel(work, upper, diag_col, diag_row, lower, inv_hi, inv_lo, inv_t_hi, inv_t_lo)
    link = exact(low_rows[:, :PW], inverse, NT).astype(BF16)
    link_out[...] = link
    lower[PW:, :] = link.astype(F32)
    link_t[...] = link.astype(F32).T.astype(BF16)
    rest[...] = low_rows[:, PW:] - dot(link, link, NT)


def second_kernel(rest, lower, inv_hi, inv_lo, inv_t_hi, inv_t_lo, work, upper, diag_col, diag_row):
    start_panel(work, diag_col, diag_row, rest[...])
    factor_panel(work, upper, 0, PW // BLK)
    finish_panel(work, upper, diag_col, diag_row, lower, inv_hi, inv_lo, inv_t_hi, inv_t_lo)


def place_kernel(sizes, place, inverse_map, held, *outs):
    cols, fan, tiles, slice_cols = sizes
    my_row, my_col = place[0], place[1]
    my_q = my_row % fan

    def fetch(block, i):
        tile = inverse_map[block * tiles + i]
        at = pl.multiple_of((tile % tiles) * TS, TS)
        return held[tile // tiles, :, pl.ds(at, TS)]

    for i in range(tiles):
        mine = fetch(my_row, i)
        for d in range(cols):
            outs[d][:slice_cols, i * TS : (i + 1) * TS] = mine
    for d in range(cols):
        for i in range(tiles):
            outs[d][slice_cols:, i * TS : (i + 1) * TS] = fetch((my_col ^ d) * fan + my_q, i)


def together(*parts):
    parts = list(parts)
    while parts:
        for part in list(parts):
            try:
                next(part)
            except StopIteration:
                parts.remove(part)


def col_kernel(sizes, place, group_of, kid_of, strips, near_kids, far_kids,
               piv, inv1_hi, inv1_lo, inv2_hi, inv2_lo, link, out, strip, kids):
    rows, fan, share, block_cols, local_rows, tiles, wide = sizes
    my_row, my_col = place[0], place[1]
    my_q = my_row % fan
    j = pl.program_id(0)
    q = (j * block_cols) // local_rows
    group_col = pivot_values(group_of, tiles, share, True)
    kid_col = pivot_values(kid_of, tiles, share, True)

    @pl.when(q == my_q)
    def _():
        kids[...] = near_kids[...]

    @pl.when(q != my_q)
    def _():
        kids[...] = far_kids[...]

    def col_solve(n, pile):
        at = slice(n * wide, (n + 1) * wide)
        for r in range(rows):
            piece = strips[r, :, at].astype(F32)
            for k in range(NP):
                low = k * PW + r * share
                pile[low : low + share, :] = piece[k * share : (k + 1) * share]
        tile = my_col * fan * tiles + (j * block_cols + n * wide) // TS
        group_all = tile_values(group_of, tile, wide // TS)
        kid_all = tile_values(kid_of, tile, wide // TS)
        product = dot(piv[...], kids[:, at])
        yield
        full = jnp.where(group_col == group_all, pile[...], 0.0) + jnp.where(
            kid_col == kid_all, product, 0.0
        )
        first, second = full[:PW].astype(BF16), full[PW:]
        yield
        both = dot(jnp.concatenate([inv1_hi[...], inv1_lo[...]], axis=0), first)
        yield
        head = (both[:PW] + both[PW:]).astype(BF16)
        out[:PW, at] = -head
        yield
        second = (second - dot(link[...], head)).astype(BF16)
        yield
        both = dot(jnp.concatenate([inv2_hi[...], inv2_lo[...]], axis=0), second)
        yield
        out[PW:, at] = (-(both[:PW] + both[PW:])).astype(BF16)

    together(*[col_solve(n, strip.at[n]) for n in range(block_cols // wide)])


def schur_kernel(sizes, masks, place, group_of, kid_of,
                 piv_t, lower1, lower2, inv1_t_hi, inv1_t_lo, inv2_t_hi, inv2_t_lo, link_t, *refs):
    cols, fan, share, held, slice_cols, block_rows, local_rows, local_cols, tiles = sizes
    front, solved_cols, near_kids, far_kids = refs[:4]
    sources = refs[4 : 4 + cols]
    halves = [refs[4 + cols : 4 + 2 * cols], refs[4 + 2 * cols : 4 + 3 * cols]]
    out, panel = refs[4 + 3 * cols : 6 + 3 * cols]
    (fronts, outs, kids, own_t, pieces, flipped, solved_even, solved_odd, own_even, own_odd,
     front_sems, out_sems, flip_sem, kid_sems, own_sems, piece_sems) = refs[6 + 3 * cols :]
    my_row, my_col = place[0], place[1]
    my_q = my_row % fan
    first_tile = my_col * fan * tiles
    steps = local_rows // block_rows
    depth = fronts.shape[0] // 2
    half_rows = local_rows // 2

    def rows_at(i):
        return pl.ds(pl.multiple_of(i * block_rows, block_rows), block_rows)

    def front_copy(i, slot):
        return pltpu.make_async_copy(front.at[rows_at(i), :], fronts.at[slot], front_sems.at[slot])

    def out_copy(i, slot):
        return pltpu.make_async_copy(outs.at[slot], out.at[rows_at(i), :], out_sems.at[slot])

    kid_copies = [
        pltpu.make_async_copy(
            source,
            kids.at[:, pl.ds(pl.multiple_of((my_q ^ q) * local_rows, local_rows), local_rows)],
            kid_sems.at[q],
        )
        for q, source in enumerate((near_kids, far_kids))
    ]
    flip_copy = pltpu.make_async_copy(solved_cols, flipped, flip_sem)
    own_copies = [
        pltpu.make_async_copy(
            source.at[:slice_cols, :], own_t.at[d * slice_cols : (d + 1) * slice_cols, :], own_sems.at[d]
        )
        for d, source in enumerate(sources)
    ]
    piece_copies = [
        pltpu.make_async_copy(
            halves[half][i],
            pieces.at[my_col ^ mask, half * half_rows : (half + 1) * half_rows, :],
            piece_sems.at[half * cols + i],
        )
        for half in range(2)
        for i, mask in enumerate(masks[half])
    ]
    for copy in own_copies + piece_copies + [flip_copy] + kid_copies:
        copy.start()
    front_copy(0, 0).start()
    for copy in own_copies + piece_copies:
        copy.wait()
    col_share = PW // cols
    subs = block_rows // TS
    per_tile = 128 // col_share
    span = min(512, local_cols)
    group_row = pivot_values(group_of, tiles, share, False)
    kid_row = pivot_values(kid_of, tiles, share, False)
    lane = lax.broadcasted_iota(jnp.int32, (block_rows, 128), 1)

    def row_solve(step, opening, own_ref, solved):
        own = own_t[:, rows_at(step)].astype(F32).T.astype(BF16)
        own_ref[...] = own
        product = dot(own, piv_t[...])
        yield
        entries = jnp.concatenate(
            [
                pieces[c, rows_at(step), k * col_share : (k + 1) * col_share]
                for k in range(NP)
                for c in range(cols)
            ],
            axis=1,
        )
        my_tile = my_row * tiles + step * subs
        parts = []
        for i in range(subs):
            part = slice(i * TS, (i + 1) * TS)
            parts.append(
                jnp.where(group_row == group_of[my_tile + i], entries[part], 0.0)
                + jnp.where(kid_row == kid_of[my_tile + i], product[part], 0.0)
            )
        full = jnp.concatenate(parts, axis=0)
        high, low = split(full[:, :PW])
        yield
        head = dot(high, inv1_t_hi[...]) + dot(high, inv1_t_lo[...]) + dot(low, inv1_t_hi[...])
        solved[:, :PW] = head
        yield
        high, low = split(full[:, PW:] - dot(head.astype(BF16), link_t[...]))
        yield
        solved[:, PW:] = dot(high, inv2_t_hi[...]) + dot(high, inv2_t_lo[...]) + dot(low, inv2_t_hi[...])
        yield
        if opening:
            at = pl.multiple_of(my_row * share, share)
            solved[:share, :PW] = lower1[pl.ds(at, share), :]
            solved[:share, PW:] = jnp.zeros((share, PW), F32)
            solved[share : 2 * share, :PW] = lower1[pl.ds(PW + at, share), :]
            solved[share : 2 * share, PW:] = lower2[pl.ds(at, share), :]
        moved_out = jnp.zeros((block_rows, 128), F32)
        for k in range(NP):
            tile = pl.multiple_of(k * PW + (my_col // per_tile) * 128, 128)
            turn = (128 + k * col_share - (my_col % per_tile) * col_share) % 128
            moved = pltpu.roll(solved[:, pl.ds(tile, 128)], turn, 1)
            moved_out = jnp.where(lane // col_share == k, moved, moved_out)
        panel[rows_at(step), :] = moved_out[:, : NP * col_share].astype(BF16)

    def update(step, slot, own_ref, solved):
        lead, own = solved[...].astype(BF16), own_ref[...]
        my_tile = my_row * tiles + step * subs
        for n in range(local_cols // span):
            at = slice(n * span, (n + 1) * span)
            change = dot(lead, flipped[:, at])
            product = dot(own, kids[:, at])
            group_all = tile_values(group_of, first_tile + n * (span // TS), span // TS)
            kid_all = tile_values(kid_of, first_tile + n * (span // TS), span // TS)
            for i in range(subs):
                part = slice(i * TS, (i + 1) * TS)
                outs[slot, part, at] = (
                    jnp.where(group_all == group_of[my_tile + i], fronts[slot, part, at], 0.0)
                    + jnp.where(kid_all == kid_of[my_tile + i], product[part], 0.0)
                    + change[part]
                )
            yield

    together(row_solve(0, True, own_even, solved_even))
    for copy in [flip_copy] + kid_copies:
        copy.wait()
    for i in range(1, 2 * depth):
        front_copy(i, i).start()

    def two_blocks(pair, carry):
        for odd in range(2):
            step = 2 * pair + odd
            slot = 2 * lax.rem(pair, depth) + odd
            front_copy(step, slot).wait()

            @pl.when(pair >= depth)
            def _():
                out_copy(step - 2 * depth, slot).wait()

            if odd:
                mine, later = (own_odd, solved_odd), (own_even, solved_even)
            else:
                mine, later = (own_even, solved_even), (own_odd, solved_odd)
            together(update(step, slot, *mine), row_solve(jnp.minimum(step + 1, steps - 1), False, *later))
            for q in range(fan):
                outs[slot, :, q * local_rows : q * local_rows + held] = jnp.zeros((block_rows, held), F32)
            if not odd:

                @pl.when(pair == 0)
                def _():
                    outs[slot, :held, :] = jnp.zeros((held, local_cols), F32)

            out_copy(step, slot).start()

            @pl.when(pair + depth < steps // 2)
            def _():
                front_copy(step + 2 * depth, slot).start()

        return carry

    lax.fori_loop(0, steps // 2, two_blocks, 0)
    for i in range(steps - 2 * depth, steps):
        out_copy(i, i % (2 * depth)).wait()


def params():
    return pltpu.CompilerParams(vmem_limit_bytes=VMEM_BYTES)


def local(front_entries, tile_group, child_factor, row_map):
    rows, cols = lax.axis_size("row"), lax.axis_size("col")
    fan = rows // cols
    assert fan == 2
    local_rows, local_cols = front_entries.shape
    slice_cols = child_factor.shape[1]
    kid_cols = slice_cols * cols
    tiles = local_rows // TS
    share = PW // rows
    held = NP * share
    my_row, my_col = lax.axis_index("row"), lax.axis_index("col")
    place = jnp.stack([my_row, my_col]).astype(jnp.int32)

    flipped = child_factor.T
    own_map = lax.dynamic_slice_in_dim(row_map, my_row * tiles, tiles)
    starts = flipped.reshape(slice_cols, tiles, TS)[:, :, :held]

    def chosen(block):
        keep = (own_map == block * tiles)[None, :, None]
        return jnp.sum(jnp.where(keep, starts, 0), axis=1, dtype=F32)

    corner = jnp.concatenate(
        [
            front_entries[:held, q * local_rows + k * share : q * local_rows + (k + 1) * share]
            for k in range(NP)
            for q in range(fan)
        ],
        axis=1,
    )
    kids = jnp.concatenate([chosen(my_row), chosen(jnp.bitwise_xor(my_row, rows // 2))], axis=1)
    packet = jnp.concatenate([corner, kids], axis=0)
    packets = [swapped(packet, "row", d * fan) for d in range(cols)]

    row_strip = jnp.concatenate(
        [
            front_entries[:, q * local_rows + k * share : q * local_rows + (k + 1) * share]
            for k in range(NP)
            for q in range(fan)
        ],
        axis=1,
    )
    gathered = lax.all_gather(flipped, "row", axis=0)
    col_strip, *packets = lax.optimization_barrier((front_entries[:held].astype(BF16), *packets))
    col_strips = lax.all_gather(col_strip, "row", axis=0)
    steps = [1 << i for i in range(cols.bit_length() - 1)]
    orders = [steps, steps[::-1]]
    halves = [[row_strip[: local_rows // 2]], [row_strip[local_rows // 2 :]]]
    masks = [[0], [0]]

    def pass_on(halves, count, own_only):
        for h in range(2):
            for step in orders[h][:count]:
                for piece, mask in list(zip(halves[h], masks[h])):
                    if mask ^ step not in masks[h] and (mask == 0 or not own_only):
                        halves[h].append(swapped(piece, "col", step))
                        masks[h].append(mask ^ step)

    pass_on(halves, 1, True)
    merged = []
    for d in range(cols):
        kid = packets[d][held:, :held] + packets[d ^ (cols // 2)][held:, held:]
        half = slice_cols // 2
        merged.append(
            jnp.concatenate(
                [packets[d][:held], jnp.concatenate([kid[:half], kid[half:]], axis=1)], axis=0
            )
        )
    merged = jnp.stack(merged)
    near = jnp.stack([swapped(merged, "col", d) for d in range(cols)])
    far = swapped(near, "row", 1)

    tile_ids = jnp.arange(row_map.shape[0], dtype=jnp.int32)
    inverse_map = jnp.sum(
        jnp.where(row_map[None, :] == tile_ids[:, None], tile_ids[None, :], 0), axis=1, dtype=jnp.int32
    )
    kid_of = (inverse_map >= row_map.shape[0] // 2).astype(F32)
    group_of = jnp.repeat(tile_group, MT // TS).astype(F32)

    state = jax.ShapeDtypeStruct((PW, PW), F32)
    state_scratch = [pltpu.VMEM((PW, PW), F32), pltpu.VMEM((PW, PW), F32)]
    diag_scratch = [pltpu.VMEM((PW, 128), F32), pltpu.VMEM((8, PW), F32)]
    begun, begun_upper, diag_col, diag_row, low_rows, piv_t, piv = pl.pallas_call(
        functools.partial(open_kernel, (cols, fan, share, held, tiles)),
        out_shape=[
            state, state,
            jax.ShapeDtypeStruct((PW, 128), F32),
            jax.ShapeDtypeStruct((8, PW), F32),
            jax.ShapeDtypeStruct((PW, NPIV), F32),
            jax.ShapeDtypeStruct((kid_cols, NPIV), BF16),
            jax.ShapeDtypeStruct((NPIV, kid_cols), BF16),
        ],
        in_specs=[smem_spec()] * 3 + [whole_spec()] * 2,
        out_specs=[whole_spec()] * 7,
        scratch_shapes=[pltpu.VMEM((NPIV, NPIV), F32), pltpu.VMEM((NPIV, kid_cols), F32)],
        compiler_params=params(),
        cost_estimate=pl.CostEstimate(flops=10**10, bytes_accessed=3 * 10**7, transcendentals=0),
        name="open_pivots",
    )(place, group_of, kid_of, near, far)

    begun, gathered, halves[0][0], halves[1][0] = lax.optimization_barrier(
        (begun, gathered, halves[0][0], halves[1][0])
    )
    pass_on(halves, cols, True)
    placed = pl.pallas_call(
        functools.partial(place_kernel, (cols, fan, tiles, slice_cols)),
        out_shape=[jax.ShapeDtypeStruct((2 * slice_cols, local_rows), BF16)] * cols,
        in_specs=[smem_spec()] * 2 + [whole_spec()],
        out_specs=[whole_spec()] * cols,
        compiler_params=params(),
        cost_estimate=pl.CostEstimate(flops=0, bytes_accessed=2**16, transcendentals=0),
        name="place_tiles",
    )(place, inverse_map, gathered)
    begun, *placed = lax.optimization_barrier((begun, *placed))
    kid_parts = [swapped(placed[d], "col", d) for d in range(cols)]

    square = jax.ShapeDtypeStruct((PW, PW), BF16)
    lower1, inv1_hi, inv1_lo, inv1_t_hi, inv1_t_lo, link, link_t, rest = pl.pallas_call(
        first_kernel,
        out_shape=[
            jax.ShapeDtypeStruct((2 * PW, PW), F32),
            square, square, square, square, square, square, state,
        ],
        in_specs=[whole_spec()] * 5,
        out_specs=[whole_spec()] * 8,
        scratch_shapes=state_scratch,
        compiler_params=params(),
        cost_estimate=pl.CostEstimate(flops=10**9, bytes_accessed=10**6, transcendentals=0),
        name="first_pivots",
    )(begun, begun_upper, diag_col, diag_row, low_rows)
    lower2, inv2_hi, inv2_lo, inv2_t_hi, inv2_t_lo = pl.pallas_call(
        second_kernel,
        out_shape=[jax.ShapeDtypeStruct((PW, PW), F32), square, square, square, square],
        in_specs=[whole_spec()],
        out_specs=[whole_spec()] * 5,
        scratch_shapes=state_scratch + diag_scratch,
        compiler_params=params(),
        cost_estimate=pl.CostEstimate(flops=2 * 10**9, bytes_accessed=10**6, transcendentals=0),
        name="second_pivots",
    )(rest)

    lower2, kid_parts, halves = lax.optimization_barrier((lower2, kid_parts, halves))
    near_kids = jnp.concatenate([part[slice_cols:] for part in kid_parts], axis=0)
    far_kids = swapped(near_kids, "row", 1)
    pass_on(halves, cols, False)

    block_cols = min(1024, local_rows)
    per_block = local_rows // block_cols
    wide = min(512, block_cols)
    solved_cols = pl.pallas_call(
        functools.partial(col_kernel, (rows, fan, share, block_cols, local_rows, tiles, wide)),
        grid=(local_cols // block_cols,),
        out_shape=jax.ShapeDtypeStruct((NPIV, local_cols), BF16),
        in_specs=[smem_spec()] * 3
        + [
            pl.BlockSpec((rows, held, block_cols), lambda j: (0, 0, j)),
            pl.BlockSpec((kid_cols, block_cols), lambda j: (0, j % per_block)),
            pl.BlockSpec((kid_cols, block_cols), lambda j: (0, j % per_block)),
        ]
        + [whole_spec()] * 6,
        out_specs=pl.BlockSpec((NPIV, block_cols), lambda j: (0, j)),
        scratch_shapes=[
            pltpu.VMEM((block_cols // wide, NPIV, wide), F32),
            pltpu.VMEM((kid_cols, block_cols), BF16),
        ],
        compiler_params=params(),
        cost_estimate=pl.CostEstimate(flops=10**10, bytes_accessed=3 * 10**7, transcendentals=0),
        name="col_factors",
    )(
        place, group_of, kid_of, col_strips, near_kids, far_kids,
        piv, inv1_hi, inv1_lo, inv2_hi, inv2_lo, link,
    )

    block_rows = min(256, local_rows)
    depth = min(2, local_rows // block_rows // 2)
    schur_block, factor_panels = pl.pallas_call(
        functools.partial(
            schur_kernel,
            (cols, fan, share, held, slice_cols, block_rows, local_rows, local_cols, tiles),
            masks,
        ),
        out_shape=[
            jax.ShapeDtypeStruct((local_rows, local_cols), F32),
            jax.ShapeDtypeStruct((local_rows, NP * PW // cols), BF16),
        ],
        in_specs=[smem_spec()] * 3 + [whole_spec()] * 8 + [any_spec()] * (4 + 3 * cols),
        out_specs=[any_spec(), whole_spec()],
        scratch_shapes=[
            pltpu.VMEM((2 * depth, block_rows, local_cols), F32),
            pltpu.VMEM((2 * depth, block_rows, local_cols), F32),
            pltpu.VMEM((kid_cols, local_cols), BF16),
            pltpu.VMEM((kid_cols, local_rows), BF16),
            pltpu.VMEM((cols, local_rows, fan * held), F32),
            pltpu.VMEM((NPIV, local_cols), BF16),
            pltpu.VMEM((block_rows, NPIV), F32),
            pltpu.VMEM((block_rows, NPIV), F32),
            pltpu.VMEM((block_rows, kid_cols), BF16),
            pltpu.VMEM((block_rows, kid_cols), BF16),
            pltpu.SemaphoreType.DMA((2 * depth,)),
            pltpu.SemaphoreType.DMA((2 * depth,)),
            pltpu.SemaphoreType.DMA,
            pltpu.SemaphoreType.DMA((fan,)),
            pltpu.SemaphoreType.DMA((cols,)),
            pltpu.SemaphoreType.DMA((2 * cols,)),
        ],
        compiler_params=params(),
        cost_estimate=pl.CostEstimate(flops=3 * 10**10, bytes_accessed=9 * 10**7, transcendentals=0),
        name="schur_update",
    )(
        place, group_of, kid_of, piv_t, lower1, lower2,
        inv1_t_hi, inv1_t_lo, inv2_t_hi, inv2_t_lo, link_t,
        front_entries, solved_cols, near_kids, far_kids, *kid_parts,
        *halves[0], *halves[1],
    )
    return (factor_panels, schur_block)


def solution(mesh):
    placed = (P("row", "col"), P(), P("row", "col"), P())
    return jax.shard_map(
        local,
        mesh=mesh,
        in_specs=placed,
        out_specs=(P("row", "col"), P("row", "col")),
        check_vma=False,
    )
```
